32 devices in a mesh: fsdp: 2 (over y), tensor: 16 (over z, x, core).
Axes of the slice: x: 2, y: 2, z: 4, core: 2. Of those that a mesh axis runs over, the one named last changes fastest.
Arguments:
- tokens: bfloat16 [256, 8192], P('fsdp', 'tensor'), may hold values from -6 to 6
- in_values: bfloat16 [8192, 3, 8192], P('fsdp', None, 'tensor'), may hold values from -0.09375 to 0.09375
- in_scales: bfloat16 [64, 3, 8192], P('fsdp', None, 'tensor'), may hold values from 0.5 to 2
- filters: float32 [512, 128], P('tensor'), may hold values from -0.6 to 0.6
- out_weight: bfloat16 [8192, 8192], P('tensor', 'fsdp'), may hold values from -0.0625 to 0.0625
- cotangent: bfloat16 [256, 8192], P('fsdp', 'tensor'), may hold values from -15 to 15
Outputs:
- input_grad: bfloat16 [256, 8192], P('fsdp', 'tensor')
- filter_grad: float32 [512, 128], P('tensor')
The draws below stay inside these ranges and needn't reach their ends.
All inputs are finite; a program needn't handle non-finite values.
Results may differ from the reference program's by a relative error of at most 0.012.
Values may be sent and summed in bfloat16 or wider, within the bound.
No kernel may reach another device: no remote copies, remote signals or barrier semaphores. Data moves between devices by JAX's collectives and lax.ppermute only.
A program may use at most 192 MiB of HBM per device.

```python
import math
import jax
import jax.numpy as jnp
from jax import lax

D = 8192
GROUP = 16
TAPS = 128
BLOCK = 128
TOK_DEV = 128
LENGTH = 256


def draw_filters(key, part):
    key_noise = jax.random.fold_in(key, 11)
    key_rate = jax.random.fold_in(key, 23)
    lags = jnp.arange(TAPS, dtype=jnp.float32)[None, :]
    noise = jnp.clip(jax.random.normal(key_noise, (D // GROUP, TAPS), jnp.float32), -4.0, 4.0)
    rates = jnp.exp(jax.random.uniform(key_rate, (D // GROUP, 1), jnp.float32, math.log(1.0 / 400.0), math.log(1.0 / 25.0)))
    return 0.15 * noise * jnp.exp(-rates * lags)


def draw_cotangent(key, part):
    key_noise = jax.random.fold_in(key, 37)
    ramp = 1.0 + 2.0 * jnp.arange(LENGTH, dtype=jnp.float32)[:, None] / (LENGTH - 1)
    noise = jnp.clip(jax.random.normal(key_noise, (LENGTH, D), jnp.float32), -5.0, 5.0)
    return (noise * ramp).astype(jnp.bfloat16)


def strengthened(result, key, source, target, shards_of, factor):
    owner, partner = [(jnp.arange(result.shape[position]) // (result.shape[position] // shards_of)).reshape([-1 if axis == position else 1 for axis in range(result.ndim)]) for position in (source, target)]
    chosen = jax.random.permutation(key, shards_of)[partner]
    strong = (owner == chosen) | (owner == (partner + shards_of // 2) % shards_of)
    return jnp.where(strong, factor * result, result)


def levels(rng, shape, cuts, smallest, largest):
    loudness = 1.0
    for axis_at, parts in cuts:
        steps = jax.random.uniform(jax.random.fold_in(jax.random.fold_in(rng, 6), axis_at), (parts,), jnp.float32, smallest / len(cuts), largest / len(cuts))
        loudness = loudness * jnp.repeat(jnp.exp(steps), shape[axis_at] // parts).reshape((-1,) + (1,) * (len(shape) - 1 - axis_at))
    return loudness


def normal_values(rng, shape, spread, most, pieces=(), kind=jnp.bfloat16):
    drawn = jax.random.normal(rng, shape, jnp.float32) * spread
    if len(pieces) > 0:
        drawn = levels(rng, shape, pieces, -0.22, 0.18) * drawn
    return jnp.clip(drawn, min=-most, max=most).astype(kind)


def bell_draw_with(stream_key, extent, width, bound, pieces, heavy, kind=jnp.bfloat16):
    drawn = width * jax.random.normal(stream_key, extent, jnp.float32)
    if pieces:
        drawn = drawn * levels(stream_key, extent, pieces, -0.22, 0.18)
    return jnp.clip(strengthened(drawn, jax.random.fold_in(stream_key, 3), *heavy), -bound, bound).astype(kind)


def setup_inputs(seed: int = 0) -> dict:
    key_list = jax.random.split(jax.random.key(seed), 7)
    return {
        "tokens": normal_values(key_list[0], (LENGTH, D), 1.0, 6.0, ((0, 2), (1, 16))),
        "in_values": bell_draw_with(key_list[1], (D, 3, D), D ** -0.5, 0.09375, ((0, 2), (2, 16)), (2, 0, 16, 2.0)),
        "in_scales": jnp.clip(jnp.exp(math.log(2.0) - 1.3862944 * jax.random.uniform(key_list[2], (D // BLOCK, 3, D), jnp.float32) ** levels(key_list[2], (D // BLOCK, 3, D), ((0, 2), (2, 16)), -0.2, 0.2)), 0.5, 2.0).astype(jnp.bfloat16),
        "filters": draw_filters(jax.random.fold_in(key_list[6], 71), 0),
        "out_weight": normal_values(key_list[4], (D, D), D ** -0.5, 0.0625, ((0, 16), (1, 2))),
        "cotangent": draw_cotangent(jax.random.fold_in(key_list[6], 71), 0),
    }


def dequantize(values, scales):
    scaled = values.astype(jnp.float32).reshape(D // BLOCK, BLOCK, 3, D) * scales.astype(jnp.float32)[:, None]
    return scaled.reshape(D, 3 * D).astype(jnp.bfloat16)


def reference(tokens, in_values, in_scales, filters, out_weight, cotangent):
    length = tokens.shape[0]
    weight = dequantize(in_values, in_scales)
    proj = jnp.dot(tokens, weight, preferred_element_type=jnp.float32).astype(jnp.bfloat16).reshape(length, 3, D)
    query = proj[:, 0].astype(jnp.float32)
    key_part = proj[:, 1].astype(jnp.float32)
    value_part = proj[:, 2].astype(jnp.float32)
    product = key_part * value_part
    repeated = jnp.repeat(filters, GROUP, axis=0)
    padded_past = jnp.concatenate([jnp.zeros((TAPS - 1, D), jnp.float32), product], 0)

    def causal_step(lag_index, total):
        offset = (TAPS - 1 - lag_index).astype(jnp.int32)
        slab = lax.dynamic_slice_in_dim(padded_past, offset, length, 0)
        column = lax.dynamic_slice_in_dim(repeated, jnp.asarray(lag_index).astype(jnp.int32), 1, 1)[:, 0]
        return total + column[None, :] * slab

    conv = lax.fori_loop(0, TAPS, causal_step, jnp.zeros((length, D), jnp.float32))
    grad_z = jnp.dot(cotangent, out_weight.T, preferred_element_type=jnp.float32)
    grad_query = grad_z * conv
    grad_conv = grad_z * query
    padded_next = jnp.concatenate([grad_conv, jnp.zeros((TAPS - 1, D), jnp.float32)], 0)

    def later_step(lag_index, total):
        offset = jnp.asarray(lag_index).astype(jnp.int32)
        slab = lax.dynamic_slice_in_dim(padded_next, offset, length, 0)
        column = lax.dynamic_slice_in_dim(repeated, offset, 1, 1)[:, 0]
        return total + column[None, :] * slab

    grad_product = lax.fori_loop(0, TAPS, later_step, jnp.zeros((length, D), jnp.float32))
    grad_proj = jnp.stack([grad_query, grad_product * value_part, grad_product * key_part], axis=1)
    grad_proj = grad_proj.astype(jnp.bfloat16).reshape(length, 3 * D)
    input_grad = jnp.dot(grad_proj, weight.T, preferred_element_type=jnp.float32).astype(jnp.bfloat16)

    def one_lag(lag_index):
        offset = (TAPS - 1 - lag_index).astype(jnp.int32)
        slab = lax.dynamic_slice_in_dim(padded_past, offset, length, 0)
        return jnp.sum((grad_conv * slab).reshape(length, D // GROUP, GROUP), axis=(0, 2))

    per_lag = lax.map(one_lag, jnp.arange(TAPS, dtype=jnp.int32))
    filter_grad = per_lag.T / TOK_DEV
    return input_grad, filter_grad
```

```python
import functools

import jax
import jax.numpy as jnp
from jax import lax
from jax.experimental import pallas as pl
from jax.experimental.pallas import tpu as pltpu
from jax.sharding import PartitionSpec as P

BLOCK = 128
TOK_DEV = 128
BF16 = jnp.bfloat16
F32 = jnp.float32
MIB = 1 << 20


def cost(flops, read):
    return pl.CostEstimate(flops=int(flops), bytes_accessed=int(read), transcendentals=0)


def params(mib):
    return pltpu.CompilerParams(vmem_limit_bytes=mib * MIB)


def dequantized(v_ref, s_ref, part):
    blocks = s_ref.shape[2]
    rows = []
    for b in range(blocks):
        scale = s_ref[part, 0, b : b + 1, :].astype(F32)
        values = v_ref[part, b * BLOCK : (b + 1) * BLOCK, :].astype(F32)
        rows.append((values * scale).astype(BF16))
    return jnp.concatenate(rows, 0) if blocks > 1 else rows[0]


def piece_into(step, refs, held):
    for r, ref in enumerate(refs):

        @pl.when(step == r)
        def _(ref=ref):
            held[...] = ref[...]


def proj_kernel(pieces, runs, place_ref, *refs):
    xs, (v_ref, s_ref, out_ref, held, total) = refs[:pieces], refs[pieces:]
    step = pl.program_id(0)
    piece_into(step, xs, held)
    channels = v_ref.shape[2]
    x = held[...]
    for j in range(3):
        cols = slice(j * channels, (j + 1) * channels)
        term = jnp.dot(x, dequantized(v_ref, s_ref, j), preferred_element_type=F32)

        @pl.when(step == 0)
        def _(term=term, cols=cols):
            total[:, cols] = term

        @pl.when(step > 0)
        def _(term=term, cols=cols):
            total[:, cols] += term

    @pl.when(step == pieces - 1)
    def _():
        run = x.shape[0] // runs
        for h in range(runs):
            at = pl.ds(pl.multiple_of(place_ref[pieces + h], BLOCK), run)
            for j in range(3):
                cols = slice(j * channels, (j + 1) * channels)
                out_ref[j, :, at] = total[h * run : (h + 1) * run, cols].T.astype(BF16)


def proj_partial(xs, place, runs, values, scales):
    pieces = len(xs)
    tokens, rows = xs[0].shape
    channels = values.shape[2]
    blocks = rows // BLOCK
    return pl.pallas_call(
        functools.partial(proj_kernel, pieces, runs),
        grid_spec=pltpu.PrefetchScalarGridSpec(
            num_scalar_prefetch=1,
            grid=(pieces,),
            in_specs=[pl.BlockSpec((tokens, rows), lambda i, p: (0, 0))] * pieces
            + [
                pl.BlockSpec((3, rows, channels), lambda i, p: (0, p[i], 0)),
                pl.BlockSpec((3, 1, blocks, channels), lambda i, p: (0, p[i], 0, 0)),
            ],
            out_specs=pl.BlockSpec((3, channels, tokens), lambda i, p: (0, 0, 0)),
            scratch_shapes=[
                pltpu.VMEM((tokens, rows), BF16),
                pltpu.VMEM((tokens, 3 * channels), F32),
            ],
        ),
        out_shape=jax.ShapeDtypeStruct((3, channels, tokens), BF16),
        compiler_params=params(32),
        cost_estimate=cost(
            2 * tokens * pieces * rows * 3 * channels, 2 * pieces * rows * (3 * channels + tokens)
        ),
        name="proj_partial",
    )(place, *xs, values, scales)


def grad_z_kernel(pieces, runs, place_ref, *refs):
    xs, (w_ref, out_ref, held, total) = refs[:pieces], refs[pieces:]
    step = pl.program_id(0)
    piece_into(step, xs, held)
    term = lax.dot_general(
        w_ref[...], held[...], (((1,), (1,)), ((), ())), preferred_element_type=F32
    )

    @pl.when(step == 0)
    def _():
        total[...] = term

    @pl.when(step > 0)
    def _():
        total[...] += term

    @pl.when(step == pieces - 1)
    def _():
        run = total.shape[1] // runs
        for h in range(runs):
            at = pl.ds(pl.multiple_of(place_ref[pieces + h], BLOCK), run)
            out_ref[:, at] = total[:, h * run : (h + 1) * run].astype(BF16)


def grad_z_partial(xs, place, runs, out_weight):
    pieces = len(xs)
    tokens, rows = xs[0].shape
    channels = out_weight.shape[0]
    return pl.pallas_call(
        functools.partial(grad_z_kernel, pieces, runs),
        grid_spec=pltpu.PrefetchScalarGridSpec(
            num_scalar_prefetch=1,
            grid=(pieces,),
            in_specs=[pl.BlockSpec((tokens, rows), lambda i, p: (0, 0))] * pieces
            + [pl.BlockSpec((channels, rows), lambda i, p: (0, p[i]))],
            out_specs=pl.BlockSpec((channels, tokens), lambda i, p: (0, 0)),
            scratch_shapes=[
                pltpu.VMEM((tokens, rows), BF16),
                pltpu.VMEM((channels, tokens), F32),
            ],
        ),
        out_shape=jax.ShapeDtypeStruct((channels, tokens), BF16),
        compiler_params=params(32),
        cost_estimate=cost(
            2 * tokens * pieces * rows * channels, 2 * pieces * rows * (channels + tokens)
        ),
        name="grad_z_partial",
    )(place, *xs, out_weight)


def iotas():
    shape = (BLOCK, BLOCK)
    return lax.broadcasted_iota(jnp.int32, shape, 0), lax.broadcasted_iota(jnp.int32, shape, 1)


def sheared(array):
    return pltpu.roll(array, 0, 1, stride=1, stride_axis=0)


def toeplitz_kernel(taps_ref, back_ref, past_ref, next_ref):
    row, lane = iotas()
    for g in range(taps_ref.shape[0]):
        ahead = sheared(jnp.broadcast_to(taps_ref[g : g + 1, :], (BLOCK, BLOCK)))
        behind = sheared(jnp.broadcast_to(back_ref[g : g + 1, :], (BLOCK, BLOCK)))
        past_ref[g, :BLOCK] = jnp.where(lane < row, ahead, 0.0).astype(BF16)
        past_ref[g, BLOCK:] = jnp.where(lane >= row, ahead, 0.0).astype(BF16)
        next_ref[g, :BLOCK] = jnp.where(lane <= row, behind, 0.0).astype(BF16)
        next_ref[g, BLOCK:] = jnp.where(lane > row, behind, 0.0).astype(BF16)


def toeplitz(filters):
    groups, taps = filters.shape
    back = jnp.roll(filters[:, ::-1], 1, axis=1)
    step = min(8, groups)
    shape = jax.ShapeDtypeStruct((groups, 2 * BLOCK, taps), BF16)
    return pl.pallas_call(
        toeplitz_kernel,
        grid=(groups // step,),
        in_specs=[pl.BlockSpec((step, taps), lambda i: (i, 0))] * 2,
        out_specs=[pl.BlockSpec((step, 2 * BLOCK, taps), lambda i: (i, 0, 0))] * 2,
        out_shape=[shape, shape],
        cost_estimate=cost(groups * taps * 2000, groups * taps * 1024),
        name="toeplitz",
    )(filters, back)


def block_of(array, i):
    blocks = array.shape[1] // BLOCK
    if 0 <= i < blocks:
        return array[:, i * BLOCK : (i + 1) * BLOCK]
    return jnp.zeros((array.shape[0], BLOCK), array.dtype)


def paired(array, by):
    blocks = array.shape[1] // BLOCK
    low, high = min(by, 0), max(by, 0)
    return jnp.concatenate(
        [
            jnp.concatenate([block_of(array, i + low), block_of(array, i + high)], 1)
            for i in range(blocks)
        ],
        0,
    )


def unstacked(array, blocks):
    rows = array.shape[0] // blocks
    return jnp.concatenate([array[i * rows : (i + 1) * rows] for i in range(blocks)], 1)


def conv_kernel(parts, groups, *refs):
    partials, (past_ref, proj_ref, prod_ref, conv_ref) = refs[:parts], refs[parts:]
    proj = partials[0][...].astype(F32)
    for ref in partials[1:]:
        proj = proj + ref[...].astype(F32)
    proj = proj.astype(BF16)
    proj_ref[...] = proj
    product = (proj[1].astype(F32) * proj[2].astype(F32)).astype(BF16)
    prod_ref[...] = product
    channels, tokens = product.shape
    per = channels // groups
    for g in range(groups):
        rows = slice(g * per, (g + 1) * per)
        result = jnp.dot(paired(product[rows], -1), past_ref[g], preferred_element_type=F32)
        conv_ref[rows] = unstacked(result, tokens // BLOCK)


def conv_forward(partials, past):
    _, channels, tokens = partials[0].shape
    groups = past.shape[0]
    steps = max(1, groups // 8)
    chunk = channels // steps
    parts = len(partials)
    three = pl.BlockSpec((3, chunk, tokens), lambda i: (0, i, 0))
    one = pl.BlockSpec((chunk, tokens), lambda i: (i, 0))
    return pl.pallas_call(
        functools.partial(conv_kernel, parts, groups // steps),
        grid=(steps,),
        in_specs=[three] * parts
        + [pl.BlockSpec((groups // steps,) + past.shape[1:], lambda i: (i, 0, 0))],
        out_specs=[three, one, one],
        out_shape=[
            jax.ShapeDtypeStruct((3, channels, tokens), BF16),
            jax.ShapeDtypeStruct((channels, tokens), BF16),
            jax.ShapeDtypeStruct((channels, tokens), F32),
        ],
        compiler_params=params(32),
        cost_estimate=cost(4 * channels * tokens * BLOCK * 8, channels * tokens * 24),
        name="conv_forward",
    )(*partials, past)


def conv_back_kernel(parts, groups, *refs):
    partials, (proj_ref, conv_ref, next_ref, out_ref, grad_ref) = refs[:parts], refs[parts:]
    grad_z = partials[0][...].astype(F32)
    for ref in partials[1:]:
        grad_z = grad_z + ref[...].astype(F32)
    out_ref[0] = (grad_z * conv_ref[...]).astype(BF16)
    grad = (grad_z * proj_ref[0].astype(F32)).astype(BF16)
    grad_ref[...] = grad
    channels, tokens = grad.shape
    per = channels // groups
    for g in range(groups):
        rows = slice(g * per, (g + 1) * per)
        result = jnp.dot(paired(grad[rows], 1), next_ref[g], preferred_element_type=F32)
        result = unstacked(result, tokens // BLOCK)
        out_ref[1, rows] = (result * proj_ref[2, rows].astype(F32)).astype(BF16)
        out_ref[2, rows] = (result * proj_ref[1, rows].astype(F32)).astype(BF16)


def conv_backward(partials, proj, conv, after):
    channels, tokens = conv.shape
    groups = after.shape[0]
    steps = max(1, groups // 8)
    chunk = channels // steps
    parts = len(partials)
    three = pl.BlockSpec((3, chunk, tokens), lambda i: (0, i, 0))
    one = pl.BlockSpec((chunk, tokens), lambda i: (i, 0))
    return pl.pallas_call(
        functools.partial(conv_back_kernel, parts, groups // steps),
        grid=(steps,),
        in_specs=[one] * parts
        + [
            three,
            one,
            pl.BlockSpec((groups // steps,) + after.shape[1:], lambda i: (i, 0, 0)),
        ],
        out_specs=[three, one],
        out_shape=[
            jax.ShapeDtypeStruct((3, channels, tokens), BF16),
            jax.ShapeDtypeStruct((channels, tokens), BF16),
        ],
        compiler_params=params(32),
        cost_estimate=cost(4 * channels * tokens * BLOCK * 8, channels * tokens * 24),
        name="conv_backward",
    )(*partials, proj, conv, after)


def taps_kernel(groups, prod_ref, grad_ref, out_ref):
    row, lane = iotas()
    flip = (row + lane == BLOCK - 1).astype(F32).astype(BF16)
    channels, tokens = prod_ref.shape
    per = channels // groups
    blocks = tokens // BLOCK
    for g in range(groups):
        rows = slice(g * per, (g + 1) * per)
        earlier = paired(prod_ref[rows, :], -1)
        grad = grad_ref[rows, :]
        later = jnp.concatenate([block_of(grad, i) for i in range(blocks)], 0)
        later = jnp.dot(later, flip, preferred_element_type=F32).astype(BF16)
        both = lax.dot_general(
            earlier, later, (((0,), (0,)), ((), ())), preferred_element_type=F32
        )
        folded = jnp.where(row + lane <= BLOCK - 1, both[BLOCK:], both[:BLOCK])
        out_ref[g : g + 1, :] = jnp.sum(sheared(folded), axis=0, keepdims=True)


def taps_gradient(product, grad, groups):
    channels, tokens = product.shape
    steps = max(1, groups // 8)
    chunk = channels // steps
    one = pl.BlockSpec((chunk, tokens), lambda i: (i, 0))
    backwards = pl.pallas_call(
        functools.partial(taps_kernel, groups // steps),
        grid=(steps,),
        in_specs=[one, one],
        out_specs=pl.BlockSpec((groups // steps, BLOCK), lambda i: (i, 0)),
        out_shape=jax.ShapeDtypeStruct((groups, BLOCK), F32),
        compiler_params=params(32),
        cost_estimate=cost(4 * channels * tokens * BLOCK * 8, channels * tokens * 24),
        name="taps_gradient",
    )(product, grad)
    return backwards[:, ::-1] / TOK_DEV


def input_kernel(place_ref, v_ref, s_ref, g_ref, out_ref):
    total = None
    for j in range(3):
        term = jnp.dot(dequantized(v_ref, s_ref, j), g_ref[j], preferred_element_type=F32)
        total = term if total is None else total + term
    out_ref[0] = total.astype(BF16)


def input_partial(place, pieces, rows, values, scales, grad_proj):
    _, channels, tokens = grad_proj.shape
    blocks = rows // BLOCK
    return pl.pallas_call(
        input_kernel,
        grid_spec=pltpu.PrefetchScalarGridSpec(
            num_scalar_prefetch=1,
            grid=(pieces,),
            in_specs=[
                pl.BlockSpec((3, rows, channels), lambda i, p: (0, p[i], 0)),
                pl.BlockSpec((3, 1, blocks, channels), lambda i, p: (0, p[i], 0, 0)),
                pl.BlockSpec((3, channels, tokens), lambda i, p: (0, 0, 0)),
            ],
            out_specs=pl.BlockSpec((1, rows, tokens), lambda i, p: (i, 0, 0)),
        ),
        out_shape=jax.ShapeDtypeStruct((pieces, rows, tokens), BF16),
        compiler_params=params(32),
        cost_estimate=cost(
            2 * tokens * pieces * rows * 3 * channels, 2 * pieces * rows * (3 * channels + tokens)
        ),
        name="input_partial",
    )(place, values, scales, grad_proj)


def across(array, mask):
    return lax.ppermute(array, "tensor", [(i, i ^ mask) for i in range(16)])


def other_row(array):
    return lax.ppermute(array, "fsdp", [(0, 1), (1, 0)])


Z1, Z0, X, CORE = 8, 4, 2, 1
MINE = (0, X, Z0, X + Z0)


def gathered(array, home):
    far = across(array, Z1)
    keep = jnp.where(home, array, far)
    send = jnp.where(home, far, array)
    own = jnp.concatenate([keep, other_row(send)], 0)
    same = [own] + [across(own, mask) for mask in MINE[1:]]
    return same + [across(piece, CORE) for piece in same]


def scattered(same, others, home, y):
    got = across(others, CORE)
    summed = [(same[i].astype(F32) + got[i].astype(F32)).astype(BF16) for i in range(4)]
    total = summed[0].astype(F32)
    for piece, mask in zip(summed[1:], MINE[1:]):
        total = total + across(piece, mask).astype(F32)
    total = total.astype(BF16)
    first, second = total[:, :TOK_DEV], total[:, TOK_DEV:]
    keep = jnp.where(y == 0, first, second)
    far = other_row(jnp.where(y == 0, second, first))
    stay = jnp.where(home, keep, far)
    leave = jnp.where(home, far, keep)
    return (stay.astype(F32) + across(leave, Z1).astype(F32)).astype(BF16).T


def on_small_slice(tokens, values, scales, filters, out_weight, cotangent):
    rows = tokens.shape[1]
    k = lax.axis_index("tensor")
    y = lax.axis_index("fsdp")
    home = (k // Z1) == y
    low = k % Z1
    order = MINE + tuple(mask + CORE for mask in MINE)
    slices = [low ^ mask for mask in order]
    place = jnp.stack(slices + [y * TOK_DEV, (1 - y) * TOK_DEV]).astype(jnp.int32)
    past, after = toeplitz(filters)
    xs = gathered(tokens, home)
    cots = gathered(cotangent, home)
    proj_part = proj_partial(xs, place, 2, values, scales)
    proj, product, conv = conv_forward([proj_part, other_row(proj_part)], past)
    z_part = grad_z_partial(cots, place, 2, out_weight)
    grad_proj, grad = conv_backward([z_part, other_row(z_part)], proj, conv, after)
    others = input_partial(place[4:8], 4, rows, values, scales, grad_proj)
    same = input_partial(place[:4], 4, rows, values, scales, grad_proj)
    input_grad = scattered(same, others, home, y)
    return input_grad, taps_gradient(product, grad, filters.shape[0])


def on_any_slice(tokens, values, scales, filters, out_weight, cotangent):
    count = lax.axis_size("fsdp")
    rows = values.shape[1]
    piece = min(rows, 512)
    pieces = rows // piece
    place = jnp.arange(pieces + 1, dtype=jnp.int32) * (jnp.arange(pieces + 1) < pieces)

    def gather(array):
        whole = lax.all_gather(array, "tensor", axis=1, tiled=True)
        mine = lax.all_to_all(whole, "fsdp", 1, 0, tiled=True)
        return [mine[:, i * piece : (i + 1) * piece] for i in range(pieces)]

    def shares(array):
        every = lax.all_gather(array, "fsdp", axis=0)
        return [every[i] for i in range(count)]

    past, after = toeplitz(filters)
    proj_part = proj_partial(gather(tokens), place, 1, values, scales)
    proj, product, conv = conv_forward(shares(proj_part), past)
    z_part = grad_z_partial(gather(cotangent), place, 1, out_weight)
    grad_proj, grad = conv_backward(shares(z_part), proj, conv, after)
    partial = input_partial(place[:pieces], pieces, piece, values, scales, grad_proj)
    partial = partial.reshape(rows, partial.shape[2]).astype(F32)
    partial = lax.all_to_all(partial, "fsdp", 1, 0, tiled=True)
    summed = lax.psum_scatter(partial, "tensor", scatter_dimension=0, tiled=True)
    return summed.T.astype(BF16), taps_gradient(product, grad, filters.shape[0])


def on_device(tokens, in_values, in_scales, filters, out_weight, cotangent):
    values = jnp.transpose(in_values, (1, 0, 2))
    small = lax.axis_size("fsdp") == 2 and lax.axis_size("tensor") == 16
    piece = tokens.shape[1] if small else min(values.shape[1], 512)
    scales = jnp.transpose(in_scales, (1, 0, 2))
    scales = scales.reshape(3, -1, piece // BLOCK, scales.shape[2])
    inner = on_small_slice if small else on_any_slice
    return inner(tokens, values, scales, filters, out_weight, cotangent)


def solution(mesh):
    placed = (
        P("fsdp", "tensor"),
        P("fsdp", None, "tensor"),
        P("fsdp", None, "tensor"),
        P("tensor", None),
        P("tensor", "fsdp"),
        P("fsdp", "tensor"),
    )
    return jax.shard_map(
        on_device,
        mesh=mesh,
        in_specs=placed,
        out_specs=(P("fsdp", "tensor"), P("tensor", None)),
        check_vma=False,
    )
```

```python
import functools

import jax
import jax.numpy as jnp
from jax import lax
from jax.experimental import pallas as pl
from jax.experimental.pallas import tpu as pltpu
from jax.sharding import PartitionSpec as P

BLOCK = 128
TOK_DEV = 128
BF16 = jnp.bfloat16
F32 = jnp.float32
MIB = 1 << 20


def cost(flops, read):
    return pl.CostEstimate(flops=int(flops) >> 12, bytes_accessed=int(read) >> 12, transcendentals=0)


def params(mib):
    return pltpu.CompilerParams(vmem_limit_bytes=mib * MIB)


def in_hbm(array):
    return pltpu.with_memory_space_constraint(array, pltpu.HBM)


VMEM_SPEC = pl.BlockSpec(memory_space=pltpu.VMEM)
SMEM_SPEC = pl.BlockSpec(memory_space=pltpu.SMEM)
LATER_SPEC = pl.BlockSpec(memory_space=pl.ANY)


def copy_kernel(in_ref, *refs):
    refs[-1][...] = in_ref[...]


def copied(array, *earlier):
    return pl.pallas_call(
        copy_kernel,
        in_specs=[VMEM_SPEC] + [LATER_SPEC] * len(earlier),
        out_specs=VMEM_SPEC,
        out_shape=jax.ShapeDtypeStruct(array.shape, array.dtype),
        compiler_params=params(8),
        cost_estimate=cost(0, 4 * array.size),
        name="copied",
    )(array, *earlier)


def at_home():
    return lax.axis_index("tensor") // Z1 == lax.axis_index("fsdp")


def stack_kernel(first_ref, second_ref, out_ref, sems):
    run = first_ref.shape[0]
    copies = [
        pltpu.make_async_copy(ref, out_ref.at[pl.ds(n * run, run), :], sems.at[n])
        for n, ref in enumerate((first_ref, second_ref))
    ]
    for copy in copies:
        copy.start()
    for copy in copies:
        copy.wait()


def stacked(first, second):
    shape = (2 * first.shape[0], first.shape[1])
    return pl.pallas_call(
        stack_kernel,
        in_specs=[LATER_SPEC] * 2,
        out_specs=VMEM_SPEC,
        out_shape=pltpu.VMEM(shape, first.dtype),
        scratch_shapes=[pltpu.SemaphoreType.DMA((2,))],
        compiler_params=params(8),
        cost_estimate=cost(0, 8 * first.size),
        name="stacked",
    )(in_hbm(first), in_hbm(second))


def own_kernel(both_ref, turned_ref, crossed_ref, *out_refs):
    run = both_ref.shape[0] // 2
    home = at_home()
    for n, out_ref in enumerate(out_refs):
        at = slice(n * run, (n + 1) * run)

        @pl.when(home)
        def _(out_ref=out_ref, at=at):
            out_ref[:run] = both_ref[at]
            out_ref[run:] = turned_ref[at]

        @pl.when(jnp.logical_not(home))
        def _(out_ref=out_ref, at=at):
            out_ref[:run] = turned_ref[at]
            out_ref[run:] = crossed_ref[at]


def own_slices(both, turned, crossed):
    out = jax.ShapeDtypeStruct(both.shape, both.dtype)
    return pl.pallas_call(
        own_kernel,
        in_specs=[VMEM_SPEC] * 3,
        out_specs=[VMEM_SPEC] * 2,
        out_shape=[out, out],
        compiler_params=params(8),
        cost_estimate=cost(0, 10 * both.size),
        name="own_slices",
    )(both, turned, crossed)


def in_vmem(array):
    return pltpu.with_memory_space_constraint(array, pltpu.VMEM)


AHEAD = 3


def prepare_kernel(v_ref, s_ref, ow_ref, *refs):
    weights, (ow_out, done_ref, held, ins, in_sems, ow_sem) = refs[-9:-6], refs[-6:]
    piece = ins.shape[2]
    pieces = v_ref.shape[1] // piece

    def rows(i):
        return pl.ds(pl.multiple_of(i * piece, BLOCK), piece)

    def fetch(i, j):
        slot = lax.rem(i, AHEAD)
        return pltpu.make_async_copy(
            v_ref.at[j, rows(i), :], ins.at[slot, j], in_sems.at[slot, j]
        )

    for i in range(min(AHEAD, pieces)):
        for j in range(3):
            fetch(i, j).start()
    whole = pltpu.make_async_copy(ow_ref, ow_out, ow_sem)
    whole.start()
    held[...] = s_ref[...].astype(F32)
    done_ref[...] = jnp.zeros(done_ref.shape, F32)

    def one(i, carry):
        for j in range(3):
            fetch(i, j).wait()
            for b in range(piece // BLOCK):
                scale = held[j, pl.ds(i * (piece // BLOCK) + b, 1), :]
                at = pl.ds(pl.multiple_of(i * piece + b * BLOCK, BLOCK), BLOCK)
                values = ins[lax.rem(i, AHEAD), j, b * BLOCK : (b + 1) * BLOCK, :]
                weights[j][at, :] = (values.astype(F32) * scale).astype(BF16)

            @pl.when(i + AHEAD < pieces)
            def _(j=j):
                fetch(i + AHEAD, j).start()

        return carry

    lax.fori_loop(0, pieces, one, 0)
    whole.wait()


def prepared(values, scales, out_weight, *earlier):
    _, rows, channels = values.shape
    piece = min(rows, 512)
    *weights, out_held, ready = pl.pallas_call(
        prepare_kernel,
        in_specs=[LATER_SPEC, VMEM_SPEC, LATER_SPEC] + [LATER_SPEC] * len(earlier),
        out_specs=[VMEM_SPEC] * 5,
        out_shape=[pltpu.VMEM((rows, channels), BF16)] * 3
        + [pltpu.VMEM(out_weight.shape, BF16), jax.ShapeDtypeStruct((8, 128), F32)],
        scratch_shapes=[
            pltpu.VMEM(scales.shape, F32),
            pltpu.VMEM((AHEAD, 3, piece, channels), BF16),
            pltpu.SemaphoreType.DMA((AHEAD, 3)),
            pltpu.SemaphoreType.DMA,
        ],
        compiler_params=params(16),
        cost_estimate=cost(values.size * 4, 4 * values.size),
        name="prepare",
    )(in_hbm(values), scales, in_hbm(out_weight), *earlier)
    return weights, out_held, ready


Z1, Z0, X, CORE = 8, 4, 2, 1
MINE = (0, X, Z0, X + Z0)
OTHERS = tuple(mask + CORE for mask in MINE)


def slices_of(masks):
    low = lax.rem(lax.axis_index("tensor"), Z1)
    return [low ^ mask for mask in masks]


def run_starts(runs, run):
    if runs == 1:
        return [0]
    y = lax.axis_index("fsdp")
    return [pl.multiple_of(y * run, BLOCK), pl.multiple_of((1 - y) * run, BLOCK)]


def piece_rows(masks, n, rows):
    if masks is None:
        return pl.ds(n * rows, rows)
    return pl.ds(pl.multiple_of(slices_of(masks)[n] * rows, BLOCK), rows)


def assembled(masks, refs, held):
    for n, ref in enumerate(refs):
        held[:, piece_rows(masks, n, ref.shape[1])] = ref[...]


def proj_part(runs, held_ref, w_ref, out_ref):
    run = held_ref.shape[0] // runs
    total = jnp.dot(held_ref[...], w_ref[...], preferred_element_type=F32)
    for h, start in enumerate(run_starts(runs, run)):
        out_ref[:, pl.ds(start, run)] = total[h * run : (h + 1) * run].T.astype(BF16)


def first_proj_kernel(masks, runs, *refs):
    xs, (key_ref, value_ref, key_out, value_out, held_ref) = refs[:-5], refs[-5:]
    assembled(masks, xs, held_ref)
    proj_part(runs, held_ref, key_ref, key_out)
    proj_part(runs, held_ref, value_ref, value_out)


def more_proj_kernel(runs, held_ref, w_ref, out_ref):
    proj_part(runs, held_ref, w_ref, out_ref)


def proj_partial(xs, masks, runs, weights):
    tokens = xs[0].shape[0]
    depth, channels = weights[0].shape
    flops = 2 * tokens * depth * channels
    weights = [in_vmem(weight) for weight in weights]
    part = jax.ShapeDtypeStruct((channels, tokens), BF16)
    *keys, held = pl.pallas_call(
        functools.partial(first_proj_kernel, masks, runs),
        in_specs=[VMEM_SPEC] * (len(xs) + 2),
        out_specs=[VMEM_SPEC] * 3,
        out_shape=[part, part, pltpu.VMEM((tokens, depth), BF16)],
        compiler_params=params(16),
        cost_estimate=cost(2 * flops, 4 * depth * channels),
        name="proj_keys_values",
    )(*xs, *weights[1:])
    others = pl.pallas_call(
        functools.partial(more_proj_kernel, runs),
        in_specs=[VMEM_SPEC] * 2,
        out_specs=VMEM_SPEC,
        out_shape=part,
        compiler_params=params(16),
        cost_estimate=cost(flops, 2 * depth * channels),
        name="proj_queries",
    )(held, weights[0])
    return keys, others


def grad_z_kernel(masks, runs, *refs):
    xs, (w_ref, out_ref, held) = refs[:-3], refs[-3:]
    assembled(masks, xs, held)
    total = lax.dot_general(
        w_ref[...], held[...], (((1,), (1,)), ((), ())), preferred_element_type=F32
    )
    run = total.shape[1] // runs
    for h, start in enumerate(run_starts(runs, run)):
        out_ref[:, pl.ds(start, run)] = total[:, h * run : (h + 1) * run].astype(BF16)


def grad_z_partial(xs, masks, runs, out_weight):
    tokens = xs[0].shape[0]
    channels, depth = out_weight.shape
    return pl.pallas_call(
        functools.partial(grad_z_kernel, masks, runs),
        in_specs=[VMEM_SPEC] * (len(xs) + 1),
        out_specs=VMEM_SPEC,
        out_shape=jax.ShapeDtypeStruct((channels, tokens), BF16),
        scratch_shapes=[pltpu.VMEM((tokens, depth), BF16)],
        compiler_params=params(16),
        cost_estimate=cost(2 * tokens * depth * channels, 2 * depth * channels),
        name="grad_z_partial",
    )(*xs, in_vmem(out_weight))


def iotas():
    shape = (BLOCK, BLOCK)
    return lax.broadcasted_iota(jnp.int32, shape, 0), lax.broadcasted_iota(jnp.int32, shape, 1)


def sheared(array):
    return pltpu.roll(array, 0, 1, stride=1, stride_axis=0)


def toeplitz_kernel(taps_ref, *refs):
    past_ref, next_ref = refs[-2:]
    row, lane = iotas()
    for g in range(taps_ref.shape[0]):
        ahead = sheared(jnp.broadcast_to(taps_ref[g : g + 1, :], (BLOCK, BLOCK)))
        behind = ahead.T
        past_ref[g, :BLOCK] = jnp.where(lane < row, ahead, 0.0).astype(BF16)
        past_ref[g, BLOCK:] = jnp.where(lane >= row, ahead, 0.0).astype(BF16)
        next_ref[g, :BLOCK] = jnp.where(lane <= row, behind, 0.0).astype(BF16)
        next_ref[g, BLOCK:] = jnp.where(lane > row, behind, 0.0).astype(BF16)


def toeplitz(filters, *earlier):
    groups, taps = filters.shape
    step = min(8, groups)
    shape = pltpu.VMEM((groups, 2 * BLOCK, taps), BF16)
    return pl.pallas_call(
        toeplitz_kernel,
        grid=(groups // step,),
        in_specs=[pl.BlockSpec((step, taps), lambda i: (i, 0))]
        + [LATER_SPEC] * len(earlier),
        out_specs=[pl.BlockSpec((step, 2 * BLOCK, taps), lambda i: (i, 0, 0))] * 2,
        out_shape=[shape, shape],
        compiler_params=params(16),
        cost_estimate=cost(groups * taps * 2000, groups * taps * 1024),
        name="toeplitz",
    )(filters, *earlier)


def block_of(array, i):
    blocks = array.shape[1] // BLOCK
    if 0 <= i < blocks:
        return array[:, i * BLOCK : (i + 1) * BLOCK]
    return jnp.zeros((array.shape[0], BLOCK), array.dtype)


def paired(array, by):
    blocks = array.shape[1] // BLOCK
    low, high = min(by, 0), max(by, 0)
    return jnp.concatenate(
        [
            jnp.concatenate([block_of(array, i + low), block_of(array, i + high)], 1)
            for i in range(blocks)
        ],
        0,
    )


def unstacked(array, blocks):
    rows = array.shape[0] // blocks
    return jnp.concatenate([array[i * rows : (i + 1) * rows] for i in range(blocks)], 1)


def summed(refs):
    total = refs[0][...].astype(F32)
    for ref in refs[1:]:
        total = total + ref[...].astype(F32)
    return total.astype(BF16)


def conv_kernel(parts, groups, *refs):
    keys, values, queries = (refs[n * parts : (n + 1) * parts] for n in range(3))
    past_ref, proj_ref, prod_ref, conv_ref = refs[3 * parts :]
    key, value = summed(keys), summed(values)
    proj_ref[0] = summed(queries)
    proj_ref[1] = key
    proj_ref[2] = value
    product = (key.astype(F32) * value.astype(F32)).astype(BF16)
    prod_ref[...] = product
    channels, tokens = product.shape
    per = channels // groups
    for g in range(groups):
        rows = slice(g * per, (g + 1) * per)
        result = jnp.dot(paired(product[rows], -1), past_ref[g], preferred_element_type=F32)
        conv_ref[rows] = unstacked(result, tokens // BLOCK)


def conv_forward(keys, values, queries, past):
    channels, tokens = keys[0].shape
    groups = past.shape[0]
    steps = max(1, groups // 8)
    chunk = channels // steps
    parts = len(keys)
    one = pl.BlockSpec((chunk, tokens), lambda i: (i, 0))
    return pl.pallas_call(
        functools.partial(conv_kernel, parts, groups // steps),
        grid=(steps,),
        in_specs=[one] * (3 * parts)
        + [pl.BlockSpec((groups // steps,) + past.shape[1:], lambda i: (i, 0, 0))],
        out_specs=[pl.BlockSpec((3, chunk, tokens), lambda i: (0, i, 0)), one, one],
        out_shape=[
            jax.ShapeDtypeStruct((3, channels, tokens), BF16),
            jax.ShapeDtypeStruct((channels, tokens), BF16),
            jax.ShapeDtypeStruct((channels, tokens), F32),
        ],
        compiler_params=params(16),
        cost_estimate=cost(4 * channels * tokens * BLOCK * 8, channels * tokens * 24),
        name="conv_forward",
    )(*keys, *values, *queries, past)


def conv_back_kernel(parts, groups, *refs):
    partials, (proj_ref, conv_ref, next_ref, out_ref, grad_ref) = refs[:parts], refs[parts:]
    grad_z = partials[0][...].astype(F32)
    for ref in partials[1:]:
        grad_z = grad_z + ref[...].astype(F32)
    out_ref[0] = (grad_z * conv_ref[...]).astype(BF16)
    grad = (grad_z * proj_ref[0].astype(F32)).astype(BF16)
    grad_ref[...] = grad
    channels, tokens = grad.shape
    per = channels // groups
    for g in range(groups):
        rows = slice(g * per, (g + 1) * per)
        result = jnp.dot(paired(grad[rows], 1), next_ref[g], preferred_element_type=F32)
        result = unstacked(result, tokens // BLOCK)
        out_ref[1, rows] = (result * proj_ref[2, rows].astype(F32)).astype(BF16)
        out_ref[2, rows] = (result * proj_ref[1, rows].astype(F32)).astype(BF16)


def conv_backward(partials, proj, conv, after):
    channels, tokens = conv.shape
    groups = after.shape[0]
    steps = max(1, groups // 8)
    chunk = channels // steps
    parts = len(partials)
    three = pl.BlockSpec((3, chunk, tokens), lambda i: (0, i, 0))
    one = pl.BlockSpec((chunk, tokens), lambda i: (i, 0))
    return pl.pallas_call(
        functools.partial(conv_back_kernel, parts, groups // steps),
        grid=(steps,),
        in_specs=[one] * parts
        + [
            three,
            one,
            pl.BlockSpec((groups // steps,) + after.shape[1:], lambda i: (i, 0, 0)),
        ],
        out_specs=[three, one],
        out_shape=[
            jax.ShapeDtypeStruct((3, channels, tokens), BF16),
            jax.ShapeDtypeStruct((channels, tokens), BF16),
        ],
        compiler_params=params(16),
        cost_estimate=cost(4 * channels * tokens * BLOCK * 8, channels * tokens * 24),
        name="conv_backward",
    )(*partials, proj, conv, after)


def taps_kernel(groups, prod_ref, grad_ref, out_ref):
    row, lane = iotas()
    flip = (row + lane == BLOCK - 1).astype(F32).astype(BF16)
    channels, tokens = prod_ref.shape
    per = channels // groups
    blocks = tokens // BLOCK
    for g in range(groups):
        rows = slice(g * per, (g + 1) * per)
        product, grad = prod_ref[rows, :], grad_ref[rows, :]
        turned = jnp.dot(
            jnp.concatenate([block_of(product, i) for i in range(blocks)], 0),
            flip,
            preferred_element_type=F32,
        )
        earlier = paired(unstacked(turned.astype(BF16), blocks), -1)
        later = jnp.concatenate([block_of(grad, i) for i in range(blocks)], 0)
        both = lax.dot_general(
            earlier, later, (((0,), (0,)), ((), ())), preferred_element_type=F32
        )
        folded = jnp.where(row + lane >= BLOCK - 1, both[BLOCK:], both[:BLOCK])
        out_ref[g : g + 1, :] = jnp.sum(sheared(folded), axis=0, keepdims=True)
    out_ref[...] = pltpu.roll(out_ref[...], 1, 1) / TOK_DEV


def taps_gradient(product, grad, groups):
    channels, tokens = product.shape
    steps = max(1, groups // 8)
    chunk = channels // steps
    one = pl.BlockSpec((chunk, tokens), lambda i: (i, 0))
    return pl.pallas_call(
        functools.partial(taps_kernel, groups // steps),
        grid=(steps,),
        in_specs=[one, one],
        out_specs=pl.BlockSpec((groups // steps, BLOCK), lambda i: (i, 0)),
        out_shape=jax.ShapeDtypeStruct((groups, BLOCK), F32),
        compiler_params=params(16),
        cost_estimate=cost(4 * channels * tokens * BLOCK * 8, channels * tokens * 24),
        name="taps_gradient",
    )(product, grad)


def input_kernel(masks, *refs):
    w_refs, (g_ref, out_ref) = refs[:3], refs[3:]
    pieces, rows, _ = out_ref.shape
    for i in range(pieces):
        at = piece_rows(masks, i, rows)
        w = jnp.concatenate([ref[at, :] for ref in w_refs], 1)
        out_ref[i] = jnp.dot(w, g_ref[...], preferred_element_type=F32).astype(BF16)


def input_partial(masks, pieces, rows, weights, grad_proj):
    _, channels, tokens = grad_proj.shape
    return pl.pallas_call(
        functools.partial(input_kernel, masks),
        in_specs=[VMEM_SPEC] * 4,
        out_specs=VMEM_SPEC,
        out_shape=jax.ShapeDtypeStruct((pieces, rows, tokens), BF16),
        compiler_params=params(16),
        cost_estimate=cost(
            2 * tokens * pieces * rows * 3 * channels, 2 * pieces * rows * (3 * channels + tokens)
        ),
        name="input_partial",
    )(*[in_vmem(weight) for weight in weights], grad_proj.reshape(3 * channels, tokens))


def across(array, mask):
    return lax.ppermute(array, "tensor", [(i, i ^ mask) for i in range(16)])


def other_row(array):
    return lax.ppermute(array, "fsdp", [(0, 1), (1, 0)])


def in_square(array, turn):
    pairs = []
    for i in range(32):
        y, k = divmod(i, 16)
        target = turn(y, k // Z1)
        if target is not None:
            pairs.append((i, target[0] * 16 + target[1] * Z1 + k % Z1))
    return lax.ppermute(array, ("fsdp", "tensor"), pairs)


def from_turn(y, z1):
    return (y, 1 - z1) if y == z1 else (1 - y, z1)


def over_diagonal(y, z1):
    return None if y == z1 else (1 - y, 1 - z1)


def first_stage(array):
    return in_square(array, from_turn), in_square(array, over_diagonal)


def second_stage(own):
    return [own] + [across(own, mask) for mask in MINE[1:]]


def both_cores(same):
    return same + [across(piece, CORE) for piece in same]


def split_kernel(same_ref, got_ref, *out_refs):
    pieces = same_ref.shape[0]
    y = lax.axis_index("fsdp")
    leave = pl.ds(pl.multiple_of((1 - y) * TOK_DEV, BLOCK), TOK_DEV)
    stay = pl.ds(pl.multiple_of(y * TOK_DEV, BLOCK), TOK_DEV)
    for n in range(pieces):
        for at, out_ref in ((leave, out_refs[n]), (stay, out_refs[pieces + n])):
            total = same_ref[n, :, at].astype(F32) + got_ref[n, :, at].astype(F32)
            out_ref[...] = total.astype(BF16)


def split(same, got):
    pieces, rows, _ = same.shape
    out = jax.ShapeDtypeStruct((rows, TOK_DEV), BF16)
    halves = pl.pallas_call(
        split_kernel,
        in_specs=[VMEM_SPEC] * 2,
        out_specs=[VMEM_SPEC] * (2 * pieces),
        out_shape=[out] * (2 * pieces),
        compiler_params=params(8),
        cost_estimate=cost(0, 6 * same.size),
        name="split",
    )(same, got)
    return halves[:pieces], halves[pieces:]


def sum_kernel(*refs):
    total = refs[0][...].astype(F32)
    for ref in refs[1:-1]:
        total = total + ref[...].astype(F32)
    refs[-1][...] = total.astype(BF16)


def total_of(pieces):
    return pl.pallas_call(
        sum_kernel,
        in_specs=[VMEM_SPEC] * len(pieces),
        out_specs=VMEM_SPEC,
        out_shape=jax.ShapeDtypeStruct(pieces[0].shape, BF16),
        compiler_params=params(8),
        cost_estimate=cost(0, 8 * pieces[0].size),
        name="total",
    )(*pieces)


def sides_kernel(near_ref, far_ref, keep_ref, send_ref):
    home = at_home()

    @pl.when(home)
    def _():
        keep_ref[...] = near_ref[...]
        send_ref[...] = far_ref[...]

    @pl.when(jnp.logical_not(home))
    def _():
        keep_ref[...] = far_ref[...]
        send_ref[...] = near_ref[...]


def sides(near, far):
    out = jax.ShapeDtypeStruct(near.shape, BF16)
    return pl.pallas_call(
        sides_kernel,
        in_specs=[VMEM_SPEC] * 2,
        out_specs=[VMEM_SPEC] * 2,
        out_shape=[out] * 2,
        compiler_params=params(8),
        cost_estimate=cost(0, 8 * near.size),
        name="sides",
    )(near, far)


def last_kernel(keep_ref, got_ref, out_ref):
    total = keep_ref[...].astype(F32) + got_ref[...].astype(F32)
    out_ref[...] = total.T.astype(BF16)


def last_sum(keep, got):
    return pl.pallas_call(
        last_kernel,
        in_specs=[VMEM_SPEC] * 2,
        out_specs=VMEM_SPEC,
        out_shape=jax.ShapeDtypeStruct(keep.shape[::-1], BF16),
        compiler_params=params(8),
        cost_estimate=cost(0, 6 * keep.size),
        name="last_sum",
    )(keep, got)


def moved(pieces):
    return [pieces[0]] + [across(piece, mask) for piece, mask in zip(pieces[1:], MINE[1:])]


def scattered(same, others):
    leave, stay = split(same, across(others, CORE))
    leave, stay = moved(leave), moved(stay)
    far = other_row(total_of(leave))
    keep, send = sides(total_of(stay), far)
    return last_sum(keep, across(send, Z1))


def on_small_slice(tokens, values, scales, filters, out_weight, cotangent):
    rows = tokens.shape[1]
    both = stacked(tokens, cotangent)
    token_own, cot_own = own_slices(both, *first_stage(both))
    token_same = second_stage(token_own)
    weights, out_held, ready = prepared(values, scales, out_weight, token_own)
    past, later = toeplitz(filters, token_own)
    cot_own = copied(cot_own, ready, past, *token_same[1:])
    cot_same = second_stage(cot_own)
    keys, queries = proj_partial(both_cores(token_same), MINE + OTHERS, 2, weights)
    proj, product, conv = conv_forward(
        *[[part, other_row(part)] for part in (*keys, queries)], past
    )
    z_part = grad_z_partial(both_cores(cot_same), MINE + OTHERS, 2, out_held)
    grad_proj, grad = conv_backward([z_part, other_row(z_part)], proj, conv, later)
    others = input_partial(OTHERS, 4, rows, weights, grad_proj)
    same = input_partial(MINE, 4, rows, weights, grad_proj)
    return scattered(same, others), taps_gradient(product, grad, filters.shape[0])


def on_any_slice(tokens, values, scales, filters, out_weight, cotangent):
    count = lax.axis_size("fsdp")
    rows = values.shape[1]
    piece = min(rows, 512)
    pieces = rows // piece

    def gather(array):
        whole = lax.all_gather(array, "tensor", axis=1, tiled=True)
        mine = lax.all_to_all(whole, "fsdp", 1, 0, tiled=True)
        return [mine[:, i * piece : (i + 1) * piece] for i in range(pieces)]

    def shares(array):
        every = lax.all_gather(array, "fsdp", axis=0)
        return [every[i] for i in range(count)]

    weights, out_held, _ = prepared(values, scales, out_weight)
    past, later = toeplitz(filters)
    keys, queries = proj_partial(gather(tokens), None, 1, weights)
    proj, product, conv = conv_forward(*[shares(part) for part in (*keys, queries)], past)
    z_part = grad_z_partial(gather(cotangent), None, 1, out_held)
    grad_proj, grad = conv_backward(shares(z_part), proj, conv, later)
    partial = input_partial(None, pieces, piece, weights, grad_proj)
    partial = partial.reshape(rows, partial.shape[2]).astype(F32)
    partial = lax.all_to_all(partial, "fsdp", 1, 0, tiled=True)
    total = lax.psum_scatter(partial, "tensor", scatter_dimension=0, tiled=True)
    return total.T.astype(BF16), taps_gradient(product, grad, filters.shape[0])


def on_device(tokens, in_values, in_scales, filters, out_weight, cotangent):
    values = jnp.transpose(in_values, (1, 0, 2))
    scales = jnp.transpose(in_scales, (1, 0, 2))
    small = lax.axis_size("fsdp") == 2 and lax.axis_size("tensor") == 16
    inner = on_small_slice if small else on_any_slice
    return inner(tokens, values, scales, filters, out_weight, cotangent)


def solution(mesh):
    placed = (
        P("fsdp", "tensor"),
        P("fsdp", None, "tensor"),
        P("fsdp", None, "tensor"),
        P("tensor", None),
        P("tensor", "fsdp"),
        P("fsdp", "tensor"),
    )
    return jax.shard_map(
        on_device,
        mesh=mesh,
        in_specs=placed,
        out_specs=(P("fsdp", "tensor"), P("tensor", None)),
        check_vma=False,
    )
```

```python
import functools

import jax
import jax.numpy as jnp
from jax import lax
from jax.experimental import pallas as pl
from jax.experimental.pallas import tpu as pltpu
from jax.sharding import PartitionSpec as P

BLOCK = 128
TOK_DEV = 128
BF16 = jnp.bfloat16
F32 = jnp.float32
MIB = 1 << 20


def cost(flops, read):
    return pl.CostEstimate(flops=int(flops) >> 12, bytes_accessed=int(read) >> 12, transcendentals=0)


def params(mib):
    return pltpu.CompilerParams(vmem_limit_bytes=mib * MIB)


def in_hbm(array):
    return pltpu.with_memory_space_constraint(array, pltpu.HBM)


VMEM_SPEC = pl.BlockSpec(memory_space=pltpu.VMEM)
SMEM_SPEC = pl.BlockSpec(memory_space=pltpu.SMEM)
LATER_SPEC = pl.BlockSpec(memory_space=pl.ANY)


def copy_kernel(in_ref, *refs):
    refs[-1][...] = in_ref[...]


def copied(array, *earlier):
    return pl.pallas_call(
        copy_kernel,
        in_specs=[VMEM_SPEC] + [LATER_SPEC] * len(earlier),
        out_specs=VMEM_SPEC,
        out_shape=jax.ShapeDtypeStruct(array.shape, array.dtype),
        compiler_params=params(8),
        cost_estimate=cost(0, 4 * array.size),
        name="copied",
    )(array, *earlier)


def at_home():
    return lax.axis_index("tensor") // Z1 == lax.axis_index("fsdp")


def stack_kernel(first_ref, second_ref, out_ref, sems):
    run = first_ref.shape[0]
    copies = [
        pltpu.make_async_copy(ref, out_ref.at[pl.ds(n * run, run), :], sems.at[n])
        for n, ref in enumerate((first_ref, second_ref))
    ]
    for copy in copies:
        copy.start()
    for copy in copies:
        copy.wait()


def stacked(first, second):
    shape = (2 * first.shape[0], first.shape[1])
    return pl.pallas_call(
        stack_kernel,
        in_specs=[LATER_SPEC] * 2,
        out_specs=VMEM_SPEC,
        out_shape=pltpu.VMEM(shape, first.dtype),
        scratch_shapes=[pltpu.SemaphoreType.DMA((2,))],
        compiler_params=params(8),
        cost_estimate=cost(0, 8 * first.size),
        name="stacked",
    )(in_hbm(first), in_hbm(second))


def own_kernel(both_ref, turned_ref, crossed_ref, *refs):
    out_refs = refs[-2:]
    run = both_ref.shape[0] // 2
    home = at_home()
    for n, out_ref in enumerate(out_refs):
        at = slice(n * run, (n + 1) * run)

        @pl.when(home)
        def _(out_ref=out_ref, at=at):
            out_ref[:run] = both_ref[at]
            out_ref[run:] = turned_ref[at]

        @pl.when(jnp.logical_not(home))
        def _(out_ref=out_ref, at=at):
            out_ref[:run] = turned_ref[at]
            out_ref[run:] = crossed_ref[at]


def own_slices(both, turned, crossed, *earlier):
    out = jax.ShapeDtypeStruct(both.shape, both.dtype)
    return pl.pallas_call(
        own_kernel,
        in_specs=[VMEM_SPEC] * 3 + [LATER_SPEC] * len(earlier),
        out_specs=[VMEM_SPEC] * 2,
        out_shape=[out, out],
        compiler_params=params(8),
        cost_estimate=cost(0, 10 * both.size),
        name="own_slices",
    )(both, turned, crossed, *earlier)


def relay_kernel(*refs):
    del refs


def relayed(arrays, *earlier):
    count = len(arrays)
    return pl.pallas_call(
        relay_kernel,
        in_specs=[LATER_SPEC] * (count + len(earlier)),
        out_specs=[LATER_SPEC] * count,
        out_shape=[jax.ShapeDtypeStruct(array.shape, array.dtype) for array in arrays],
        input_output_aliases={n: n for n in range(count)},
        compiler_params=params(8),
        cost_estimate=cost(0, 0),
        name="relayed",
    )(*arrays, *earlier)


def in_vmem(array):
    return pltpu.with_memory_space_constraint(array, pltpu.VMEM)


AHEAD = 3


def prepare_kernel(v_ref, s_ref, ow_ref, *refs):
    weights, (ow_out, done_ref, held, ins, in_sems, ow_sem) = refs[-9:-6], refs[-6:]
    piece = ins.shape[2]
    pieces = v_ref.shape[1] // piece

    def rows(i):
        return pl.ds(pl.multiple_of(i * piece, BLOCK), piece)

    def fetch(i, j):
        slot = lax.rem(i, AHEAD)
        return pltpu.make_async_copy(
            v_ref.at[j, rows(i), :], ins.at[slot, j], in_sems.at[slot, j]
        )

    for i in range(min(AHEAD, pieces)):
        for j in range(3):
            fetch(i, j).start()
    whole = pltpu.make_async_copy(ow_ref, ow_out, ow_sem)
    whole.start()
    held[...] = s_ref[...].astype(F32)
    done_ref[...] = jnp.zeros(done_ref.shape, F32)

    def one(i, carry):
        for j in range(3):
            fetch(i, j).wait()
            for b in range(piece // BLOCK):
                scale = held[j, pl.ds(i * (piece // BLOCK) + b, 1), :]
                at = pl.ds(pl.multiple_of(i * piece + b * BLOCK, BLOCK), BLOCK)
                values = ins[lax.rem(i, AHEAD), j, b * BLOCK : (b + 1) * BLOCK, :]
                weights[j][at, :] = (values.astype(F32) * scale).astype(BF16)

            @pl.when(i + AHEAD < pieces)
            def _(j=j):
                fetch(i + AHEAD, j).start()

        return carry

    lax.fori_loop(0, pieces, one, 0)
    whole.wait()


def prepared(values, scales, out_weight, *earlier):
    _, rows, channels = values.shape
    piece = min(rows, 512)
    *weights, out_held, ready = pl.pallas_call(
        prepare_kernel,
        in_specs=[LATER_SPEC, VMEM_SPEC, LATER_SPEC] + [LATER_SPEC] * len(earlier),
        out_specs=[VMEM_SPEC] * 5,
        out_shape=[pltpu.VMEM((rows, channels), BF16)] * 3
        + [pltpu.VMEM(out_weight.shape, BF16), jax.ShapeDtypeStruct((8, 128), F32)],
        scratch_shapes=[
            pltpu.VMEM(scales.shape, F32),
            pltpu.VMEM((AHEAD, 3, piece, channels), BF16),
            pltpu.SemaphoreType.DMA((AHEAD, 3)),
            pltpu.SemaphoreType.DMA,
        ],
        compiler_params=params(16),
        cost_estimate=cost(values.size * 4, 4 * values.size),
        name="prepare",
    )(in_hbm(values), scales, in_hbm(out_weight), *earlier)
    return weights, out_held, ready


Z1, Z0, X, CORE = 8, 4, 2, 1
MINE = (0, X, Z0, X + Z0)
OTHERS = tuple(mask + CORE for mask in MINE)


def slices_of(masks):
    low = lax.rem(lax.axis_index("tensor"), Z1)
    return [low ^ mask for mask in masks]


def run_starts(runs, run):
    if runs == 1:
        return [0]
    y = lax.axis_index("fsdp")
    return [pl.multiple_of(y * run, BLOCK), pl.multiple_of((1 - y) * run, BLOCK)]


def piece_rows(masks, n, rows):
    if masks is None:
        return pl.ds(n * rows, rows)
    return pl.ds(pl.multiple_of(slices_of(masks)[n] * rows, BLOCK), rows)


def assembled(masks, refs, held):
    for n, ref in enumerate(refs):
        held[:, piece_rows(masks, n, ref.shape[1])] = ref[...]


def proj_kernel(masks, runs, *refs):
    xs, (out_ref, held) = refs[:-5], refs[-2:]
    assembled(masks, xs, held)
    run = held.shape[0] // runs
    for j, w_ref in enumerate(refs[-5:-2]):
        total = jnp.dot(held[...], w_ref[...], preferred_element_type=F32)
        for h, start in enumerate(run_starts(runs, run)):
            out_ref[j, :, pl.ds(start, run)] = total[h * run : (h + 1) * run].T.astype(BF16)


def proj_partial(xs, masks, runs, weights):
    tokens = xs[0].shape[0]
    depth, channels = weights[0].shape
    return pl.pallas_call(
        functools.partial(proj_kernel, masks, runs),
        in_specs=[VMEM_SPEC] * (len(xs) + 3),
        out_specs=VMEM_SPEC,
        out_shape=jax.ShapeDtypeStruct((3, channels, tokens), BF16),
        scratch_shapes=[pltpu.VMEM((tokens, depth), BF16)],
        compiler_params=params(16),
        cost_estimate=cost(6 * tokens * depth * channels, 6 * depth * channels),
        name="proj_partial",
    )(*xs, *[in_vmem(weight) for weight in weights])


def grad_z_kernel(masks, runs, *refs):
    xs, (w_ref, out_ref, held) = refs[:-3], refs[-3:]
    assembled(masks, xs, held)
    total = lax.dot_general(
        w_ref[...], held[...], (((1,), (1,)), ((), ())), preferred_element_type=F32
    )
    run = total.shape[1] // runs
    for h, start in enumerate(run_starts(runs, run)):
        out_ref[:, pl.ds(start, run)] = total[:, h * run : (h + 1) * run].astype(BF16)


def grad_z_partial(xs, masks, runs, out_weight):
    tokens = xs[0].shape[0]
    channels, depth = out_weight.shape
    return pl.pallas_call(
        functools.partial(grad_z_kernel, masks, runs),
        in_specs=[VMEM_SPEC] * (len(xs) + 1),
        out_specs=VMEM_SPEC,
        out_shape=jax.ShapeDtypeStruct((channels, tokens), BF16),
        scratch_shapes=[pltpu.VMEM((tokens, depth), BF16)],
        compiler_params=params(16),
        cost_estimate=cost(2 * tokens * depth * channels, 2 * depth * channels),
        name="grad_z_partial",
    )(*xs, in_vmem(out_weight))


def iotas():
    shape = (BLOCK, BLOCK)
    return lax.broadcasted_iota(jnp.int32, shape, 0), lax.broadcasted_iota(jnp.int32, shape, 1)


def sheared(array):
    return pltpu.roll(array, 0, 1, stride=1, stride_axis=0)


def toeplitz_kernel(taps_ref, *refs):
    past_ref, next_ref = refs[-2:]
    row, lane = iotas()
    for g in range(taps_ref.shape[0]):
        ahead = sheared(jnp.broadcast_to(taps_ref[g : g + 1, :], (BLOCK, BLOCK)))
        behind = ahead.T
        past_ref[g, :BLOCK] = jnp.where(lane < row, ahead, 0.0).astype(BF16)
        past_ref[g, BLOCK:] = jnp.where(lane >= row, ahead, 0.0).astype(BF16)
        next_ref[g, :BLOCK] = jnp.where(lane <= row, behind, 0.0).astype(BF16)
        next_ref[g, BLOCK:] = jnp.where(lane > row, behind, 0.0).astype(BF16)


def toeplitz(filters, *earlier):
    groups, taps = filters.shape
    step = min(8, groups)
    shape = pltpu.VMEM((groups, 2 * BLOCK, taps), BF16)
    return pl.pallas_call(
        toeplitz_kernel,
        grid=(groups // step,),
        in_specs=[pl.BlockSpec((step, taps), lambda i: (i, 0))]
        + [LATER_SPEC] * len(earlier),
        out_specs=[pl.BlockSpec((step, 2 * BLOCK, taps), lambda i: (i, 0, 0))] * 2,
        out_shape=[shape, shape],
        compiler_params=params(16),
        cost_estimate=cost(groups * taps * 2000, groups * taps * 1024),
        name="toeplitz",
    )(filters, *earlier)


def block_of(array, i):
    blocks = array.shape[1] // BLOCK
    if 0 <= i < blocks:
        return array[:, i * BLOCK : (i + 1) * BLOCK]
    return jnp.zeros((array.shape[0], BLOCK), array.dtype)


def paired(array, by):
    blocks = array.shape[1] // BLOCK
    low, high = min(by, 0), max(by, 0)
    return jnp.concatenate(
        [
            jnp.concatenate([block_of(array, i + low), block_of(array, i + high)], 1)
            for i in range(blocks)
        ],
        0,
    )


def unstacked(array, blocks):
    rows = array.shape[0] // blocks
    return jnp.concatenate([array[i * rows : (i + 1) * rows] for i in range(blocks)], 1)


def summed(refs, part):
    total = refs[0][part].astype(F32)
    for ref in refs[1:]:
        total = total + ref[part].astype(F32)
    return total.astype(BF16)


def conv_kernel(parts, groups, *refs):
    shares, (past_ref, proj_ref, prod_ref, conv_ref) = refs[:parts], refs[parts:]
    key, value = summed(shares, 1), summed(shares, 2)
    proj_ref[0] = summed(shares, 0)
    proj_ref[1] = key
    proj_ref[2] = value
    product = (key.astype(F32) * value.astype(F32)).astype(BF16)
    prod_ref[...] = product
    channels, tokens = product.shape
    per = channels // groups
    for g in range(groups):
        rows = slice(g * per, (g + 1) * per)
        result = jnp.dot(paired(product[rows], -1), past_ref[g], preferred_element_type=F32)
        conv_ref[rows] = unstacked(result, tokens // BLOCK)


def conv_forward(shares, past):
    _, channels, tokens = shares[0].shape
    groups = past.shape[0]
    steps = max(1, groups // 8)
    chunk = channels // steps
    parts = len(shares)
    three = pl.BlockSpec((3, chunk, tokens), lambda i: (0, i, 0))
    one = pl.BlockSpec((chunk, tokens), lambda i: (i, 0))
    return pl.pallas_call(
        functools.partial(conv_kernel, parts, groups // steps),
        grid=(steps,),
        in_specs=[three] * parts
        + [pl.BlockSpec((groups // steps,) + past.shape[1:], lambda i: (i, 0, 0))],
        out_specs=[three, one, one],
        out_shape=[
            jax.ShapeDtypeStruct((3, channels, tokens), BF16),
            jax.ShapeDtypeStruct((channels, tokens), BF16),
            jax.ShapeDtypeStruct((channels, tokens), F32),
        ],
        compiler_params=params(16),
        cost_estimate=cost(4 * channels * tokens * BLOCK * 8, channels * tokens * 24),
        name="conv_forward",
    )(*shares, past)


def conv_back_kernel(parts, groups, *refs):
    partials, (proj_ref, conv_ref, next_ref, out_ref, grad_ref) = refs[:parts], refs[parts:]
    grad_z = partials[0][...].astype(F32)
    for ref in partials[1:]:
        grad_z = grad_z + ref[...].astype(F32)
    out_ref[0] = (grad_z * conv_ref[...]).astype(BF16)
    grad = (grad_z * proj_ref[0].astype(F32)).astype(BF16)
    grad_ref[...] = grad
    channels, tokens = grad.shape
    per = channels // groups
    for g in range(groups):
        rows = slice(g * per, (g + 1) * per)
        result = jnp.dot(paired(grad[rows], 1), next_ref[g], preferred_element_type=F32)
        result = unstacked(result, tokens // BLOCK)
        out_ref[1, rows] = (result * proj_ref[2, rows].astype(F32)).astype(BF16)
        out_ref[2, rows] = (result * proj_ref[1, rows].astype(F32)).astype(BF16)


def conv_backward(partials, proj, conv, after):
    channels, tokens = conv.shape
    groups = after.shape[0]
    steps = max(1, groups // 8)
    chunk = channels // steps
    parts = len(partials)
    three = pl.BlockSpec((3, chunk, tokens), lambda i: (0, i, 0))
    one = pl.BlockSpec((chunk, tokens), lambda i: (i, 0))
    return pl.pallas_call(
        functools.partial(conv_back_kernel, parts, groups // steps),
        grid=(steps,),
        in_specs=[one] * parts
        + [
            three,
            one,
            pl.BlockSpec((groups // steps,) + after.shape[1:], lambda i: (i, 0, 0)),
        ],
        out_specs=[three, one],
        out_shape=[
            jax.ShapeDtypeStruct((3, channels, tokens), BF16),
            jax.ShapeDtypeStruct((channels, tokens), BF16),
        ],
        compiler_params=params(16),
        cost_estimate=cost(4 * channels * tokens * BLOCK * 8, channels * tokens * 24),
        name="conv_backward",
    )(*partials, proj, conv, after)


def taps_kernel(groups, prod_ref, grad_ref, out_ref):
    row, lane = iotas()
    flip = (row + lane == BLOCK - 1).astype(F32).astype(BF16)
    channels, tokens = prod_ref.shape
    per = channels // groups
    blocks = tokens // BLOCK
    for g in range(groups):
        rows = slice(g * per, (g + 1) * per)
        product, grad = prod_ref[rows, :], grad_ref[rows, :]
        turned = jnp.dot(
            jnp.concatenate([block_of(product, i) for i in range(blocks)], 0),
            flip,
            preferred_element_type=F32,
        )
        earlier = paired(unstacked(turned.astype(BF16), blocks), -1)
        later = jnp.concatenate([block_of(grad, i) for i in range(blocks)], 0)
        both = lax.dot_general(
            earlier, later, (((0,), (0,)), ((), ())), preferred_element_type=F32
        )
        folded = jnp.where(row + lane >= BLOCK - 1, both[BLOCK:], both[:BLOCK])
        out_ref[g : g + 1, :] = jnp.sum(sheared(folded), axis=0, keepdims=True)
    out_ref[...] = pltpu.roll(out_ref[...], 1, 1) / TOK_DEV


def taps_gradient(product, grad, groups):
    channels, tokens = product.shape
    steps = max(1, groups // 8)
    chunk = channels // steps
    one = pl.BlockSpec((chunk, tokens), lambda i: (i, 0))
    return pl.pallas_call(
        functools.partial(taps_kernel, groups // steps),
        grid=(steps,),
        in_specs=[one, one],
        out_specs=pl.BlockSpec((groups // steps, BLOCK), lambda i: (i, 0)),
        out_shape=jax.ShapeDtypeStruct((groups, BLOCK), F32),
        compiler_params=params(16),
        cost_estimate=cost(4 * channels * tokens * BLOCK * 8, channels * tokens * 24),
        name="taps_gradient",
    )(product, grad)


def input_kernel(masks, *refs):
    w_refs, (g_ref, out_ref) = refs[:3], refs[3:]
    pieces, rows, _ = out_ref.shape
    for i in range(pieces):
        at = piece_rows(masks, i, rows)
        w = jnp.concatenate([ref[at, :] for ref in w_refs], 1)
        out_ref[i] = jnp.dot(w, g_ref[...], preferred_element_type=F32).astype(BF16)


def input_partial(masks, pieces, rows, weights, grad_proj):
    _, channels, tokens = grad_proj.shape
    return pl.pallas_call(
        functools.partial(input_kernel, masks),
        in_specs=[VMEM_SPEC] * 4,
        out_specs=VMEM_SPEC,
        out_shape=jax.ShapeDtypeStruct((pieces, rows, tokens), BF16),
        compiler_params=params(16),
        cost_estimate=cost(
            2 * tokens * pieces * rows * 3 * channels, 2 * pieces * rows * (3 * channels + tokens)
        ),
        name="input_partial",
    )(*[in_vmem(weight) for weight in weights], grad_proj.reshape(3 * channels, tokens))


def across(array, mask):
    return lax.ppermute(array, "tensor", [(i, i ^ mask) for i in range(16)])


def other_row(array):
    return lax.ppermute(array, "fsdp", [(0, 1), (1, 0)])


def in_square(array, turn):
    pairs = []
    for i in range(32):
        y, k = divmod(i, 16)
        target = turn(y, k // Z1)
        if target is not None:
            pairs.append((i, target[0] * 16 + target[1] * Z1 + k % Z1))
    return lax.ppermute(array, ("fsdp", "tensor"), pairs)


def from_turn(y, z1):
    return (y, 1 - z1) if y == z1 else (1 - y, z1)


def over_diagonal(y, z1):
    return None if y == z1 else (1 - y, 1 - z1)


def first_stage(array):
    return in_square(array, from_turn), in_square(array, over_diagonal)


def second_stage(own):
    return [own] + [across(own, mask) for mask in MINE[1:]]


def both_cores(same):
    return same + [across(piece, CORE) for piece in same]


def split_kernel(same_ref, got_ref, *out_refs):
    pieces = same_ref.shape[0]
    y = lax.axis_index("fsdp")
    leave = pl.ds(pl.multiple_of((1 - y) * TOK_DEV, BLOCK), TOK_DEV)
    stay = pl.ds(pl.multiple_of(y * TOK_DEV, BLOCK), TOK_DEV)
    for n in range(pieces):
        for at, out_ref in ((leave, out_refs[n]), (stay, out_refs[pieces + n])):
            total = same_ref[n, :, at].astype(F32) + got_ref[n, :, at].astype(F32)
            out_ref[...] = total.astype(BF16)


def split(same, got):
    pieces, rows, _ = same.shape
    out = jax.ShapeDtypeStruct((rows, TOK_DEV), BF16)
    halves = pl.pallas_call(
        split_kernel,
        in_specs=[VMEM_SPEC] * 2,
        out_specs=[VMEM_SPEC] * (2 * pieces),
        out_shape=[out] * (2 * pieces),
        compiler_params=params(8),
        cost_estimate=cost(0, 6 * same.size),
        name="split",
    )(same, got)
    return halves[:pieces], halves[pieces:]


def sum_kernel(*refs):
    total = refs[0][...].astype(F32)
    for ref in refs[1:-1]:
        total = total + ref[...].astype(F32)
    refs[-1][...] = total.astype(BF16)


def total_of(pieces):
    return pl.pallas_call(
        sum_kernel,
        in_specs=[VMEM_SPEC] * len(pieces),
        out_specs=VMEM_SPEC,
        out_shape=jax.ShapeDtypeStruct(pieces[0].shape, BF16),
        compiler_params=params(8),
        cost_estimate=cost(0, 8 * pieces[0].size),
        name="total",
    )(*pieces)


def sides_kernel(near_ref, far_ref, keep_ref, send_ref):
    home = at_home()

    @pl.when(home)
    def _():
        keep_ref[...] = near_ref[...]
        send_ref[...] = far_ref[...]

    @pl.when(jnp.logical_not(home))
    def _():
        keep_ref[...] = far_ref[...]
        send_ref[...] = near_ref[...]


def sides(near, far):
    out = jax.ShapeDtypeStruct(near.shape, BF16)
    return pl.pallas_call(
        sides_kernel,
        in_specs=[VMEM_SPEC] * 2,
        out_specs=[VMEM_SPEC] * 2,
        out_shape=[out] * 2,
        compiler_params=params(8),
        cost_estimate=cost(0, 8 * near.size),
        name="sides",
    )(near, far)


def last_kernel(keep_ref, got_ref, out_ref):
    total = keep_ref[...].astype(F32) + got_ref[...].astype(F32)
    out_ref[...] = total.T.astype(BF16)


def last_sum(keep, got):
    return pl.pallas_call(
        last_kernel,
        in_specs=[VMEM_SPEC] * 2,
        out_specs=VMEM_SPEC,
        out_shape=jax.ShapeDtypeStruct(keep.shape[::-1], BF16),
        compiler_params=params(8),
        cost_estimate=cost(0, 6 * keep.size),
        name="last_sum",
    )(keep, got)


def moved(pieces):
    return [pieces[0]] + [across(piece, mask) for piece, mask in zip(pieces[1:], MINE[1:])]


def scattered(same, others):
    leave, stay = split(same, across(others, CORE))
    leave, stay = moved(leave), moved(stay)
    far = other_row(total_of(leave))
    keep, send = sides(total_of(stay), far)
    return last_sum(keep, across(send, Z1))


def on_small_slice(tokens, values, scales, filters, out_weight, cotangent):
    rows = tokens.shape[1]
    both = stacked(tokens, cotangent)
    turned, crossed = first_stage(both)
    weights, out_held, ready = prepared(values, scales, out_weight, both)
    past, later = toeplitz(filters, both)
    token_own, cot_own = own_slices(both, turned, crossed, ready, past)
    token_same = second_stage(token_own)
    cot_own = copied(cot_own, *token_same[1:])
    cot_same = second_stage(cot_own)
    proj_part = proj_partial(both_cores(token_same), MINE + OTHERS, 2, weights)
    cot_same = list(relayed(cot_same, proj_part))
    proj, product, conv = conv_forward([proj_part, other_row(proj_part)], past)
    z_part = grad_z_partial(both_cores(cot_same), MINE + OTHERS, 2, out_held)
    grad_proj, grad = conv_backward([z_part, other_row(z_part)], proj, conv, later)
    others = input_partial(OTHERS, 4, rows, weights, grad_proj)
    same = input_partial(MINE, 4, rows, weights, grad_proj)
    return scattered(same, others), taps_gradient(product, grad, filters.shape[0])


def on_any_slice(tokens, values, scales, filters, out_weight, cotangent):
    count = lax.axis_size("fsdp")
    rows = values.shape[1]
    piece = min(rows, 512)
    pieces = rows // piece

    def gather(array):
        whole = lax.all_gather(array, "tensor", axis=1, tiled=True)
        mine = lax.all_to_all(whole, "fsdp", 1, 0, tiled=True)
        return [mine[:, i * piece : (i + 1) * piece] for i in range(pieces)]

    def shares(array):
        every = lax.all_gather(array, "fsdp", axis=0)
        return [every[i] for i in range(count)]

    weights, out_held, _ = prepared(values, scales, out_weight)
    past, later = toeplitz(filters)
    proj_part = proj_partial(gather(tokens), None, 1, weights)
    proj, product, conv = conv_forward(shares(proj_part), past)
    z_part = grad_z_partial(gather(cotangent), None, 1, out_held)
    grad_proj, grad = conv_backward(shares(z_part), proj, conv, later)
    partial = input_partial(None, pieces, piece, weights, grad_proj)
    partial = partial.reshape(rows, partial.shape[2]).astype(F32)
    partial = lax.all_to_all(partial, "fsdp", 1, 0, tiled=True)
    total = lax.psum_scatter(partial, "tensor", scatter_dimension=0, tiled=True)
    return total.T.astype(BF16), taps_gradient(product, grad, filters.shape[0])


def on_device(tokens, in_values, in_scales, filters, out_weight, cotangent):
    values = jnp.transpose(in_values, (1, 0, 2))
    scales = jnp.transpose(in_scales, (1, 0, 2))
    small = lax.axis_size("fsdp") == 2 and lax.axis_size("tensor") == 16
    inner = on_small_slice if small else on_any_slice
    return inner(tokens, values, scales, filters, out_weight, cotangent)


def solution(mesh):
    placed = (
        P("fsdp", "tensor"),
        P("fsdp", None, "tensor"),
        P("fsdp", None, "tensor"),
        P("tensor", None),
        P("tensor", "fsdp"),
        P("fsdp", "tensor"),
    )
    return jax.shard_map(
        on_device,
        mesh=mesh,
        in_specs=placed,
        out_specs=(P("fsdp", "tensor"), P("tensor", None)),
        check_vma=False,
    )
```

```python
import functools

import jax
import jax.numpy as jnp
from jax import lax
from jax.experimental import pallas as pl
from jax.experimental.pallas import tpu as pltpu
from jax.sharding import PartitionSpec as P

BLOCK = 128
TOK_DEV = 128
BF16 = jnp.bfloat16
F32 = jnp.float32
MIB = 1 << 20


def cost(flops, read):
    return pl.CostEstimate(flops=int(flops) >> 12, bytes_accessed=int(read) >> 12, transcendentals=0)


def params(mib):
    return pltpu.CompilerParams(vmem_limit_bytes=mib * MIB)


def in_hbm(array):
    return pltpu.with_memory_space_constraint(array, pltpu.HBM)


VMEM_SPEC = pl.BlockSpec(memory_space=pltpu.VMEM)
SMEM_SPEC = pl.BlockSpec(memory_space=pltpu.SMEM)
LATER_SPEC = pl.BlockSpec(memory_space=pl.ANY)


def copy_kernel(in_ref, *refs):
    refs[-1][...] = in_ref[...]


def copied(array, *earlier):
    return pl.pallas_call(
        copy_kernel,
        in_specs=[VMEM_SPEC] + [LATER_SPEC] * len(earlier),
        out_specs=VMEM_SPEC,
        out_shape=jax.ShapeDtypeStruct(array.shape, array.dtype),
        compiler_params=params(8),
        cost_estimate=cost(0, 4 * array.size),
        name="copied",
    )(array, *earlier)


def at_home():
    return lax.axis_index("tensor") // Z1 == lax.axis_index("fsdp")


def own_kernel(array_ref, turned_ref, crossed_ref, *refs):
    out_ref, sem = refs[-2:]
    run = array_ref.shape[0]
    home = at_home()

    @pl.when(home)
    def _():
        copy = pltpu.make_async_copy(array_ref, out_ref.at[pl.ds(0, run), :], sem)
        copy.start()
        out_ref[run:] = turned_ref[...]
        copy.wait()

    @pl.when(jnp.logical_not(home))
    def _():
        out_ref[:run] = turned_ref[...]
        out_ref[run:] = crossed_ref[...]


def own_slice(array, turned, crossed, *earlier):
    return pl.pallas_call(
        own_kernel,
        in_specs=[LATER_SPEC] + [VMEM_SPEC] * 2 + [LATER_SPEC] * len(earlier),
        out_specs=VMEM_SPEC,
        out_shape=jax.ShapeDtypeStruct((2 * array.shape[0], array.shape[1]), array.dtype),
        scratch_shapes=[pltpu.SemaphoreType.DMA],
        compiler_params=params(8),
        cost_estimate=cost(0, 10 * array.size),
        name="own_slice",
    )(array, turned, crossed, *earlier)


def relay_kernel(*refs):
    del refs


def relayed(arrays, *earlier):
    count = len(arrays)
    return pl.pallas_call(
        relay_kernel,
        in_specs=[LATER_SPEC] * (count + len(earlier)),
        out_specs=[LATER_SPEC] * count,
        out_shape=[jax.ShapeDtypeStruct(array.shape, array.dtype) for array in arrays],
        input_output_aliases={n: n for n in range(count)},
        compiler_params=params(8),
        cost_estimate=cost(0, 0),
        name="relayed",
    )(*arrays, *earlier)


def in_vmem(array):
    return pltpu.with_memory_space_constraint(array, pltpu.VMEM)


AHEAD = 3


def prepare_kernel(v_ref, s_ref, ow_ref, *refs):
    weights, (ow_out, done_ref, held, ins, in_sems, ow_sem) = refs[-9:-6], refs[-6:]
    piece = ins.shape[2]
    pieces = v_ref.shape[1] // piece

    def rows(i):
        return pl.ds(pl.multiple_of(i * piece, BLOCK), piece)

    def fetch(i, j):
        slot = lax.rem(i, AHEAD)
        return pltpu.make_async_copy(
            v_ref.at[j, rows(i), :], ins.at[slot, j], in_sems.at[slot, j]
        )

    for i in range(min(AHEAD, pieces)):
        for j in range(3):
            fetch(i, j).start()
    whole = pltpu.make_async_copy(ow_ref, ow_out, ow_sem)
    whole.start()
    held[...] = s_ref[...].astype(F32)
    done_ref[...] = jnp.zeros(done_ref.shape, F32)

    def one(i, carry):
        for j in range(3):
            fetch(i, j).wait()
            for b in range(piece // BLOCK):
                scale = held[j, pl.ds(i * (piece // BLOCK) + b, 1), :]
                at = pl.ds(pl.multiple_of(i * piece + b * BLOCK, BLOCK), BLOCK)
                values = ins[lax.rem(i, AHEAD), j, b * BLOCK : (b + 1) * BLOCK, :]
                weights[j][at, :] = (values.astype(F32) * scale).astype(BF16)

            @pl.when(i + AHEAD < pieces)
            def _(j=j):
                fetch(i + AHEAD, j).start()

        return carry

    lax.fori_loop(0, pieces, one, 0)
    whole.wait()


def prepared(values, scales, out_weight, *earlier):
    _, rows, channels = values.shape
    piece = min(rows, 512)
    *weights, out_held, ready = pl.pallas_call(
        prepare_kernel,
        in_specs=[LATER_SPEC, VMEM_SPEC, LATER_SPEC] + [LATER_SPEC] * len(earlier),
        out_specs=[VMEM_SPEC] * 5,
        out_shape=[pltpu.VMEM((rows, channels), BF16)] * 3
        + [pltpu.VMEM(out_weight.shape, BF16), jax.ShapeDtypeStruct((8, 128), F32)],
        scratch_shapes=[
            pltpu.VMEM(scales.shape, F32),
            pltpu.VMEM((AHEAD, 3, piece, channels), BF16),
            pltpu.SemaphoreType.DMA((AHEAD, 3)),
            pltpu.SemaphoreType.DMA,
        ],
        compiler_params=params(16),
        cost_estimate=cost(values.size * 4, 4 * values.size),
        name="prepare",
    )(in_hbm(values), scales, in_hbm(out_weight), *earlier)
    return weights, out_held, ready


Z1, Z0, X, CORE = 8, 4, 2, 1
MINE = (0, X, Z0, X + Z0)
OTHERS = tuple(mask + CORE for mask in MINE)


def slices_of(masks):
    low = lax.rem(lax.axis_index("tensor"), Z1)
    return [low ^ mask for mask in masks]


def run_starts(runs, run):
    if runs == 1:
        return [0]
    y = lax.axis_index("fsdp")
    return [pl.multiple_of(y * run, BLOCK), pl.multiple_of((1 - y) * run, BLOCK)]


def piece_rows(masks, n, rows):
    if masks is None:
        return pl.ds(n * rows, rows)
    return pl.ds(pl.multiple_of(slices_of(masks)[n] * rows, BLOCK), rows)


def assembled(masks, refs, held):
    for n, ref in enumerate(refs):
        held[:, piece_rows(masks, n, ref.shape[1])] = ref[...]


def proj_kernel(masks, runs, *refs):
    xs, (out_ref, held) = refs[:-5], refs[-2:]
    assembled(masks, xs, held)
    run = held.shape[0] // runs
    for j, w_ref in enumerate(refs[-5:-2]):
        total = jnp.dot(held[...], w_ref[...], preferred_element_type=F32)
        for h, start in enumerate(run_starts(runs, run)):
            out_ref[j, :, pl.ds(start, run)] = total[h * run : (h + 1) * run].T.astype(BF16)


def proj_partial(xs, masks, runs, weights):
    tokens = xs[0].shape[0]
    depth, channels = weights[0].shape
    return pl.pallas_call(
        functools.partial(proj_kernel, masks, runs),
        in_specs=[VMEM_SPEC] * (len(xs) + 3),
        out_specs=VMEM_SPEC,
        out_shape=jax.ShapeDtypeStruct((3, channels, tokens), BF16),
        scratch_shapes=[pltpu.VMEM((tokens, depth), BF16)],
        compiler_params=params(16),
        cost_estimate=cost(6 * tokens * depth * channels, 6 * depth * channels),
        name="proj_partial",
    )(*xs, *[in_vmem(weight) for weight in weights])


def grad_z_kernel(masks, runs, *refs):
    xs, (w_ref, out_ref, held) = refs[:-3], refs[-3:]
    assembled(masks, xs, held)
    total = lax.dot_general(
        w_ref[...], held[...], (((1,), (1,)), ((), ())), preferred_element_type=F32
    )
    run = total.shape[1] // runs
    for h, start in enumerate(run_starts(runs, run)):
        out_ref[:, pl.ds(start, run)] = total[:, h * run : (h + 1) * run].astype(BF16)


def grad_z_partial(xs, masks, runs, out_weight):
    tokens = xs[0].shape[0]
    channels, depth = out_weight.shape
    return pl.pallas_call(
        functools.partial(grad_z_kernel, masks, runs),
        in_specs=[VMEM_SPEC] * (len(xs) + 1),
        out_specs=VMEM_SPEC,
        out_shape=jax.ShapeDtypeStruct((channels, tokens), BF16),
        scratch_shapes=[pltpu.VMEM((tokens, depth), BF16)],
        compiler_params=params(16),
        cost_estimate=cost(2 * tokens * depth * channels, 2 * depth * channels),
        name="grad_z_partial",
    )(*xs, in_vmem(out_weight))


def iotas():
    shape = (BLOCK, BLOCK)
    return lax.broadcasted_iota(jnp.int32, shape, 0), lax.broadcasted_iota(jnp.int32, shape, 1)


def sheared(array):
    return pltpu.roll(array, 0, 1, stride=1, stride_axis=0)


def toeplitz_kernel(taps_ref, *refs):
    past_ref, next_ref = refs[-2:]
    row, lane = iotas()
    for g in range(taps_ref.shape[0]):
        ahead = sheared(jnp.broadcast_to(taps_ref[g : g + 1, :], (BLOCK, BLOCK)))
        behind = ahead.T
        past_ref[g, :BLOCK] = jnp.where(lane < row, ahead, 0.0).astype(BF16)
        past_ref[g, BLOCK:] = jnp.where(lane >= row, ahead, 0.0).astype(BF16)
        next_ref[g, :BLOCK] = jnp.where(lane <= row, behind, 0.0).astype(BF16)
        next_ref[g, BLOCK:] = jnp.where(lane > row, behind, 0.0).astype(BF16)


def toeplitz(filters, *earlier):
    groups, taps = filters.shape
    step = min(8, groups)
    shape = pltpu.VMEM((groups, 2 * BLOCK, taps), BF16)
    return pl.pallas_call(
        toeplitz_kernel,
        grid=(groups // step,),
        in_specs=[pl.BlockSpec((step, taps), lambda i: (i, 0))]
        + [LATER_SPEC] * len(earlier),
        out_specs=[pl.BlockSpec((step, 2 * BLOCK, taps), lambda i: (i, 0, 0))] * 2,
        out_shape=[shape, shape],
        compiler_params=params(16),
        cost_estimate=cost(groups * taps * 2000, groups * taps * 1024),
        name="toeplitz",
    )(filters, *earlier)


def block_of(array, i):
    blocks = array.shape[1] // BLOCK
    if 0 <= i < blocks:
        return array[:, i * BLOCK : (i + 1) * BLOCK]
    return jnp.zeros((array.shape[0], BLOCK), array.dtype)


def paired(array, by):
    blocks = array.shape[1] // BLOCK
    low, high = min(by, 0), max(by, 0)
    return jnp.concatenate(
        [
            jnp.concatenate([block_of(array, i + low), block_of(array, i + high)], 1)
            for i in range(blocks)
        ],
        0,
    )


def unstacked(array, blocks):
    rows = array.shape[0] // blocks
    return jnp.concatenate([array[i * rows : (i + 1) * rows] for i in range(blocks)], 1)


def summed(refs, part):
    total = refs[0][part].astype(F32)
    for ref in refs[1:]:
        total = total + ref[part].astype(F32)
    return total.astype(BF16)


def conv_kernel(parts, groups, *refs):
    shares, (past_ref, proj_ref, prod_ref, conv_ref) = refs[:parts], refs[parts:]
    key, value = summed(shares, 1), summed(shares, 2)
    proj_ref[0] = summed(shares, 0)
    proj_ref[1] = key
    proj_ref[2] = value
    product = (key.astype(F32) * value.astype(F32)).astype(BF16)
    prod_ref[...] = product
    channels, tokens = product.shape
    per = channels // groups
    for g in range(groups):
        rows = slice(g * per, (g + 1) * per)
        result = jnp.dot(paired(product[rows], -1), past_ref[g], preferred_element_type=F32)
        conv_ref[rows] = unstacked(result, tokens // BLOCK)


def conv_forward(shares, past):
    _, channels, tokens = shares[0].shape
    groups = past.shape[0]
    steps = max(1, groups // 8)
    chunk = channels // steps
    parts = len(shares)
    three = pl.BlockSpec((3, chunk, tokens), lambda i: (0, i, 0))
    one = pl.BlockSpec((chunk, tokens), lambda i: (i, 0))
    return pl.pallas_call(
        functools.partial(conv_kernel, parts, groups // steps),
        grid=(steps,),
        in_specs=[three] * parts
        + [pl.BlockSpec((groups // steps,) + past.shape[1:], lambda i: (i, 0, 0))],
        out_specs=[three, one, one],
        out_shape=[
            jax.ShapeDtypeStruct((3, channels, tokens), BF16),
            jax.ShapeDtypeStruct((channels, tokens), BF16),
            jax.ShapeDtypeStruct((channels, tokens), F32),
        ],
        compiler_params=params(16),
        cost_estimate=cost(4 * channels * tokens * BLOCK * 8, channels * tokens * 24),
        name="conv_forward",
    )(*shares, past)


def conv_back_kernel(parts, groups, *refs):
    partials, (proj_ref, conv_ref, next_ref, out_ref, grad_ref) = refs[:parts], refs[parts:]
    grad_z = partials[0][...].astype(F32)
    for ref in partials[1:]:
        grad_z = grad_z + ref[...].astype(F32)
    out_ref[0] = (grad_z * conv_ref[...]).astype(BF16)
    grad = (grad_z * proj_ref[0].astype(F32)).astype(BF16)
    grad_ref[...] = grad
    channels, tokens = grad.shape
    per = channels // groups
    for g in range(groups):
        rows = slice(g * per, (g + 1) * per)
        result = jnp.dot(paired(grad[rows], 1), next_ref[g], preferred_element_type=F32)
        result = unstacked(result, tokens // BLOCK)
        out_ref[1, rows] = (result * proj_ref[2, rows].astype(F32)).astype(BF16)
        out_ref[2, rows] = (result * proj_ref[1, rows].astype(F32)).astype(BF16)


def conv_backward(partials, proj, conv, after):
    channels, tokens = conv.shape
    groups = after.shape[0]
    steps = max(1, groups // 8)
    chunk = channels // steps
    parts = len(partials)
    three = pl.BlockSpec((3, chunk, tokens), lambda i: (0, i, 0))
    one = pl.BlockSpec((chunk, tokens), lambda i: (i, 0))
    return pl.pallas_call(
        functools.partial(conv_back_kernel, parts, groups // steps),
        grid=(steps,),
        in_specs=[one] * parts
        + [
            three,
            one,
            pl.BlockSpec((groups // steps,) + after.shape[1:], lambda i: (i, 0, 0)),
        ],
        out_specs=[three, one],
        out_shape=[
            jax.ShapeDtypeStruct((3, channels, tokens), BF16),
            jax.ShapeDtypeStruct((channels, tokens), BF16),
        ],
        compiler_params=params(16),
        cost_estimate=cost(4 * channels * tokens * BLOCK * 8, channels * tokens * 24),
        name="conv_backward",
    )(*partials, proj, conv, after)


def taps_kernel(groups, prod_ref, grad_ref, out_ref):
    row, lane = iotas()
    flip = (row + lane == BLOCK - 1).astype(F32).astype(BF16)
    channels, tokens = prod_ref.shape
    per = channels // groups
    blocks = tokens // BLOCK

    def cut(ref, i):
        return ref[:, i * BLOCK : (i + 1) * BLOCK]

    turned = [
        jnp.dot(cut(prod_ref, i), flip, preferred_element_type=F32).astype(BF16)
        for i in range(blocks)
    ]
    grad = [cut(grad_ref, i) for i in range(blocks)]

    def correlated(earlier, later, rows):
        return lax.dot_general(
            jnp.concatenate([block[rows] for block in earlier], 0),
            jnp.concatenate([block[rows] for block in later], 0),
            (((0,), (0,)), ((), ())),
            preferred_element_type=F32,
        )

    for g in range(groups):
        rows = slice(g * per, (g + 1) * per)
        within = correlated(turned, grad, rows)
        before = correlated(turned[:-1], grad[1:], rows)
        folded = jnp.where(row + lane >= BLOCK - 1, within, before)
        out_ref[g : g + 1, :] = jnp.sum(sheared(folded), axis=0, keepdims=True)
    out_ref[...] = pltpu.roll(out_ref[...], 1, 1) / TOK_DEV


def taps_gradient(product, grad, groups):
    channels, tokens = product.shape
    steps = max(1, groups // 8)
    chunk = channels // steps
    one = pl.BlockSpec((chunk, tokens), lambda i: (i, 0))
    return pl.pallas_call(
        functools.partial(taps_kernel, groups // steps),
        grid=(steps,),
        in_specs=[one, one],
        out_specs=pl.BlockSpec((groups // steps, BLOCK), lambda i: (i, 0)),
        out_shape=jax.ShapeDtypeStruct((groups, BLOCK), F32),
        compiler_params=params(16),
        cost_estimate=cost(4 * channels * tokens * BLOCK * 8, channels * tokens * 24),
        name="taps_gradient",
    )(product, grad)


def input_kernel(masks, *refs):
    w_refs, (g_ref, out_ref) = refs[:3], refs[3:]
    pieces, rows, _ = out_ref.shape
    for i in range(pieces):
        at = piece_rows(masks, i, rows)
        w = jnp.concatenate([ref[at, :] for ref in w_refs], 1)
        out_ref[i] = jnp.dot(w, g_ref[...], preferred_element_type=F32).astype(BF16)


def input_partial(masks, pieces, rows, weights, grad_proj):
    _, channels, tokens = grad_proj.shape
    return pl.pallas_call(
        functools.partial(input_kernel, masks),
        in_specs=[VMEM_SPEC] * 4,
        out_specs=VMEM_SPEC,
        out_shape=jax.ShapeDtypeStruct((pieces, rows, tokens), BF16),
        compiler_params=params(16),
        cost_estimate=cost(
            2 * tokens * pieces * rows * 3 * channels, 2 * pieces * rows * (3 * channels + tokens)
        ),
        name="input_partial",
    )(*[in_vmem(weight) for weight in weights], grad_proj.reshape(3 * channels, tokens))


def across(array, mask):
    return lax.ppermute(array, "tensor", [(i, i ^ mask) for i in range(16)])


def other_row(array):
    return lax.ppermute(array, "fsdp", [(0, 1), (1, 0)])


def in_square(array, turn):
    pairs = []
    for i in range(32):
        y, k = divmod(i, 16)
        target = turn(y, k // Z1)
        if target is not None:
            pairs.append((i, target[0] * 16 + target[1] * Z1 + k % Z1))
    return lax.ppermute(array, ("fsdp", "tensor"), pairs)


def from_turn(y, z1):
    return (y, 1 - z1) if y == z1 else (1 - y, z1)


def over_diagonal(y, z1):
    return None if y == z1 else (1 - y, 1 - z1)


def first_stage(array):
    return in_square(array, from_turn), in_square(array, over_diagonal)


def second_stage(own):
    return [own] + [across(own, mask) for mask in MINE[1:]]


def both_cores(same):
    return same + [across(piece, CORE) for piece in same]


def split_kernel(same_ref, got_ref, *out_refs):
    pieces = same_ref.shape[0]
    y = lax.axis_index("fsdp")
    leave = pl.ds(pl.multiple_of((1 - y) * TOK_DEV, BLOCK), TOK_DEV)
    stay = pl.ds(pl.multiple_of(y * TOK_DEV, BLOCK), TOK_DEV)
    for n in range(pieces):
        for at, out_ref in ((leave, out_refs[n]), (stay, out_refs[pieces + n])):
            total = same_ref[n, :, at].astype(F32) + got_ref[n, :, at].astype(F32)
            out_ref[...] = total.astype(BF16)


def split(same, got):
    pieces, rows, _ = same.shape
    out = jax.ShapeDtypeStruct((rows, TOK_DEV), BF16)
    halves = pl.pallas_call(
        split_kernel,
        in_specs=[VMEM_SPEC] * 2,
        out_specs=[VMEM_SPEC] * (2 * pieces),
        out_shape=[out] * (2 * pieces),
        compiler_params=params(8),
        cost_estimate=cost(0, 6 * same.size),
        name="split",
    )(same, got)
    return halves[:pieces], halves[pieces:]


def sum_kernel(*refs):
    total = refs[0][...].astype(F32)
    for ref in refs[1:-1]:
        total = total + ref[...].astype(F32)
    refs[-1][...] = total.astype(BF16)


def total_of(pieces):
    return pl.pallas_call(
        sum_kernel,
        in_specs=[VMEM_SPEC] * len(pieces),
        out_specs=VMEM_SPEC,
        out_shape=jax.ShapeDtypeStruct(pieces[0].shape, BF16),
        compiler_params=params(8),
        cost_estimate=cost(0, 8 * pieces[0].size),
        name="total",
    )(*pieces)


def sides_kernel(near_ref, far_ref, keep_ref, send_ref):
    home = at_home()

    @pl.when(home)
    def _():
        keep_ref[...] = near_ref[...]
        send_ref[...] = far_ref[...]

    @pl.when(jnp.logical_not(home))
    def _():
        keep_ref[...] = far_ref[...]
        send_ref[...] = near_ref[...]


def sides(near, far):
    out = jax.ShapeDtypeStruct(near.shape, BF16)
    return pl.pallas_call(
        sides_kernel,
        in_specs=[VMEM_SPEC] * 2,
        out_specs=[VMEM_SPEC] * 2,
        out_shape=[out] * 2,
        compiler_params=params(8),
        cost_estimate=cost(0, 8 * near.size),
        name="sides",
    )(near, far)


def last_kernel(keep_ref, got_ref, out_ref):
    total = keep_ref[...].astype(F32) + got_ref[...].astype(F32)
    out_ref[...] = total.T.astype(BF16)


def last_sum(keep, got):
    return pl.pallas_call(
        last_kernel,
        in_specs=[VMEM_SPEC] * 2,
        out_specs=VMEM_SPEC,
        out_shape=jax.ShapeDtypeStruct(keep.shape[::-1], BF16),
        compiler_params=params(8),
        cost_estimate=cost(0, 6 * keep.size),
        name="last_sum",
    )(keep, got)


def moved(pieces):
    return [pieces[0]] + [across(piece, mask) for piece, mask in zip(pieces[1:], MINE[1:])]


def scattered(same, others):
    leave, stay = split(same, across(others, CORE))
    leave, stay = moved(leave), moved(stay)
    far = other_row(total_of(leave))
    keep, send = sides(total_of(stay), far)
    return last_sum(keep, across(send, Z1))


def on_small_slice(tokens, values, scales, filters, out_weight, cotangent):
    rows = tokens.shape[1]
    token_stage = first_stage(tokens)
    weights, out_held, ready = prepared(values, scales, out_weight)
    token_own = own_slice(in_hbm(tokens), *token_stage, ready)
    token_same = second_stage(token_own)
    past, later = toeplitz(filters, token_own)
    cotangent = copied(cotangent, past)
    cot_own = own_slice(cotangent, *first_stage(cotangent))
    *token_same, cot_own = relayed([*token_same, cot_own])
    cot_same = second_stage(cot_own)
    proj_part = proj_partial(both_cores(token_same), MINE + OTHERS, 2, weights)
    cot_same = list(relayed(cot_same, proj_part))
    proj, product, conv = conv_forward([proj_part, other_row(proj_part)], past)
    z_part = grad_z_partial(both_cores(cot_same), MINE + OTHERS, 2, out_held)
    grad_proj, grad = conv_backward([z_part, other_row(z_part)], proj, conv, later)
    others = input_partial(OTHERS, 4, rows, weights, grad_proj)
    same = input_partial(MINE, 4, rows, weights, grad_proj)
    return scattered(same, others), taps_gradient(product, grad, filters.shape[0])


def on_any_slice(tokens, values, scales, filters, out_weight, cotangent):
    count = lax.axis_size("fsdp")
    rows = values.shape[1]
    piece = min(rows, 512)
    pieces = rows // piece

    def gather(array):
        whole = lax.all_gather(array, "tensor", axis=1, tiled=True)
        mine = lax.all_to_all(whole, "fsdp", 1, 0, tiled=True)
        return [mine[:, i * piece : (i + 1) * piece] for i in range(pieces)]

    def shares(array):
        every = lax.all_gather(array, "fsdp", axis=0)
        return [every[i] for i in range(count)]

    weights, out_held, _ = prepared(values, scales, out_weight)
    past, later = toeplitz(filters)
    proj_part = proj_partial(gather(tokens), None, 1, weights)
    proj, product, conv = conv_forward(shares(proj_part), past)
    z_part = grad_z_partial(gather(cotangent), None, 1, out_held)
    grad_proj, grad = conv_backward(shares(z_part), proj, conv, later)
    partial = input_partial(None, pieces, piece, weights, grad_proj)
    partial = partial.reshape(rows, partial.shape[2]).astype(F32)
    partial = lax.all_to_all(partial, "fsdp", 1, 0, tiled=True)
    total = lax.psum_scatter(partial, "tensor", scatter_dimension=0, tiled=True)
    return total.T.astype(BF16), taps_gradient(product, grad, filters.shape[0])


def on_device(tokens, in_values, in_scales, filters, out_weight, cotangent):
    values = jnp.transpose(in_values, (1, 0, 2))
    scales = jnp.transpose(in_scales, (1, 0, 2))
    small = lax.axis_size("fsdp") == 2 and lax.axis_size("tensor") == 16
    inner = on_small_slice if small else on_any_slice
    return inner(tokens, values, scales, filters, out_weight, cotangent)


def solution(mesh):
    placed = (
        P("fsdp", "tensor"),
        P("fsdp", None, "tensor"),
        P("fsdp", None, "tensor"),
        P("tensor", None),
        P("tensor", "fsdp"),
        P("fsdp", "tensor"),
    )
    return jax.shard_map(
        on_device,
        mesh=mesh,
        in_specs=placed,
        out_specs=(P("fsdp", "tensor"), P("tensor", None)),
        check_vma=False,
    )
```

```python
import functools

import jax
import jax.numpy as jnp
from jax import lax
from jax.experimental import pallas as pl
from jax.experimental.pallas import tpu as pltpu
from jax.sharding import PartitionSpec as P

BLOCK = 128
TOK_DEV = 128
BF16 = jnp.bfloat16
F32 = jnp.float32
MIB = 1 << 20


def cost(flops, read):
    return pl.CostEstimate(flops=int(flops) >> 12, bytes_accessed=int(read) >> 12, transcendentals=0)


def params(mib):
    return pltpu.CompilerParams(vmem_limit_bytes=mib * MIB)


def in_hbm(array):
    return pltpu.with_memory_space_constraint(array, pltpu.HBM)


VMEM_SPEC = pl.BlockSpec(memory_space=pltpu.VMEM)
SMEM_SPEC = pl.BlockSpec(memory_space=pltpu.SMEM)
LATER_SPEC = pl.BlockSpec(memory_space=pl.ANY)


def copy_kernel(in_ref, *refs):
    refs[-1][...] = in_ref[...]


def copied(array, *earlier):
    return pl.pallas_call(
        copy_kernel,
        in_specs=[VMEM_SPEC] + [LATER_SPEC] * len(earlier),
        out_specs=VMEM_SPEC,
        out_shape=jax.ShapeDtypeStruct(array.shape, array.dtype),
        compiler_params=params(8),
        cost_estimate=cost(0, 4 * array.size),
        name="copied",
    )(array, *earlier)


def at_home():
    return lax.axis_index("tensor") // Z1 == lax.axis_index("fsdp")


def own_kernel(array_ref, turned_ref, crossed_ref, *refs):
    out_ref, sem = refs[-2:]
    run = array_ref.shape[0]
    home = at_home()

    @pl.when(home)
    def _():
        copy = pltpu.make_async_copy(array_ref, out_ref.at[pl.ds(0, run), :], sem)
        copy.start()
        out_ref[run:] = turned_ref[...]
        copy.wait()

    @pl.when(jnp.logical_not(home))
    def _():
        out_ref[:run] = turned_ref[...]
        out_ref[run:] = crossed_ref[...]


def own_slice(array, turned, crossed, *earlier):
    return pl.pallas_call(
        own_kernel,
        in_specs=[LATER_SPEC] + [VMEM_SPEC] * 2 + [LATER_SPEC] * len(earlier),
        out_specs=VMEM_SPEC,
        out_shape=jax.ShapeDtypeStruct((2 * array.shape[0], array.shape[1]), array.dtype),
        scratch_shapes=[pltpu.SemaphoreType.DMA],
        compiler_params=params(8),
        cost_estimate=cost(0, 10 * array.size),
        name="own_slice",
    )(array, turned, crossed, *earlier)


def relay_kernel(*refs):
    del refs


def relayed(arrays, *earlier):
    count = len(arrays)
    return pl.pallas_call(
        relay_kernel,
        in_specs=[LATER_SPEC] * (count + len(earlier)),
        out_specs=[LATER_SPEC] * count,
        out_shape=[jax.ShapeDtypeStruct(array.shape, array.dtype) for array in arrays],
        input_output_aliases={n: n for n in range(count)},
        compiler_params=params(8),
        cost_estimate=cost(0, 0),
        name="relayed",
    )(*arrays, *earlier)


def in_vmem(array):
    return pltpu.with_memory_space_constraint(array, pltpu.VMEM)


AHEAD = 3


def prepare_kernel(v_ref, s_ref, *refs):
    weights, (done_ref, raw, held, ins, in_sems, s_sem) = refs[-9:-6], refs[-6:]
    piece = ins.shape[2]
    pieces = v_ref.shape[1] // piece

    def rows(i):
        return pl.ds(pl.multiple_of(i * piece, BLOCK), piece)

    def fetch(i, j):
        slot = lax.rem(i, AHEAD)
        return pltpu.make_async_copy(
            v_ref.at[j, rows(i), :], ins.at[slot, j], in_sems.at[slot, j]
        )

    scales = pltpu.make_async_copy(s_ref, raw, s_sem)
    scales.start()
    for i in range(min(AHEAD, pieces)):
        for j in range(3):
            fetch(i, j).start()
    scales.wait()
    held[...] = raw[...].astype(F32)
    done_ref[...] = jnp.zeros(done_ref.shape, F32)

    def one(i, carry):
        for j in range(3):
            fetch(i, j).wait()
            for b in range(piece // BLOCK):
                scale = held[j, pl.ds(i * (piece // BLOCK) + b, 1), :]
                at = pl.ds(pl.multiple_of(i * piece + b * BLOCK, BLOCK), BLOCK)
                values = ins[lax.rem(i, AHEAD), j, b * BLOCK : (b + 1) * BLOCK, :]
                weights[j][at, :] = (values.astype(F32) * scale).astype(BF16)

            @pl.when(i + AHEAD < pieces)
            def _(j=j):
                fetch(i + AHEAD, j).start()

        return carry

    lax.fori_loop(0, pieces, one, 0)


def prepared(values, scales, *earlier):
    _, rows, channels = values.shape
    piece = min(rows, 512)
    *weights, ready = pl.pallas_call(
        prepare_kernel,
        in_specs=[LATER_SPEC] * (2 + len(earlier)),
        out_specs=[VMEM_SPEC] * 4,
        out_shape=[pltpu.VMEM((rows, channels), BF16)] * 3
        + [jax.ShapeDtypeStruct((8, 128), F32)],
        scratch_shapes=[
            pltpu.VMEM(scales.shape, BF16),
            pltpu.VMEM(scales.shape, F32),
            pltpu.VMEM((AHEAD, 3, piece, channels), BF16),
            pltpu.SemaphoreType.DMA((AHEAD, 3)),
            pltpu.SemaphoreType.DMA,
        ],
        compiler_params=params(16),
        cost_estimate=cost(values.size * 4, 4 * values.size),
        name="prepare",
    )(in_hbm(values), in_hbm(scales), *earlier)
    return weights, ready


Z1, Z0, X, CORE = 8, 4, 2, 1
MINE = (0, X, Z0, X + Z0)
OTHERS = tuple(mask + CORE for mask in MINE)


def slices_of(masks):
    low = lax.rem(lax.axis_index("tensor"), Z1)
    return [low ^ mask for mask in masks]


def run_starts(runs, run):
    if runs == 1:
        return [0]
    y = lax.axis_index("fsdp")
    return [pl.multiple_of(y * run, BLOCK), pl.multiple_of((1 - y) * run, BLOCK)]


def piece_rows(masks, n, rows):
    if masks is None:
        return pl.ds(n * rows, rows)
    return pl.ds(pl.multiple_of(slices_of(masks)[n] * rows, BLOCK), rows)


def load_kernel(in_ref, *refs):
    out_ref, sem = refs[-2:]
    copy = pltpu.make_async_copy(in_ref, out_ref, sem)
    copy.start()
    copy.wait()


def loaded(array, *earlier):
    return pl.pallas_call(
        load_kernel,
        in_specs=[LATER_SPEC] * (1 + len(earlier)),
        out_specs=VMEM_SPEC,
        out_shape=pltpu.VMEM(array.shape, array.dtype),
        scratch_shapes=[pltpu.SemaphoreType.DMA],
        compiler_params=params(8),
        cost_estimate=cost(0, 4 * array.size),
        name="loaded",
    )(in_hbm(array), *earlier)


def assembled(masks, refs, held):
    for n, ref in enumerate(refs):
        held[:, piece_rows(masks, n, ref.shape[1])] = ref[...]


def proj_part(runs, held_ref, w_ref, out_ref):
    run = held_ref.shape[0] // runs
    total = jnp.dot(held_ref[...], w_ref[...], preferred_element_type=F32)
    for h, start in enumerate(run_starts(runs, run)):
        out_ref[:, pl.ds(start, run)] = total[h * run : (h + 1) * run].T.astype(BF16)


def pair_kernel(masks, runs, *refs):
    xs, (key_ref, value_ref, out_ref, held_ref) = refs[:-4], refs[-4:]
    assembled(masks, xs, held_ref)
    proj_part(runs, held_ref, key_ref, out_ref.at[0])
    proj_part(runs, held_ref, value_ref, out_ref.at[1])


def query_kernel(runs, held_ref, w_ref, out_ref):
    proj_part(runs, held_ref, w_ref, out_ref)


def proj_partial(xs, masks, runs, weights):
    tokens = xs[0].shape[0]
    depth, channels = weights[0].shape
    flops = 2 * tokens * depth * channels
    weights = [in_vmem(weight) for weight in weights]
    pair, held = pl.pallas_call(
        functools.partial(pair_kernel, masks, runs),
        in_specs=[VMEM_SPEC] * (len(xs) + 2),
        out_specs=[VMEM_SPEC] * 2,
        out_shape=[
            jax.ShapeDtypeStruct((2, channels, tokens), BF16),
            pltpu.VMEM((tokens, depth), BF16),
        ],
        compiler_params=params(16),
        cost_estimate=cost(2 * flops, 4 * depth * channels),
        name="proj_pair",
    )(*xs, *weights[1:])
    queries = pl.pallas_call(
        functools.partial(query_kernel, runs),
        in_specs=[VMEM_SPEC] * 2,
        out_specs=VMEM_SPEC,
        out_shape=jax.ShapeDtypeStruct((channels, tokens), BF16),
        compiler_params=params(16),
        cost_estimate=cost(flops, 2 * depth * channels),
        name="proj_queries",
    )(held, weights[0])
    return pair, queries


def grad_z_kernel(masks, runs, *refs):
    xs, (w_ref, out_ref, held) = refs[:-3], refs[-3:]
    assembled(masks, xs, held)
    total = lax.dot_general(
        w_ref[...], held[...], (((1,), (1,)), ((), ())), preferred_element_type=F32
    )
    run = total.shape[1] // runs
    for h, start in enumerate(run_starts(runs, run)):
        out_ref[:, pl.ds(start, run)] = total[:, h * run : (h + 1) * run].astype(BF16)


def grad_z_partial(xs, masks, runs, out_weight):
    tokens = xs[0].shape[0]
    channels, depth = out_weight.shape
    return pl.pallas_call(
        functools.partial(grad_z_kernel, masks, runs),
        in_specs=[VMEM_SPEC] * (len(xs) + 1),
        out_specs=VMEM_SPEC,
        out_shape=jax.ShapeDtypeStruct((channels, tokens), BF16),
        scratch_shapes=[pltpu.VMEM((tokens, depth), BF16)],
        compiler_params=params(16),
        cost_estimate=cost(2 * tokens * depth * channels, 2 * depth * channels),
        name="grad_z_partial",
    )(*xs, in_vmem(out_weight))


def iotas():
    shape = (BLOCK, BLOCK)
    return lax.broadcasted_iota(jnp.int32, shape, 0), lax.broadcasted_iota(jnp.int32, shape, 1)


def sheared(array):
    return pltpu.roll(array, 0, 1, stride=1, stride_axis=0)


def toeplitz_kernel(taps_ref, *refs):
    past_ref, next_ref = refs[-2:]
    row, lane = iotas()
    for g in range(taps_ref.shape[0]):
        ahead = sheared(jnp.broadcast_to(taps_ref[g : g + 1, :], (BLOCK, BLOCK)))
        behind = ahead.T
        past_ref[g, :BLOCK] = jnp.where(lane < row, ahead, 0.0).astype(BF16)
        past_ref[g, BLOCK:] = jnp.where(lane >= row, ahead, 0.0).astype(BF16)
        next_ref[g, :BLOCK] = jnp.where(lane <= row, behind, 0.0).astype(BF16)
        next_ref[g, BLOCK:] = jnp.where(lane > row, behind, 0.0).astype(BF16)


def toeplitz(filters, *earlier):
    groups, taps = filters.shape
    step = min(8, groups)
    shape = pltpu.VMEM((groups, 2 * BLOCK, taps), BF16)
    return pl.pallas_call(
        toeplitz_kernel,
        grid=(groups // step,),
        in_specs=[pl.BlockSpec((step, taps), lambda i: (i, 0))]
        + [LATER_SPEC] * len(earlier),
        out_specs=[pl.BlockSpec((step, 2 * BLOCK, taps), lambda i: (i, 0, 0))] * 2,
        out_shape=[shape, shape],
        compiler_params=params(16),
        cost_estimate=cost(groups * taps * 2000, groups * taps * 1024),
        name="toeplitz",
    )(filters, *earlier)


def block_of(array, i):
    blocks = array.shape[1] // BLOCK
    if 0 <= i < blocks:
        return array[:, i * BLOCK : (i + 1) * BLOCK]
    return jnp.zeros((array.shape[0], BLOCK), array.dtype)


def paired(array, by):
    blocks = array.shape[1] // BLOCK
    low, high = min(by, 0), max(by, 0)
    return jnp.concatenate(
        [
            jnp.concatenate([block_of(array, i + low), block_of(array, i + high)], 1)
            for i in range(blocks)
        ],
        0,
    )


def unstacked(array, blocks):
    rows = array.shape[0] // blocks
    return jnp.concatenate([array[i * rows : (i + 1) * rows] for i in range(blocks)], 1)


def summed(refs, part=...):
    total = refs[0][part].astype(F32)
    for ref in refs[1:]:
        total = total + ref[part].astype(F32)
    return total.astype(BF16)


def conv_kernel(parts, groups, *refs):
    shares, (past_ref, pair_ref, prod_ref, conv_ref) = refs[:parts], refs[parts:]
    key, value = summed(shares, 0), summed(shares, 1)
    pair_ref[0] = key
    pair_ref[1] = value
    product = (key.astype(F32) * value.astype(F32)).astype(BF16)
    prod_ref[...] = product
    channels, tokens = product.shape
    per = channels // groups
    for g in range(groups):
        rows = slice(g * per, (g + 1) * per)
        result = jnp.dot(paired(product[rows], -1), past_ref[g], preferred_element_type=F32)
        conv_ref[rows] = unstacked(result, tokens // BLOCK)


def conv_forward(shares, past):
    _, channels, tokens = shares[0].shape
    groups = past.shape[0]
    steps = max(1, groups // 16)
    chunk = channels // steps
    parts = len(shares)
    two = pl.BlockSpec((2, chunk, tokens), lambda i: (0, i, 0))
    one = pl.BlockSpec((chunk, tokens), lambda i: (i, 0))
    return pl.pallas_call(
        functools.partial(conv_kernel, parts, groups // steps),
        grid=(steps,),
        in_specs=[two] * parts
        + [pl.BlockSpec((groups // steps,) + past.shape[1:], lambda i: (i, 0, 0))],
        out_specs=[two, one, one],
        out_shape=[
            jax.ShapeDtypeStruct((2, channels, tokens), BF16),
            jax.ShapeDtypeStruct((channels, tokens), BF16),
            jax.ShapeDtypeStruct((channels, tokens), F32),
        ],
        compiler_params=params(16),
        cost_estimate=cost(4 * channels * tokens * BLOCK * 8, channels * tokens * 24),
        name="conv_forward",
    )(*shares, past)


def conv_back_kernel(parts, groups, *refs):
    shares, queries = refs[:parts], refs[parts : 2 * parts]
    pair_ref, conv_ref, next_ref, out_ref, grad_ref = refs[2 * parts :]
    grad_z = shares[0][...].astype(F32)
    for ref in shares[1:]:
        grad_z = grad_z + ref[...].astype(F32)
    out_ref[0] = (grad_z * conv_ref[...]).astype(BF16)
    grad = (grad_z * summed(queries).astype(F32)).astype(BF16)
    grad_ref[...] = grad
    channels, tokens = grad.shape
    per = channels // groups
    for g in range(groups):
        rows = slice(g * per, (g + 1) * per)
        result = jnp.dot(paired(grad[rows], 1), next_ref[g], preferred_element_type=F32)
        result = unstacked(result, tokens // BLOCK)
        out_ref[1, rows] = (result * pair_ref[1, rows].astype(F32)).astype(BF16)
        out_ref[2, rows] = (result * pair_ref[0, rows].astype(F32)).astype(BF16)


def conv_backward(shares, queries, pair, conv, after):
    channels, tokens = conv.shape
    groups = after.shape[0]
    steps = max(1, groups // 16)
    chunk = channels // steps
    parts = len(shares)
    three = pl.BlockSpec((3, chunk, tokens), lambda i: (0, i, 0))
    one = pl.BlockSpec((chunk, tokens), lambda i: (i, 0))
    return pl.pallas_call(
        functools.partial(conv_back_kernel, parts, groups // steps),
        grid=(steps,),
        in_specs=[one] * (2 * parts)
        + [
            pl.BlockSpec((2, chunk, tokens), lambda i: (0, i, 0)),
            one,
            pl.BlockSpec((groups // steps,) + after.shape[1:], lambda i: (i, 0, 0)),
        ],
        out_specs=[three, one],
        out_shape=[
            jax.ShapeDtypeStruct((3, channels, tokens), BF16),
            jax.ShapeDtypeStruct((channels, tokens), BF16),
        ],
        compiler_params=params(16),
        cost_estimate=cost(4 * channels * tokens * BLOCK * 8, channels * tokens * 24),
        name="conv_backward",
    )(*shares, *queries, pair, conv, after)


def taps_kernel(groups, prod_ref, grad_ref, out_ref):
    row, lane = iotas()
    flip = (row + lane == BLOCK - 1).astype(F32).astype(BF16)
    channels, tokens = prod_ref.shape
    per = channels // groups
    blocks = tokens // BLOCK

    def cut(ref, i):
        return ref[:, i * BLOCK : (i + 1) * BLOCK]

    turned = [
        jnp.dot(cut(prod_ref, i), flip, preferred_element_type=F32).astype(BF16)
        for i in range(blocks)
    ]
    grad = [cut(grad_ref, i) for i in range(blocks)]

    def correlated(earlier, later, rows):
        return lax.dot_general(
            jnp.concatenate([block[rows] for block in earlier], 0),
            jnp.concatenate([block[rows] for block in later], 0),
            (((0,), (0,)), ((), ())),
            preferred_element_type=F32,
        )

    for g in range(groups):
        rows = slice(g * per, (g + 1) * per)
        within = correlated(turned, grad, rows)
        before = correlated(turned[:-1], grad[1:], rows)
        folded = jnp.where(row + lane >= BLOCK - 1, within, before)
        out_ref[g : g + 1, :] = jnp.sum(sheared(folded), axis=0, keepdims=True)
    out_ref[...] = pltpu.roll(out_ref[...], 1, 1) / TOK_DEV


def taps_gradient(product, grad, groups):
    channels, tokens = product.shape
    steps = max(1, groups // 8)
    chunk = channels // steps
    one = pl.BlockSpec((chunk, tokens), lambda i: (i, 0))
    return pl.pallas_call(
        functools.partial(taps_kernel, groups // steps),
        grid=(steps,),
        in_specs=[one, one],
        out_specs=pl.BlockSpec((groups // steps, BLOCK), lambda i: (i, 0)),
        out_shape=jax.ShapeDtypeStruct((groups, BLOCK), F32),
        compiler_params=params(16),
        cost_estimate=cost(4 * channels * tokens * BLOCK * 8, channels * tokens * 24),
        name="taps_gradient",
    )(product, grad)


def input_kernel(masks, *refs):
    w_refs, (g_ref, out_ref) = refs[:3], refs[3:]
    pieces, rows, _ = out_ref.shape
    for i in range(pieces):
        at = piece_rows(masks, i, rows)
        w = jnp.concatenate([ref[at, :] for ref in w_refs], 1)
        out_ref[i] = jnp.dot(w, g_ref[...], preferred_element_type=F32).astype(BF16)


def input_partial(masks, pieces, rows, weights, grad_proj):
    _, channels, tokens = grad_proj.shape
    return pl.pallas_call(
        functools.partial(input_kernel, masks),
        in_specs=[VMEM_SPEC] * 4,
        out_specs=VMEM_SPEC,
        out_shape=jax.ShapeDtypeStruct((pieces, rows, tokens), BF16),
        compiler_params=params(16),
        cost_estimate=cost(
            2 * tokens * pieces * rows * 3 * channels, 2 * pieces * rows * (3 * channels + tokens)
        ),
        name="input_partial",
    )(*[in_vmem(weight) for weight in weights], grad_proj.reshape(3 * channels, tokens))


def across(array, mask):
    return lax.ppermute(array, "tensor", [(i, i ^ mask) for i in range(16)])


def other_row(array):
    return lax.ppermute(array, "fsdp", [(0, 1), (1, 0)])


def in_square(array, turn):
    pairs = []
    for i in range(32):
        y, k = divmod(i, 16)
        target = turn(y, k // Z1)
        if target is not None:
            pairs.append((i, target[0] * 16 + target[1] * Z1 + k % Z1))
    return lax.ppermute(array, ("fsdp", "tensor"), pairs)


def from_turn(y, z1):
    return (y, 1 - z1) if y == z1 else (1 - y, z1)


def over_diagonal(y, z1):
    return None if y == z1 else (1 - y, 1 - z1)


def first_stage(array):
    return in_square(array, from_turn), in_square(array, over_diagonal)


def second_stage(own):
    return [own] + [across(own, mask) for mask in MINE[1:]]


def both_cores(same):
    return same + [across(piece, CORE) for piece in same]


def split_kernel(same_ref, got_ref, *out_refs):
    pieces = same_ref.shape[0]
    y = lax.axis_index("fsdp")
    leave = pl.ds(pl.multiple_of((1 - y) * TOK_DEV, BLOCK), TOK_DEV)
    stay = pl.ds(pl.multiple_of(y * TOK_DEV, BLOCK), TOK_DEV)
    for n in range(pieces):
        for at, out_ref in ((leave, out_refs[n]), (stay, out_refs[pieces + n])):
            total = same_ref[n, :, at].astype(F32) + got_ref[n, :, at].astype(F32)
            out_ref[...] = total.astype(BF16)


def split(same, got):
    pieces, rows, _ = same.shape
    out = jax.ShapeDtypeStruct((rows, TOK_DEV), BF16)
    halves = pl.pallas_call(
        split_kernel,
        in_specs=[VMEM_SPEC] * 2,
        out_specs=[VMEM_SPEC] * (2 * pieces),
        out_shape=[out] * (2 * pieces),
        compiler_params=params(8),
        cost_estimate=cost(0, 6 * same.size),
        name="split",
    )(same, got)
    return halves[:pieces], halves[pieces:]


def sum_kernel(*refs):
    total = refs[0][...].astype(F32)
    for ref in refs[1:-1]:
        total = total + ref[...].astype(F32)
    refs[-1][...] = total.astype(BF16)


def total_of(pieces):
    return pl.pallas_call(
        sum_kernel,
        in_specs=[VMEM_SPEC] * len(pieces),
        out_specs=VMEM_SPEC,
        out_shape=jax.ShapeDtypeStruct(pieces[0].shape, BF16),
        compiler_params=params(8),
        cost_estimate=cost(0, 8 * pieces[0].size),
        name="total",
    )(*pieces)


def sides_kernel(near_ref, far_ref, keep_ref, send_ref):
    home = at_home()

    @pl.when(home)
    def _():
        keep_ref[...] = near_ref[...]
        send_ref[...] = far_ref[...]

    @pl.when(jnp.logical_not(home))
    def _():
        keep_ref[...] = far_ref[...]
        send_ref[...] = near_ref[...]


def sides(near, far):
    out = jax.ShapeDtypeStruct(near.shape, BF16)
    return pl.pallas_call(
        sides_kernel,
        in_specs=[VMEM_SPEC] * 2,
        out_specs=[VMEM_SPEC] * 2,
        out_shape=[out] * 2,
        compiler_params=params(8),
        cost_estimate=cost(0, 8 * near.size),
        name="sides",
    )(near, far)


def last_kernel(keep_ref, got_ref, out_ref):
    total = keep_ref[...].astype(F32) + got_ref[...].astype(F32)
    out_ref[...] = total.T.astype(BF16)


def last_sum(keep, got):
    return pl.pallas_call(
        last_kernel,
        in_specs=[VMEM_SPEC] * 2,
        out_specs=VMEM_SPEC,
        out_shape=jax.ShapeDtypeStruct(keep.shape[::-1], BF16),
        compiler_params=params(8),
        cost_estimate=cost(0, 6 * keep.size),
        name="last_sum",
    )(keep, got)


def moved(pieces):
    return [pieces[0]] + [across(piece, mask) for piece, mask in zip(pieces[1:], MINE[1:])]


def scattered(same, others):
    leave, stay = split(same, across(others, CORE))
    leave, stay = moved(leave), moved(stay)
    far = other_row(total_of(leave))
    keep, send = sides(total_of(stay), far)
    return last_sum(keep, across(send, Z1))


def on_small_slice(tokens, values, scales, filters, out_weight, cotangent):
    rows = tokens.shape[1]
    token_stage = first_stage(tokens)
    weights, ready = prepared(values, scales)
    token_own = own_slice(in_hbm(tokens), *token_stage, ready)
    token_same = second_stage(token_own)
    past, later = toeplitz(filters, token_own)
    out_held = loaded(out_weight, past)
    cotangent = copied(cotangent, token_own)
    cot_own = own_slice(cotangent, *first_stage(cotangent))
    *token_same, cot_own = relayed([*token_same, cot_own], out_held)
    cot_same = second_stage(cot_own)
    pair, queries = proj_partial(both_cores(token_same), MINE + OTHERS, 2, weights)
    cot_same = list(relayed(cot_same, queries))
    pair, product, conv = conv_forward([pair, other_row(pair)], past)
    z_part = grad_z_partial(both_cores(cot_same), MINE + OTHERS, 2, out_held)
    grad_proj, grad = conv_backward(
        [z_part, other_row(z_part)], [queries, other_row(queries)], pair, conv, later
    )
    others = input_partial(OTHERS, 4, rows, weights, grad_proj)
    same = input_partial(MINE, 4, rows, weights, grad_proj)
    return scattered(same, others), taps_gradient(product, grad, filters.shape[0])


def on_any_slice(tokens, values, scales, filters, out_weight, cotangent):
    count = lax.axis_size("fsdp")
    rows = values.shape[1]
    piece = min(rows, 512)
    pieces = rows // piece

    def gather(array):
        whole = lax.all_gather(array, "tensor", axis=1, tiled=True)
        mine = lax.all_to_all(whole, "fsdp", 1, 0, tiled=True)
        return [mine[:, i * piece : (i + 1) * piece] for i in range(pieces)]

    def shares(array):
        every = lax.all_gather(array, "fsdp", axis=0)
        return [every[i] for i in range(count)]

    weights, _ = prepared(values, scales)
    out_held = loaded(out_weight)
    past, later = toeplitz(filters)
    pair, queries = proj_partial(gather(tokens), None, 1, weights)
    pair, product, conv = conv_forward(shares(pair), past)
    z_part = grad_z_partial(gather(cotangent), None, 1, out_held)
    grad_proj, grad = conv_backward(shares(z_part), shares(queries), pair, conv, later)
    partial = input_partial(None, pieces, piece, weights, grad_proj)
    partial = partial.reshape(rows, partial.shape[2]).astype(F32)
    partial = lax.all_to_all(partial, "fsdp", 1, 0, tiled=True)
    total = lax.psum_scatter(partial, "tensor", scatter_dimension=0, tiled=True)
    return total.T.astype(BF16), taps_gradient(product, grad, filters.shape[0])


def on_device(tokens, in_values, in_scales, filters, out_weight, cotangent):
    values = jnp.transpose(in_values, (1, 0, 2))
    scales = jnp.transpose(in_scales, (1, 0, 2))
    small = lax.axis_size("fsdp") == 2 and lax.axis_size("tensor") == 16
    inner = on_small_slice if small else on_any_slice
    return inner(tokens, values, scales, filters, out_weight, cotangent)


def solution(mesh):
    placed = (
        P("fsdp", "tensor"),
        P("fsdp", None, "tensor"),
        P("fsdp", None, "tensor"),
        P("tensor", None),
        P("tensor", "fsdp"),
        P("fsdp", "tensor"),
    )
    return jax.shard_map(
        on_device,
        mesh=mesh,
        in_specs=placed,
        out_specs=(P("fsdp", "tensor"), P("tensor", None)),
        check_vma=False,
    )
```

```python
import functools

import jax
import jax.numpy as jnp
from jax import lax
from jax.experimental import pallas as pl
from jax.experimental.pallas import tpu as pltpu
from jax.sharding import PartitionSpec as P

BLOCK = 128
TOK_DEV = 128
BF16 = jnp.bfloat16
F32 = jnp.float32
MIB = 1 << 20


def cost(flops, read):
    return pl.CostEstimate(flops=int(flops) >> 12, bytes_accessed=int(read) >> 12, transcendentals=0)


def params(mib):
    return pltpu.CompilerParams(vmem_limit_bytes=mib * MIB)


def in_hbm(array):
    return pltpu.with_memory_space_constraint(array, pltpu.HBM)


VMEM_SPEC = pl.BlockSpec(memory_space=pltpu.VMEM)
SMEM_SPEC = pl.BlockSpec(memory_space=pltpu.SMEM)
LATER_SPEC = pl.BlockSpec(memory_space=pl.ANY)


def copy_kernel(in_ref, *refs):
    refs[-1][...] = in_ref[...]


def copied(array, *earlier):
    return pl.pallas_call(
        copy_kernel,
        in_specs=[VMEM_SPEC] + [LATER_SPEC] * len(earlier),
        out_specs=VMEM_SPEC,
        out_shape=jax.ShapeDtypeStruct(array.shape, array.dtype),
        compiler_params=params(8),
        cost_estimate=cost(0, 4 * array.size),
        name="copied",
    )(array, *earlier)


def at_home():
    return lax.axis_index("tensor") // Z1 == lax.axis_index("fsdp")


def own_kernel(array_ref, turned_ref, crossed_ref, *refs):
    out_ref, sem = refs[-2:]
    run = array_ref.shape[0]
    home = at_home()

    @pl.when(home)
    def _():
        copy = pltpu.make_async_copy(array_ref, out_ref.at[pl.ds(0, run), :], sem)
        copy.start()
        out_ref[run:] = turned_ref[...]
        copy.wait()

    @pl.when(jnp.logical_not(home))
    def _():
        out_ref[:run] = turned_ref[...]
        out_ref[run:] = crossed_ref[...]


def own_slice(array, turned, crossed, *earlier):
    return pl.pallas_call(
        own_kernel,
        in_specs=[LATER_SPEC] + [VMEM_SPEC] * 2 + [LATER_SPEC] * len(earlier),
        out_specs=VMEM_SPEC,
        out_shape=jax.ShapeDtypeStruct((2 * array.shape[0], array.shape[1]), array.dtype),
        scratch_shapes=[pltpu.SemaphoreType.DMA],
        compiler_params=params(8),
        cost_estimate=cost(0, 10 * array.size),
        name="own_slice",
    )(array, turned, crossed, *earlier)


def relay_kernel(*refs):
    del refs


def relayed(arrays, *earlier):
    count = len(arrays)
    return pl.pallas_call(
        relay_kernel,
        in_specs=[LATER_SPEC] * (count + len(earlier)),
        out_specs=[LATER_SPEC] * count,
        out_shape=[jax.ShapeDtypeStruct(array.shape, array.dtype) for array in arrays],
        input_output_aliases={n: n for n in range(count)},
        compiler_params=params(8),
        cost_estimate=cost(0, 0),
        name="relayed",
    )(*arrays, *earlier)


def in_vmem(array):
    return pltpu.with_memory_space_constraint(array, pltpu.VMEM)


AHEAD = 3


def prepare_kernel(v_ref, s_ref, *refs):
    weights, (done_ref, raw, held, ins, in_sems, s_sem) = refs[-9:-6], refs[-6:]
    piece = ins.shape[2]
    pieces = v_ref.shape[1] // piece

    def rows(i):
        return pl.ds(pl.multiple_of(i * piece, BLOCK), piece)

    def fetch(i, j):
        slot = lax.rem(i, AHEAD)
        return pltpu.make_async_copy(
            v_ref.at[j, rows(i), :], ins.at[slot, j], in_sems.at[slot, j]
        )

    scales = pltpu.make_async_copy(s_ref, raw, s_sem)
    scales.start()
    for i in range(min(AHEAD, pieces)):
        for j in range(3):
            fetch(i, j).start()
    scales.wait()
    held[...] = raw[...].astype(F32)
    done_ref[...] = jnp.zeros(done_ref.shape, F32)

    def one(i, carry):
        for j in range(3):
            fetch(i, j).wait()
            for b in range(piece // BLOCK):
                scale = held[j, pl.ds(i * (piece // BLOCK) + b, 1), :]
                at = pl.ds(pl.multiple_of(i * piece + b * BLOCK, BLOCK), BLOCK)
                values = ins[lax.rem(i, AHEAD), j, b * BLOCK : (b + 1) * BLOCK, :]
                weights[j][at, :] = (values.astype(F32) * scale).astype(BF16)

            @pl.when(i + AHEAD < pieces)
            def _(j=j):
                fetch(i + AHEAD, j).start()

        return carry

    lax.fori_loop(0, pieces, one, 0)


def prepared(values, scales, *earlier):
    _, rows, channels = values.shape
    piece = min(rows, 512)
    *weights, ready = pl.pallas_call(
        prepare_kernel,
        in_specs=[LATER_SPEC] * (2 + len(earlier)),
        out_specs=[VMEM_SPEC] * 4,
        out_shape=[pltpu.VMEM((rows, channels), BF16)] * 3
        + [jax.ShapeDtypeStruct((8, 128), F32)],
        scratch_shapes=[
            pltpu.VMEM(scales.shape, BF16),
            pltpu.VMEM(scales.shape, F32),
            pltpu.VMEM((AHEAD, 3, piece, channels), BF16),
            pltpu.SemaphoreType.DMA((AHEAD, 3)),
            pltpu.SemaphoreType.DMA,
        ],
        compiler_params=params(16),
        cost_estimate=cost(values.size * 4, 4 * values.size),
        name="prepare",
    )(in_hbm(values), in_hbm(scales), *earlier)
    return weights, ready


Z1, Z0, X, CORE = 8, 4, 2, 1
MINE = (0, Z0, X, X + Z0)
OTHERS = tuple(mask + CORE for mask in MINE)


def slices_of(masks):
    low = lax.rem(lax.axis_index("tensor"), Z1)
    return [low ^ mask for mask in masks]


def run_starts(runs, run):
    if runs == 1:
        return [0]
    y = lax.axis_index("fsdp")
    return [pl.multiple_of(y * run, BLOCK), pl.multiple_of((1 - y) * run, BLOCK)]


def piece_rows(masks, n, rows):
    if masks is None:
        return pl.ds(n * rows, rows)
    return pl.ds(pl.multiple_of(slices_of(masks)[n] * rows, BLOCK), rows)


def load_kernel(in_ref, *refs):
    out_ref, sem = refs[-2:]
    copy = pltpu.make_async_copy(in_ref, out_ref, sem)
    copy.start()
    copy.wait()


def loaded(array, *earlier):
    return pl.pallas_call(
        load_kernel,
        in_specs=[LATER_SPEC] * (1 + len(earlier)),
        out_specs=VMEM_SPEC,
        out_shape=pltpu.VMEM(array.shape, array.dtype),
        scratch_shapes=[pltpu.SemaphoreType.DMA],
        compiler_params=params(8),
        cost_estimate=cost(0, 4 * array.size),
        name="loaded",
    )(in_hbm(array), *earlier)


def assembled(masks, refs, held):
    for n, ref in enumerate(refs):
        held[:, piece_rows(masks, n, ref.shape[1])] = ref[...]


def proj_part(runs, held_ref, w_ref, out_ref):
    run = held_ref.shape[0] // runs
    total = jnp.dot(held_ref[...], w_ref[...], preferred_element_type=F32)
    for h, start in enumerate(run_starts(runs, run)):
        out_ref[:, pl.ds(start, run)] = total[h * run : (h + 1) * run].T.astype(BF16)


def pair_kernel(masks, runs, *refs):
    xs, (key_ref, value_ref, out_ref, held_ref) = refs[:-4], refs[-4:]
    assembled(masks, xs, held_ref)
    proj_part(runs, held_ref, key_ref, out_ref.at[0])
    proj_part(runs, held_ref, value_ref, out_ref.at[1])


def query_kernel(runs, held_ref, w_ref, out_ref):
    proj_part(runs, held_ref, w_ref, out_ref)


def proj_partial(xs, masks, runs, weights):
    tokens = xs[0].shape[0]
    depth, channels = weights[0].shape
    flops = 2 * tokens * depth * channels
    weights = [in_vmem(weight) for weight in weights]
    pair, held = pl.pallas_call(
        functools.partial(pair_kernel, masks, runs),
        in_specs=[VMEM_SPEC] * (len(xs) + 2),
        out_specs=[VMEM_SPEC] * 2,
        out_shape=[
            jax.ShapeDtypeStruct((2, channels, tokens), BF16),
            pltpu.VMEM((tokens, depth), BF16),
        ],
        compiler_params=params(16),
        cost_estimate=cost(2 * flops, 4 * depth * channels),
        name="proj_pair",
    )(*xs, *weights[1:])
    queries = pl.pallas_call(
        functools.partial(query_kernel, runs),
        in_specs=[VMEM_SPEC] * 2,
        out_specs=VMEM_SPEC,
        out_shape=jax.ShapeDtypeStruct((channels, tokens), BF16),
        compiler_params=params(16),
        cost_estimate=cost(flops, 2 * depth * channels),
        name="proj_queries",
    )(held, weights[0])
    return pair, queries


def grad_z_kernel(masks, runs, *refs):
    xs, (w_ref, out_ref, held) = refs[:-3], refs[-3:]
    assembled(masks, xs, held)
    total = lax.dot_general(
        w_ref[...], held[...], (((1,), (1,)), ((), ())), preferred_element_type=F32
    )
    run = total.shape[1] // runs
    for h, start in enumerate(run_starts(runs, run)):
        out_ref[:, pl.ds(start, run)] = total[:, h * run : (h + 1) * run].astype(BF16)


def grad_z_partial(xs, masks, runs, out_weight):
    tokens = xs[0].shape[0]
    channels, depth = out_weight.shape
    return pl.pallas_call(
        functools.partial(grad_z_kernel, masks, runs),
        in_specs=[VMEM_SPEC] * (len(xs) + 1),
        out_specs=VMEM_SPEC,
        out_shape=jax.ShapeDtypeStruct((channels, tokens), BF16),
        scratch_shapes=[pltpu.VMEM((tokens, depth), BF16)],
        compiler_params=params(16),
        cost_estimate=cost(2 * tokens * depth * channels, 2 * depth * channels),
        name="grad_z_partial",
    )(*xs, in_vmem(out_weight))


def iotas():
    shape = (BLOCK, BLOCK)
    return lax.broadcasted_iota(jnp.int32, shape, 0), lax.broadcasted_iota(jnp.int32, shape, 1)


def sheared(array):
    return pltpu.roll(array, 0, 1, stride=1, stride_axis=0)


def toeplitz_kernel(taps_ref, *refs):
    past_ref, next_ref = refs[-2:]
    row, lane = iotas()
    for g in range(taps_ref.shape[0]):
        ahead = sheared(jnp.broadcast_to(taps_ref[g : g + 1, :], (BLOCK, BLOCK)))
        behind = ahead.T
        past_ref[g, :BLOCK] = jnp.where(lane < row, ahead, 0.0).astype(BF16)
        past_ref[g, BLOCK:] = jnp.where(lane >= row, ahead, 0.0).astype(BF16)
        next_ref[g, :BLOCK] = jnp.where(lane <= row, behind, 0.0).astype(BF16)
        next_ref[g, BLOCK:] = jnp.where(lane > row, behind, 0.0).astype(BF16)


def toeplitz(filters, *earlier):
    groups, taps = filters.shape
    step = min(8, groups)
    shape = pltpu.VMEM((groups, 2 * BLOCK, taps), BF16)
    return pl.pallas_call(
        toeplitz_kernel,
        grid=(groups // step,),
        in_specs=[pl.BlockSpec((step, taps), lambda i: (i, 0))]
        + [LATER_SPEC] * len(earlier),
        out_specs=[pl.BlockSpec((step, 2 * BLOCK, taps), lambda i: (i, 0, 0))] * 2,
        out_shape=[shape, shape],
        compiler_params=params(16),
        cost_estimate=cost(groups * taps * 2000, groups * taps * 1024),
        name="toeplitz",
    )(filters, *earlier)


def block_of(array, i):
    blocks = array.shape[1] // BLOCK
    if 0 <= i < blocks:
        return array[:, i * BLOCK : (i + 1) * BLOCK]
    return jnp.zeros((array.shape[0], BLOCK), array.dtype)


def paired(array, by):
    blocks = array.shape[1] // BLOCK
    low, high = min(by, 0), max(by, 0)
    return jnp.concatenate(
        [
            jnp.concatenate([block_of(array, i + low), block_of(array, i + high)], 1)
            for i in range(blocks)
        ],
        0,
    )


def unstacked(array, blocks):
    rows = array.shape[0] // blocks
    return jnp.concatenate([array[i * rows : (i + 1) * rows] for i in range(blocks)], 1)


def summed(refs, part=...):
    total = refs[0][part].astype(F32)
    for ref in refs[1:]:
        total = total + ref[part].astype(F32)
    return total.astype(BF16)


def conv_kernel(parts, groups, *refs):
    shares, (past_ref, pair_ref, prod_ref, conv_ref) = refs[:parts], refs[parts:]
    key, value = summed(shares, 0), summed(shares, 1)
    pair_ref[0] = key
    pair_ref[1] = value
    product = (key.astype(F32) * value.astype(F32)).astype(BF16)
    prod_ref[...] = product
    channels, tokens = product.shape
    per = channels // groups
    for g in range(groups):
        rows = slice(g * per, (g + 1) * per)
        result = jnp.dot(paired(product[rows], -1), past_ref[g], preferred_element_type=F32)
        conv_ref[rows] = unstacked(result, tokens // BLOCK)


def conv_forward(shares, past):
    _, channels, tokens = shares[0].shape
    groups = past.shape[0]
    steps = max(1, groups // 16)
    chunk = channels // steps
    parts = len(shares)
    two = pl.BlockSpec((2, chunk, tokens), lambda i: (0, i, 0))
    one = pl.BlockSpec((chunk, tokens), lambda i: (i, 0))
    return pl.pallas_call(
        functools.partial(conv_kernel, parts, groups // steps),
        grid=(steps,),
        in_specs=[two] * parts
        + [pl.BlockSpec((groups // steps,) + past.shape[1:], lambda i: (i, 0, 0))],
        out_specs=[two, one, one],
        out_shape=[
            jax.ShapeDtypeStruct((2, channels, tokens), BF16),
            jax.ShapeDtypeStruct((channels, tokens), BF16),
            jax.ShapeDtypeStruct((channels, tokens), F32),
        ],
        compiler_params=params(16),
        cost_estimate=cost(4 * channels * tokens * BLOCK * 8, channels * tokens * 24),
        name="conv_forward",
    )(*shares, past)


def conv_back_kernel(parts, groups, *refs):
    shares, queries = refs[:parts], refs[parts : 2 * parts]
    pair_ref, conv_ref, next_ref, out_ref, grad_ref = refs[2 * parts :]
    grad_z = shares[0][...].astype(F32)
    for ref in shares[1:]:
        grad_z = grad_z + ref[...].astype(F32)
    out_ref[0] = (grad_z * conv_ref[...]).astype(BF16)
    grad = (grad_z * summed(queries).astype(F32)).astype(BF16)
    grad_ref[...] = grad
    channels, tokens = grad.shape
    per = channels // groups
    for g in range(groups):
        rows = slice(g * per, (g + 1) * per)
        result = jnp.dot(paired(grad[rows], 1), next_ref[g], preferred_element_type=F32)
        result = unstacked(result, tokens // BLOCK)
        out_ref[1, rows] = (result * pair_ref[1, rows].astype(F32)).astype(BF16)
        out_ref[2, rows] = (result * pair_ref[0, rows].astype(F32)).astype(BF16)


def conv_backward(shares, queries, pair, conv, after):
    channels, tokens = conv.shape
    groups = after.shape[0]
    steps = max(1, groups // 16)
    chunk = channels // steps
    parts = len(shares)
    three = pl.BlockSpec((3, chunk, tokens), lambda i: (0, i, 0))
    one = pl.BlockSpec((chunk, tokens), lambda i: (i, 0))
    return pl.pallas_call(
        functools.partial(conv_back_kernel, parts, groups // steps),
        grid=(steps,),
        in_specs=[one] * (2 * parts)
        + [
            pl.BlockSpec((2, chunk, tokens), lambda i: (0, i, 0)),
            one,
            pl.BlockSpec((groups // steps,) + after.shape[1:], lambda i: (i, 0, 0)),
        ],
        out_specs=[three, one],
        out_shape=[
            jax.ShapeDtypeStruct((3, channels, tokens), BF16),
            jax.ShapeDtypeStruct((channels, tokens), BF16),
        ],
        compiler_params=params(16),
        cost_estimate=cost(4 * channels * tokens * BLOCK * 8, channels * tokens * 24),
        name="conv_backward",
    )(*shares, *queries, pair, conv, after)


def taps_kernel(groups, prod_ref, grad_ref, out_ref):
    row, lane = iotas()
    flip = (row + lane == BLOCK - 1).astype(F32).astype(BF16)
    channels, tokens = prod_ref.shape
    per = channels // groups
    blocks = tokens // BLOCK

    def cut(ref, i):
        return ref[:, i * BLOCK : (i + 1) * BLOCK]

    turned = [
        jnp.dot(cut(prod_ref, i), flip, preferred_element_type=F32).astype(BF16)
        for i in range(blocks)
    ]
    grad = [cut(grad_ref, i) for i in range(blocks)]

    def correlated(earlier, later, rows):
        return lax.dot_general(
            jnp.concatenate([block[rows] for block in earlier], 0),
            jnp.concatenate([block[rows] for block in later], 0),
            (((0,), (0,)), ((), ())),
            preferred_element_type=F32,
        )

    for g in range(groups):
        rows = slice(g * per, (g + 1) * per)
        within = correlated(turned, grad, rows)
        before = correlated(turned[:-1], grad[1:], rows)
        folded = jnp.where(row + lane >= BLOCK - 1, within, before)
        out_ref[g : g + 1, :] = jnp.sum(sheared(folded), axis=0, keepdims=True)
    out_ref[...] = pltpu.roll(out_ref[...], 1, 1) / TOK_DEV


def taps_gradient(product, grad, groups):
    channels, tokens = product.shape
    steps = max(1, groups // 8)
    chunk = channels // steps
    one = pl.BlockSpec((chunk, tokens), lambda i: (i, 0))
    return pl.pallas_call(
        functools.partial(taps_kernel, groups // steps),
        grid=(steps,),
        in_specs=[one, one],
        out_specs=pl.BlockSpec((groups // steps, BLOCK), lambda i: (i, 0)),
        out_shape=jax.ShapeDtypeStruct((groups, BLOCK), F32),
        compiler_params=params(16),
        cost_estimate=cost(4 * channels * tokens * BLOCK * 8, channels * tokens * 24),
        name="taps_gradient",
    )(product, grad)


def input_kernel(masks, *refs):
    w_refs, (g_ref, out_ref) = refs[:3], refs[3:]
    pieces, rows, _ = out_ref.shape
    for i in range(pieces):
        at = piece_rows(masks, i, rows)
        w = jnp.concatenate([ref[at, :] for ref in w_refs], 1)
        out_ref[i] = jnp.dot(w, g_ref[...], preferred_element_type=F32).astype(BF16)


def input_partial(masks, pieces, rows, weights, grad_proj):
    _, channels, tokens = grad_proj.shape
    return pl.pallas_call(
        functools.partial(input_kernel, masks),
        in_specs=[VMEM_SPEC] * 4,
        out_specs=VMEM_SPEC,
        out_shape=jax.ShapeDtypeStruct((pieces, rows, tokens), BF16),
        compiler_params=params(16),
        cost_estimate=cost(
            2 * tokens * pieces * rows * 3 * channels, 2 * pieces * rows * (3 * channels + tokens)
        ),
        name="input_partial",
    )(*[in_vmem(weight) for weight in weights], grad_proj.reshape(3 * channels, tokens))


def across(array, mask):
    return lax.ppermute(array, "tensor", [(i, i ^ mask) for i in range(16)])


def other_row(array):
    return lax.ppermute(array, "fsdp", [(0, 1), (1, 0)])


def in_square(array, turn):
    pairs = []
    for i in range(32):
        y, k = divmod(i, 16)
        target = turn(y, k // Z1)
        if target is not None:
            pairs.append((i, target[0] * 16 + target[1] * Z1 + k % Z1))
    return lax.ppermute(array, ("fsdp", "tensor"), pairs)


def from_turn(y, z1):
    return (y, 1 - z1) if y == z1 else (1 - y, z1)


def over_diagonal(y, z1):
    return None if y == z1 else (1 - y, 1 - z1)


def first_stage(array):
    return in_square(array, from_turn), in_square(array, over_diagonal)


def second_stage(own):
    return [own] + [across(own, mask) for mask in MINE[1:]]


def both_cores(same):
    return same + [across(piece, CORE) for piece in same]


def split_kernel(same_ref, got_ref, *out_refs):
    pieces = same_ref.shape[0]
    y = lax.axis_index("fsdp")
    leave = pl.ds(pl.multiple_of((1 - y) * TOK_DEV, BLOCK), TOK_DEV)
    stay = pl.ds(pl.multiple_of(y * TOK_DEV, BLOCK), TOK_DEV)
    for n in range(pieces):
        for at, out_ref in ((leave, out_refs[n]), (stay, out_refs[pieces + n])):
            total = same_ref[n, :, at].astype(F32) + got_ref[n, :, at].astype(F32)
            out_ref[...] = total.astype(BF16)


def split(same, got):
    pieces, rows, _ = same.shape
    out = jax.ShapeDtypeStruct((rows, TOK_DEV), BF16)
    halves = pl.pallas_call(
        split_kernel,
        in_specs=[VMEM_SPEC] * 2,
        out_specs=[VMEM_SPEC] * (2 * pieces),
        out_shape=[out] * (2 * pieces),
        compiler_params=params(8),
        cost_estimate=cost(0, 6 * same.size),
        name="split",
    )(same, got)
    return halves[:pieces], halves[pieces:]


def sum_kernel(*refs):
    total = refs[0][...].astype(F32)
    for ref in refs[1:-1]:
        total = total + ref[...].astype(F32)
    refs[-1][...] = total.astype(BF16)


def total_of(pieces):
    return pl.pallas_call(
        sum_kernel,
        in_specs=[VMEM_SPEC] * len(pieces),
        out_specs=VMEM_SPEC,
        out_shape=jax.ShapeDtypeStruct(pieces[0].shape, BF16),
        compiler_params=params(8),
        cost_estimate=cost(0, 8 * pieces[0].size),
        name="total",
    )(*pieces)


def sides_kernel(near_ref, far_ref, keep_ref, send_ref):
    home = at_home()

    @pl.when(home)
    def _():
        keep_ref[...] = near_ref[...]
        send_ref[...] = far_ref[...]

    @pl.when(jnp.logical_not(home))
    def _():
        keep_ref[...] = far_ref[...]
        send_ref[...] = near_ref[...]


def sides(near, far):
    out = jax.ShapeDtypeStruct(near.shape, BF16)
    return pl.pallas_call(
        sides_kernel,
        in_specs=[VMEM_SPEC] * 2,
        out_specs=[VMEM_SPEC] * 2,
        out_shape=[out] * 2,
        compiler_params=params(8),
        cost_estimate=cost(0, 8 * near.size),
        name="sides",
    )(near, far)


def last_kernel(keep_ref, got_ref, out_ref):
    total = keep_ref[...].astype(F32) + got_ref[...].astype(F32)
    out_ref[...] = total.T.astype(BF16)


def last_sum(keep, got):
    return pl.pallas_call(
        last_kernel,
        in_specs=[VMEM_SPEC] * 2,
        out_specs=VMEM_SPEC,
        out_shape=jax.ShapeDtypeStruct(keep.shape[::-1], BF16),
        compiler_params=params(8),
        cost_estimate=cost(0, 6 * keep.size),
        name="last_sum",
    )(keep, got)


def moved(pieces):
    return [pieces[0]] + [across(piece, mask) for piece, mask in zip(pieces[1:], MINE[1:])]


def scattered(same, others):
    leave, stay = split(same, across(others, CORE))
    leave, stay = moved(leave), moved(stay)
    far = other_row(total_of(leave))
    keep, send = sides(total_of(stay), far)
    return last_sum(keep, across(send, Z1))


def on_small_slice(tokens, values, scales, filters, out_weight, cotangent):
    rows = tokens.shape[1]
    token_stage = first_stage(tokens)
    weights, ready = prepared(values, scales)
    token_own = own_slice(in_hbm(tokens), *token_stage, ready)
    token_same = second_stage(token_own)
    past, later = toeplitz(filters, token_own)
    out_held = loaded(out_weight, past)
    cotangent = copied(cotangent, token_own)
    cot_own = own_slice(cotangent, *first_stage(cotangent))
    late = relayed([token_same[3]], out_held, cot_own)
    token_same = [*token_same[:3], *late]
    cot_same = second_stage(cot_own)
    pair, queries = proj_partial(both_cores(token_same), MINE + OTHERS, 2, weights)
    cot_same = list(relayed(cot_same, queries))
    pair, product, conv = conv_forward([pair, other_row(pair)], past)
    z_part = grad_z_partial(both_cores(cot_same), MINE + OTHERS, 2, out_held)
    grad_proj, grad = conv_backward(
        [z_part, other_row(z_part)], [queries, other_row(queries)], pair, conv, later
    )
    others = input_partial(OTHERS, 4, rows, weights, grad_proj)
    same = input_partial(MINE, 4, rows, weights, grad_proj)
    return scattered(same, others), taps_gradient(product, grad, filters.shape[0])


def on_any_slice(tokens, values, scales, filters, out_weight, cotangent):
    count = lax.axis_size("fsdp")
    rows = values.shape[1]
    piece = min(rows, 512)
    pieces = rows // piece

    def gather(array):
        whole = lax.all_gather(array, "tensor", axis=1, tiled=True)
        mine = lax.all_to_all(whole, "fsdp", 1, 0, tiled=True)
        return [mine[:, i * piece : (i + 1) * piece] for i in range(pieces)]

    def shares(array):
        every = lax.all_gather(array, "fsdp", axis=0)
        return [every[i] for i in range(count)]

    weights, _ = prepared(values, scales)
    out_held = loaded(out_weight)
    past, later = toeplitz(filters)
    pair, queries = proj_partial(gather(tokens), None, 1, weights)
    pair, product, conv = conv_forward(shares(pair), past)
    z_part = grad_z_partial(gather(cotangent), None, 1, out_held)
    grad_proj, grad = conv_backward(shares(z_part), shares(queries), pair, conv, later)
    partial = input_partial(None, pieces, piece, weights, grad_proj)
    partial = partial.reshape(rows, partial.shape[2]).astype(F32)
    partial = lax.all_to_all(partial, "fsdp", 1, 0, tiled=True)
    total = lax.psum_scatter(partial, "tensor", scatter_dimension=0, tiled=True)
    return total.T.astype(BF16), taps_gradient(product, grad, filters.shape[0])


def on_device(tokens, in_values, in_scales, filters, out_weight, cotangent):
    values = jnp.transpose(in_values, (1, 0, 2))
    scales = jnp.transpose(in_scales, (1, 0, 2))
    small = lax.axis_size("fsdp") == 2 and lax.axis_size("tensor") == 16
    inner = on_small_slice if small else on_any_slice
    return inner(tokens, values, scales, filters, out_weight, cotangent)


def solution(mesh):
    placed = (
        P("fsdp", "tensor"),
        P("fsdp", None, "tensor"),
        P("fsdp", None, "tensor"),
        P("tensor", None),
        P("tensor", "fsdp"),
        P("fsdp", "tensor"),
    )
    return jax.shard_map(
        on_device,
        mesh=mesh,
        in_specs=placed,
        out_specs=(P("fsdp", "tensor"), P("tensor", None)),
        check_vma=False,
    )
```

```python
import functools

import jax
import jax.numpy as jnp
from jax import lax
from jax.experimental import pallas as pl
from jax.experimental.pallas import tpu as pltpu
from jax.sharding import PartitionSpec as P

BLOCK = 128
TOK_DEV = 128
BF16 = jnp.bfloat16
F32 = jnp.float32
MIB = 1 << 20


def cost(flops, read):
    return pl.CostEstimate(flops=int(flops) >> 12, bytes_accessed=int(read) >> 12, transcendentals=0)


def params(mib):
    return pltpu.CompilerParams(vmem_limit_bytes=mib * MIB)


def in_hbm(array):
    return pltpu.with_memory_space_constraint(array, pltpu.HBM)


VMEM_SPEC = pl.BlockSpec(memory_space=pltpu.VMEM)
SMEM_SPEC = pl.BlockSpec(memory_space=pltpu.SMEM)
LATER_SPEC = pl.BlockSpec(memory_space=pl.ANY)


def copy_kernel(in_ref, *refs):
    refs[-1][...] = in_ref[...]


def copied(array, *earlier):
    return pl.pallas_call(
        copy_kernel,
        in_specs=[VMEM_SPEC] + [LATER_SPEC] * len(earlier),
        out_specs=VMEM_SPEC,
        out_shape=jax.ShapeDtypeStruct(array.shape, array.dtype),
        compiler_params=params(8),
        cost_estimate=cost(0, 4 * array.size),
        name="copied",
    )(array, *earlier)


def at_home():
    return lax.axis_index("tensor") // Z1 == lax.axis_index("fsdp")


def own_kernel(array_ref, turned_ref, crossed_ref, *refs):
    out_ref, sem = refs[-2:]
    run = array_ref.shape[0]
    home = at_home()

    @pl.when(home)
    def _():
        copy = pltpu.make_async_copy(array_ref, out_ref.at[pl.ds(0, run), :], sem)
        copy.start()
        out_ref[run:] = turned_ref[...]
        copy.wait()

    @pl.when(jnp.logical_not(home))
    def _():
        out_ref[:run] = turned_ref[...]
        out_ref[run:] = crossed_ref[...]


def own_slice(array, turned, crossed, *earlier):
    return pl.pallas_call(
        own_kernel,
        in_specs=[LATER_SPEC] + [VMEM_SPEC] * 2 + [LATER_SPEC] * len(earlier),
        out_specs=VMEM_SPEC,
        out_shape=jax.ShapeDtypeStruct((2 * array.shape[0], array.shape[1]), array.dtype),
        scratch_shapes=[pltpu.SemaphoreType.DMA],
        compiler_params=params(8),
        cost_estimate=cost(0, 10 * array.size),
        name="own_slice",
    )(array, turned, crossed, *earlier)


def relay_kernel(*refs):
    del refs


def relayed(arrays, *earlier):
    count = len(arrays)
    return pl.pallas_call(
        relay_kernel,
        in_specs=[LATER_SPEC] * (count + len(earlier)),
        out_specs=[LATER_SPEC] * count,
        out_shape=[jax.ShapeDtypeStruct(array.shape, array.dtype) for array in arrays],
        input_output_aliases={n: n for n in range(count)},
        compiler_params=params(8),
        cost_estimate=cost(0, 0),
        name="relayed",
    )(*arrays, *earlier)


def in_vmem(array):
    return pltpu.with_memory_space_constraint(array, pltpu.VMEM)


AHEAD = 3


def prepare_kernel(v_ref, s_ref, *refs):
    weights, (done_ref, raw, held, ins, in_sems, s_sem) = refs[-9:-6], refs[-6:]
    piece = ins.shape[2]
    pieces = v_ref.shape[1] // piece

    def rows(i):
        return pl.ds(pl.multiple_of(i * piece, BLOCK), piece)

    def fetch(i, j):
        slot = lax.rem(i, AHEAD)
        return pltpu.make_async_copy(
            v_ref.at[j, rows(i), :], ins.at[slot, j], in_sems.at[slot, j]
        )

    scales = pltpu.make_async_copy(s_ref, raw, s_sem)
    scales.start()
    for i in range(min(AHEAD, pieces)):
        for j in range(3):
            fetch(i, j).start()
    scales.wait()
    held[...] = raw[...].astype(F32)
    done_ref[...] = jnp.zeros(done_ref.shape, F32)

    def one(i, carry):
        for j in range(3):
            fetch(i, j).wait()
            for b in range(piece // BLOCK):
                scale = held[j, pl.ds(i * (piece // BLOCK) + b, 1), :]
                at = pl.ds(pl.multiple_of(i * piece + b * BLOCK, BLOCK), BLOCK)
                values = ins[lax.rem(i, AHEAD), j, b * BLOCK : (b + 1) * BLOCK, :]
                weights[j][at, :] = (values.astype(F32) * scale).astype(BF16)

            @pl.when(i + AHEAD < pieces)
            def _(j=j):
                fetch(i + AHEAD, j).start()

        return carry

    lax.fori_loop(0, pieces, one, 0)


def prepared(values, scales, *earlier):
    _, rows, channels = values.shape
    piece = min(rows, 512)
    *weights, ready = pl.pallas_call(
        prepare_kernel,
        in_specs=[LATER_SPEC] * (2 + len(earlier)),
        out_specs=[VMEM_SPEC] * 4,
        out_shape=[pltpu.VMEM((rows, channels), BF16)] * 3
        + [jax.ShapeDtypeStruct((8, 128), F32)],
        scratch_shapes=[
            pltpu.VMEM(scales.shape, BF16),
            pltpu.VMEM(scales.shape, F32),
            pltpu.VMEM((AHEAD, 3, piece, channels), BF16),
            pltpu.SemaphoreType.DMA((AHEAD, 3)),
            pltpu.SemaphoreType.DMA,
        ],
        compiler_params=params(16),
        cost_estimate=cost(values.size * 4, 4 * values.size),
        name="prepare",
    )(in_hbm(values), in_hbm(scales), *earlier)
    return weights, ready


Z1, Z0, X, CORE = 8, 4, 2, 1
MINE = (0, Z0, X, X + Z0)
OTHERS = tuple(mask + CORE for mask in MINE)


def slices_of(masks):
    low = lax.rem(lax.axis_index("tensor"), Z1)
    return [low ^ mask for mask in masks]


def run_starts(runs, run):
    if runs == 1:
        return [0]
    y = lax.axis_index("fsdp")
    return [pl.multiple_of(y * run, BLOCK), pl.multiple_of((1 - y) * run, BLOCK)]


def piece_rows(masks, n, rows):
    if masks is None:
        return pl.ds(n * rows, rows)
    return pl.ds(pl.multiple_of(slices_of(masks)[n] * rows, BLOCK), rows)


def load_kernel(in_ref, *refs):
    out_ref, sem = refs[-2:]
    copy = pltpu.make_async_copy(in_ref, out_ref, sem)
    copy.start()
    copy.wait()


def loaded(array, *earlier):
    return pl.pallas_call(
        load_kernel,
        in_specs=[LATER_SPEC] * (1 + len(earlier)),
        out_specs=VMEM_SPEC,
        out_shape=pltpu.VMEM(array.shape, array.dtype),
        scratch_shapes=[pltpu.SemaphoreType.DMA],
        compiler_params=params(8),
        cost_estimate=cost(0, 4 * array.size),
        name="loaded",
    )(in_hbm(array), *earlier)


def assembled(masks, refs, held):
    for n, ref in enumerate(refs):
        held[:, piece_rows(masks, n, ref.shape[1])] = ref[...]


def proj_part(runs, held_ref, w_ref, out_ref):
    run = held_ref.shape[0] // runs
    total = jnp.dot(held_ref[...], w_ref[...], preferred_element_type=F32)
    for h, start in enumerate(run_starts(runs, run)):
        out_ref[:, pl.ds(start, run)] = total[h * run : (h + 1) * run].T.astype(BF16)


def pair_kernel(masks, runs, *refs):
    xs, (key_ref, value_ref, out_ref, held_ref) = refs[:-4], refs[-4:]
    assembled(masks, xs, held_ref)
    proj_part(runs, held_ref, key_ref, out_ref.at[0])
    proj_part(runs, held_ref, value_ref, out_ref.at[1])


def query_kernel(runs, held_ref, w_ref, out_ref):
    proj_part(runs, held_ref, w_ref, out_ref)


def proj_partial(xs, masks, runs, weights):
    tokens = xs[0].shape[0]
    depth, channels = weights[0].shape
    flops = 2 * tokens * depth * channels
    weights = [in_vmem(weight) for weight in weights]
    pair, held = pl.pallas_call(
        functools.partial(pair_kernel, masks, runs),
        in_specs=[VMEM_SPEC] * (len(xs) + 2),
        out_specs=[VMEM_SPEC] * 2,
        out_shape=[
            jax.ShapeDtypeStruct((2, channels, tokens), BF16),
            pltpu.VMEM((tokens, depth), BF16),
        ],
        compiler_params=params(16),
        cost_estimate=cost(2 * flops, 4 * depth * channels),
        name="proj_pair",
    )(*xs, *weights[1:])
    queries = pl.pallas_call(
        functools.partial(query_kernel, runs),
        in_specs=[VMEM_SPEC] * 2,
        out_specs=VMEM_SPEC,
        out_shape=jax.ShapeDtypeStruct((channels, tokens), BF16),
        compiler_params=params(16),
        cost_estimate=cost(flops, 2 * depth * channels),
        name="proj_queries",
    )(held, weights[0])
    return pair, queries


def grad_z_kernel(masks, runs, *refs):
    xs, (w_ref, out_ref, held) = refs[:-3], refs[-3:]
    total = None
    for n, x_ref in enumerate(xs):
        term = lax.dot_general(
            w_ref[:, piece_rows(masks, n, x_ref.shape[1])],
            x_ref[...],
            (((1,), (1,)), ((), ())),
            preferred_element_type=F32,
        )
        total = term if total is None else total + term
    run = total.shape[1] // runs
    for h, start in enumerate(run_starts(runs, run)):
        out_ref[:, pl.ds(start, run)] = total[:, h * run : (h + 1) * run].astype(BF16)


def grad_z_partial(xs, masks, runs, out_weight):
    tokens = xs[0].shape[0]
    channels, depth = out_weight.shape
    return pl.pallas_call(
        functools.partial(grad_z_kernel, masks, runs),
        in_specs=[VMEM_SPEC] * (len(xs) + 1),
        out_specs=VMEM_SPEC,
        out_shape=jax.ShapeDtypeStruct((channels, tokens), BF16),
        scratch_shapes=[pltpu.VMEM((tokens, depth), BF16)],
        compiler_params=params(16),
        cost_estimate=cost(2 * tokens * depth * channels, 2 * depth * channels),
        name="grad_z_partial",
    )(*xs, in_vmem(out_weight))


def iotas():
    shape = (BLOCK, BLOCK)
    return lax.broadcasted_iota(jnp.int32, shape, 0), lax.broadcasted_iota(jnp.int32, shape, 1)


def sheared(array):
    return pltpu.roll(array, 0, 1, stride=1, stride_axis=0)


def toeplitz_kernel(taps_ref, *refs):
    past_ref, next_ref = refs[-2:]
    row, lane = iotas()
    for g in range(taps_ref.shape[0]):
        ahead = sheared(jnp.broadcast_to(taps_ref[g : g + 1, :], (BLOCK, BLOCK)))
        behind = ahead.T
        past_ref[g, :BLOCK] = jnp.where(lane < row, ahead, 0.0).astype(BF16)
        past_ref[g, BLOCK:] = jnp.where(lane >= row, ahead, 0.0).astype(BF16)
        next_ref[g, :BLOCK] = jnp.where(lane <= row, behind, 0.0).astype(BF16)
        next_ref[g, BLOCK:] = jnp.where(lane > row, behind, 0.0).astype(BF16)


def toeplitz(filters, *earlier):
    groups, taps = filters.shape
    step = min(8, groups)
    shape = pltpu.VMEM((groups, 2 * BLOCK, taps), BF16)
    return pl.pallas_call(
        toeplitz_kernel,
        grid=(groups // step,),
        in_specs=[pl.BlockSpec((step, taps), lambda i: (i, 0))]
        + [LATER_SPEC] * len(earlier),
        out_specs=[pl.BlockSpec((step, 2 * BLOCK, taps), lambda i: (i, 0, 0))] * 2,
        out_shape=[shape, shape],
        compiler_params=params(16),
        cost_estimate=cost(groups * taps * 2000, groups * taps * 1024),
        name="toeplitz",
    )(filters, *earlier)


def block_of(array, i):
    blocks = array.shape[1] // BLOCK
    if 0 <= i < blocks:
        return array[:, i * BLOCK : (i + 1) * BLOCK]
    return jnp.zeros((array.shape[0], BLOCK), array.dtype)


def paired(array, by):
    blocks = array.shape[1] // BLOCK
    low, high = min(by, 0), max(by, 0)
    return jnp.concatenate(
        [
            jnp.concatenate([block_of(array, i + low), block_of(array, i + high)], 1)
            for i in range(blocks)
        ],
        0,
    )


def unstacked(array, blocks):
    rows = array.shape[0] // blocks
    return jnp.concatenate([array[i * rows : (i + 1) * rows] for i in range(blocks)], 1)


def summed(refs, part=...):
    total = refs[0][part].astype(F32)
    for ref in refs[1:]:
        total = total + ref[part].astype(F32)
    return total.astype(BF16)


def conv_kernel(parts, groups, *refs):
    shares, (past_ref, pair_ref, prod_ref, conv_ref) = refs[:parts], refs[parts:]
    key, value = summed(shares, 0), summed(shares, 1)
    pair_ref[0] = key
    pair_ref[1] = value
    product = (key.astype(F32) * value.astype(F32)).astype(BF16)
    prod_ref[...] = product
    channels, tokens = product.shape
    per = channels // groups
    for g in range(groups):
        rows = slice(g * per, (g + 1) * per)
        result = jnp.dot(paired(product[rows], -1), past_ref[g], preferred_element_type=F32)
        conv_ref[rows] = unstacked(result, tokens // BLOCK)


def conv_forward(shares, past):
    _, channels, tokens = shares[0].shape
    groups = past.shape[0]
    steps = max(1, groups // 32)
    chunk = channels // steps
    parts = len(shares)
    two = pl.BlockSpec((2, chunk, tokens), lambda i: (0, i, 0))
    one = pl.BlockSpec((chunk, tokens), lambda i: (i, 0))
    return pl.pallas_call(
        functools.partial(conv_kernel, parts, groups // steps),
        grid=(steps,),
        in_specs=[two] * parts
        + [pl.BlockSpec((groups // steps,) + past.shape[1:], lambda i: (i, 0, 0))],
        out_specs=[two, one, one],
        out_shape=[
            jax.ShapeDtypeStruct((2, channels, tokens), BF16),
            jax.ShapeDtypeStruct((channels, tokens), BF16),
            jax.ShapeDtypeStruct((channels, tokens), F32),
        ],
        compiler_params=params(16),
        cost_estimate=cost(4 * channels * tokens * BLOCK * 8, channels * tokens * 24),
        name="conv_forward",
    )(*shares, past)


def conv_back_kernel(parts, groups, *refs):
    shares, queries = refs[:parts], refs[parts : 2 * parts]
    pair_ref, conv_ref, next_ref, out_ref, grad_ref = refs[2 * parts :]
    grad_z = shares[0][...].astype(F32)
    for ref in shares[1:]:
        grad_z = grad_z + ref[...].astype(F32)
    out_ref[0] = (grad_z * conv_ref[...]).astype(BF16)
    grad = (grad_z * summed(queries).astype(F32)).astype(BF16)
    grad_ref[...] = grad
    channels, tokens = grad.shape
    per = channels // groups
    for g in range(groups):
        rows = slice(g * per, (g + 1) * per)
        result = jnp.dot(paired(grad[rows], 1), next_ref[g], preferred_element_type=F32)
        result = unstacked(result, tokens // BLOCK)
        out_ref[1, rows] = (result * pair_ref[1, rows].astype(F32)).astype(BF16)
        out_ref[2, rows] = (result * pair_ref[0, rows].astype(F32)).astype(BF16)


def conv_backward(shares, queries, pair, conv, after):
    channels, tokens = conv.shape
    groups = after.shape[0]
    steps = max(1, groups // 32)
    chunk = channels // steps
    parts = len(shares)
    three = pl.BlockSpec((3, chunk, tokens), lambda i: (0, i, 0))
    one = pl.BlockSpec((chunk, tokens), lambda i: (i, 0))
    return pl.pallas_call(
        functools.partial(conv_back_kernel, parts, groups // steps),
        grid=(steps,),
        in_specs=[one] * (2 * parts)
        + [
            pl.BlockSpec((2, chunk, tokens), lambda i: (0, i, 0)),
            one,
            pl.BlockSpec((groups // steps,) + after.shape[1:], lambda i: (i, 0, 0)),
        ],
        out_specs=[three, one],
        out_shape=[
            jax.ShapeDtypeStruct((3, channels, tokens), BF16),
            jax.ShapeDtypeStruct((channels, tokens), BF16),
        ],
        compiler_params=params(16),
        cost_estimate=cost(4 * channels * tokens * BLOCK * 8, channels * tokens * 24),
        name="conv_backward",
    )(*shares, *queries, pair, conv, after)


def taps_kernel(groups, prod_ref, grad_ref, out_ref):
    row, lane = iotas()
    flip = (row + lane == BLOCK - 1).astype(F32).astype(BF16)
    channels, tokens = prod_ref.shape
    per = channels // groups
    blocks = tokens // BLOCK

    def cut(ref, i):
        return ref[:, i * BLOCK : (i + 1) * BLOCK]

    turned = [
        jnp.dot(cut(prod_ref, i), flip, preferred_element_type=F32).astype(BF16)
        for i in range(blocks)
    ]
    grad = [cut(grad_ref, i) for i in range(blocks)]

    def correlated(earlier, later, rows):
        return lax.dot_general(
            jnp.concatenate([block[rows] for block in earlier], 0),
            jnp.concatenate([block[rows] for block in later], 0),
            (((0,), (0,)), ((), ())),
            preferred_element_type=F32,
        )

    for g in range(groups):
        rows = slice(g * per, (g + 1) * per)
        within = correlated(turned, grad, rows)
        before = correlated(turned[:-1], grad[1:], rows)
        folded = jnp.where(row + lane >= BLOCK - 1, within, before)
        out_ref[g : g + 1, :] = jnp.sum(sheared(folded), axis=0, keepdims=True)
    out_ref[...] = pltpu.roll(out_ref[...], 1, 1) / TOK_DEV


def taps_gradient(product, grad, groups):
    channels, tokens = product.shape
    steps = max(1, groups // 8)
    chunk = channels // steps
    one = pl.BlockSpec((chunk, tokens), lambda i: (i, 0))
    return pl.pallas_call(
        functools.partial(taps_kernel, groups // steps),
        grid=(steps,),
        in_specs=[one, one],
        out_specs=pl.BlockSpec((groups // steps, BLOCK), lambda i: (i, 0)),
        out_shape=jax.ShapeDtypeStruct((groups, BLOCK), F32),
        compiler_params=params(16),
        cost_estimate=cost(4 * channels * tokens * BLOCK * 8, channels * tokens * 24),
        name="taps_gradient",
    )(product, grad)


def input_kernel(masks, *refs):
    w_refs, (g_ref, out_ref) = refs[:3], refs[3:]
    pieces, rows, _ = out_ref.shape
    for i in range(pieces):
        at = piece_rows(masks, i, rows)
        w = jnp.concatenate([ref[at, :] for ref in w_refs], 1)
        out_ref[i] = jnp.dot(w, g_ref[...], preferred_element_type=F32).astype(BF16)


def input_partial(masks, pieces, rows, weights, grad_proj):
    _, channels, tokens = grad_proj.shape
    return pl.pallas_call(
        functools.partial(input_kernel, masks),
        in_specs=[VMEM_SPEC] * 4,
        out_specs=VMEM_SPEC,
        out_shape=jax.ShapeDtypeStruct((pieces, rows, tokens), BF16),
        compiler_params=params(16),
        cost_estimate=cost(
            2 * tokens * pieces * rows * 3 * channels, 2 * pieces * rows * (3 * channels + tokens)
        ),
        name="input_partial",
    )(*[in_vmem(weight) for weight in weights], grad_proj.reshape(3 * channels, tokens))


def across(array, mask):
    return lax.ppermute(array, "tensor", [(i, i ^ mask) for i in range(16)])


def other_row(array):
    return lax.ppermute(array, "fsdp", [(0, 1), (1, 0)])


def in_square(array, turn):
    pairs = []
    for i in range(32):
        y, k = divmod(i, 16)
        target = turn(y, k // Z1)
        if target is not None:
            pairs.append((i, target[0] * 16 + target[1] * Z1 + k % Z1))
    return lax.ppermute(array, ("fsdp", "tensor"), pairs)


def from_turn(y, z1):
    return (y, 1 - z1) if y == z1 else (1 - y, z1)


def over_diagonal(y, z1):
    return None if y == z1 else (1 - y, 1 - z1)


def first_stage(array):
    return in_square(array, from_turn), in_square(array, over_diagonal)


def second_stage(own, order=(1, 2, 3)):
    got = {n: across(own, MINE[n]) for n in order}
    return [own] + [got[n] for n in (1, 2, 3)]


def both_cores(same):
    return same + [across(piece, CORE) for piece in same]


def split_kernel(parts, same_ref, *refs):
    got_refs, out_refs = refs[:parts], refs[parts:]
    pieces = same_ref.shape[0]
    got = [ref.at[n] for ref in got_refs for n in range(ref.shape[0])]
    y = lax.axis_index("fsdp")
    leave = pl.ds(pl.multiple_of((1 - y) * TOK_DEV, BLOCK), TOK_DEV)
    stay = pl.ds(pl.multiple_of(y * TOK_DEV, BLOCK), TOK_DEV)
    for n in range(pieces):
        for at, out_ref in ((leave, out_refs[n]), (stay, out_refs[pieces + n])):
            total = same_ref[n, :, at].astype(F32) + got[n][:, at].astype(F32)
            out_ref[...] = total.astype(BF16)


def split(same, *got):
    pieces, rows, _ = same.shape
    out = jax.ShapeDtypeStruct((rows, TOK_DEV), BF16)
    halves = pl.pallas_call(
        functools.partial(split_kernel, len(got)),
        in_specs=[VMEM_SPEC] * (1 + len(got)),
        out_specs=[VMEM_SPEC] * (2 * pieces),
        out_shape=[out] * (2 * pieces),
        compiler_params=params(8),
        cost_estimate=cost(0, 6 * same.size),
        name="split",
    )(same, *got)
    return halves[:pieces], halves[pieces:]


def sum_kernel(*refs):
    total = refs[0][...].astype(F32)
    for ref in refs[1:-1]:
        total = total + ref[...].astype(F32)
    refs[-1][...] = total.astype(BF16)


def total_of(pieces):
    return pl.pallas_call(
        sum_kernel,
        in_specs=[VMEM_SPEC] * len(pieces),
        out_specs=VMEM_SPEC,
        out_shape=jax.ShapeDtypeStruct(pieces[0].shape, BF16),
        compiler_params=params(8),
        cost_estimate=cost(0, 8 * pieces[0].size),
        name="total",
    )(*pieces)


def sides_kernel(*refs):
    far_ref, keep_ref, send_ref = refs[-3:]
    home = at_home()
    near = refs[0][...].astype(F32)
    for ref in refs[1:-3]:
        near = near + ref[...].astype(F32)
    near = near.astype(BF16)

    @pl.when(home)
    def _():
        keep_ref[...] = near
        send_ref[...] = far_ref[...]

    @pl.when(jnp.logical_not(home))
    def _():
        keep_ref[...] = far_ref[...]
        send_ref[...] = near


def sides(pieces, far):
    out = jax.ShapeDtypeStruct(far.shape, BF16)
    return pl.pallas_call(
        sides_kernel,
        in_specs=[VMEM_SPEC] * (len(pieces) + 1),
        out_specs=[VMEM_SPEC] * 2,
        out_shape=[out] * 2,
        compiler_params=params(8),
        cost_estimate=cost(0, 8 * far.size),
        name="sides",
    )(*pieces, far)


def last_kernel(keep_ref, got_ref, out_ref):
    total = keep_ref[...].astype(F32) + got_ref[...].astype(F32)
    out_ref[...] = total.T.astype(BF16)


def last_sum(keep, got):
    return pl.pallas_call(
        last_kernel,
        in_specs=[VMEM_SPEC] * 2,
        out_specs=VMEM_SPEC,
        out_shape=jax.ShapeDtypeStruct(keep.shape[::-1], BF16),
        compiler_params=params(8),
        cost_estimate=cost(0, 6 * keep.size),
        name="last_sum",
    )(keep, got)


def moved(pieces):
    return [pieces[0]] + [across(piece, mask) for piece, mask in zip(pieces[1:], MINE[1:])]


def scattered(same, *others):
    leave, stay = split(same, *[across(part, CORE) for part in others])
    leave, stay = moved(leave), moved(stay)
    far = other_row(total_of(leave))
    keep, send = sides(stay, far)
    return last_sum(keep, across(send, Z1))


def on_small_slice(tokens, values, scales, filters, out_weight, cotangent):
    rows = tokens.shape[1]
    token_stage = first_stage(tokens)
    weights, ready = prepared(values, scales)
    token_own = own_slice(in_hbm(tokens), *token_stage, ready)
    token_same = second_stage(token_own, (2, 1, 3))
    past, later = toeplitz(filters, token_own)
    out_held = loaded(out_weight, past)
    cotangent = copied(cotangent, token_own)
    cot_own = own_slice(cotangent, *first_stage(cotangent))
    late = relayed([token_same[3]], out_held, cot_own)
    token_same = [*token_same[:3], *late]
    xs = both_cores(token_same)
    cot_same = second_stage(cot_own)
    pair, queries = proj_partial(xs, MINE + OTHERS, 2, weights)
    cot_same = list(relayed(cot_same, queries))
    pair, product, conv = conv_forward([pair, other_row(pair)], past)
    z_part = grad_z_partial(both_cores(cot_same), MINE + OTHERS, 2, out_held)
    grad_proj, grad = conv_backward(
        [z_part, other_row(z_part)], [queries, other_row(queries)], pair, conv, later
    )
    others = [
        input_partial(masks, len(masks), rows, weights, grad_proj)
        for masks in (OTHERS[:3], OTHERS[3:])
    ]
    same = input_partial(MINE, 4, rows, weights, grad_proj)
    return scattered(same, *others), taps_gradient(product, grad, filters.shape[0])


def on_any_slice(tokens, values, scales, filters, out_weight, cotangent):
    count = lax.axis_size("fsdp")
    rows = values.shape[1]
    piece = min(rows, 512)
    pieces = rows // piece

    def gather(array):
        whole = lax.all_gather(array, "tensor", axis=1, tiled=True)
        mine = lax.all_to_all(whole, "fsdp", 1, 0, tiled=True)
        return [mine[:, i * piece : (i + 1) * piece] for i in range(pieces)]

    def shares(array):
        every = lax.all_gather(array, "fsdp", axis=0)
        return [every[i] for i in range(count)]

    weights, _ = prepared(values, scales)
    out_held = loaded(out_weight)
    past, later = toeplitz(filters)
    pair, queries = proj_partial(gather(tokens), None, 1, weights)
    pair, product, conv = conv_forward(shares(pair), past)
    z_part = grad_z_partial(gather(cotangent), None, 1, out_held)
    grad_proj, grad = conv_backward(shares(z_part), shares(queries), pair, conv, later)
    partial = input_partial(None, pieces, piece, weights, grad_proj)
    partial = partial.reshape(rows, partial.shape[2]).astype(F32)
    partial = lax.all_to_all(partial, "fsdp", 1, 0, tiled=True)
    total = lax.psum_scatter(partial, "tensor", scatter_dimension=0, tiled=True)
    return total.T.astype(BF16), taps_gradient(product, grad, filters.shape[0])


def on_device(tokens, in_values, in_scales, filters, out_weight, cotangent):
    values = jnp.transpose(in_values, (1, 0, 2))
    scales = jnp.transpose(in_scales, (1, 0, 2))
    small = lax.axis_size("fsdp") == 2 and lax.axis_size("tensor") == 16
    inner = on_small_slice if small else on_any_slice
    return inner(tokens, values, scales, filters, out_weight, cotangent)


def solution(mesh):
    placed = (
        P("fsdp", "tensor"),
        P("fsdp", None, "tensor"),
        P("fsdp", None, "tensor"),
        P("tensor", None),
        P("tensor", "fsdp"),
        P("fsdp", "tensor"),
    )
    return jax.shard_map(
        on_device,
        mesh=mesh,
        in_specs=placed,
        out_specs=(P("fsdp", "tensor"), P("tensor", None)),
        check_vma=False,
    )
```

```python
import functools

import jax
import jax.numpy as jnp
from jax import lax
from jax.experimental import pallas as pl
from jax.experimental.pallas import tpu as pltpu
from jax.sharding import PartitionSpec as P

BLOCK = 128
TOK_DEV = 128
BF16 = jnp.bfloat16
F32 = jnp.float32
MIB = 1 << 20


def cost(flops, read):
    return pl.CostEstimate(flops=int(flops) >> 12, bytes_accessed=int(read) >> 12, transcendentals=0)


def params(mib):
    return pltpu.CompilerParams(vmem_limit_bytes=mib * MIB)


def in_hbm(array):
    return pltpu.with_memory_space_constraint(array, pltpu.HBM)


VMEM_SPEC = pl.BlockSpec(memory_space=pltpu.VMEM)
SMEM_SPEC = pl.BlockSpec(memory_space=pltpu.SMEM)
LATER_SPEC = pl.BlockSpec(memory_space=pl.ANY)


def copy_kernel(in_ref, *refs):
    refs[-1][...] = in_ref[...]


def copied(array, *earlier):
    return pl.pallas_call(
        copy_kernel,
        in_specs=[VMEM_SPEC] + [LATER_SPEC] * len(earlier),
        out_specs=VMEM_SPEC,
        out_shape=jax.ShapeDtypeStruct(array.shape, array.dtype),
        compiler_params=params(8),
        cost_estimate=cost(0, 4 * array.size),
        name="copied",
    )(array, *earlier)


def at_home():
    return lax.axis_index("tensor") // Z1 == lax.axis_index("fsdp")


def own_kernel(array_ref, turned_ref, crossed_ref, *refs):
    out_ref, sem = refs[-2:]
    run = array_ref.shape[0]
    home = at_home()

    @pl.when(home)
    def _():
        copy = pltpu.make_async_copy(array_ref, out_ref.at[pl.ds(0, run), :], sem)
        copy.start()
        out_ref[run:] = turned_ref[...]
        copy.wait()

    @pl.when(jnp.logical_not(home))
    def _():
        out_ref[:run] = turned_ref[...]
        out_ref[run:] = crossed_ref[...]


def own_slice(array, turned, crossed, *earlier):
    return pl.pallas_call(
        own_kernel,
        in_specs=[LATER_SPEC] + [VMEM_SPEC] * 2 + [LATER_SPEC] * len(earlier),
        out_specs=VMEM_SPEC,
        out_shape=jax.ShapeDtypeStruct((2 * array.shape[0], array.shape[1]), array.dtype),
        scratch_shapes=[pltpu.SemaphoreType.DMA],
        compiler_params=params(8),
        cost_estimate=cost(0, 10 * array.size),
        name="own_slice",
    )(array, turned, crossed, *earlier)


def relay_kernel(*refs):
    del refs


def relayed(arrays, *earlier):
    count = len(arrays)
    return pl.pallas_call(
        relay_kernel,
        in_specs=[LATER_SPEC] * (count + len(earlier)),
        out_specs=[LATER_SPEC] * count,
        out_shape=[jax.ShapeDtypeStruct(array.shape, array.dtype) for array in arrays],
        input_output_aliases={n: n for n in range(count)},
        compiler_params=params(8),
        cost_estimate=cost(0, 0),
        name="relayed",
    )(*arrays, *earlier)


def in_vmem(array):
    return pltpu.with_memory_space_constraint(array, pltpu.VMEM)


AHEAD = 3


def prepare_kernel(v_ref, s_ref, *refs):
    weights, (done_ref, raw, held, ins, in_sems, s_sem) = refs[-9:-6], refs[-6:]
    piece = ins.shape[2]
    pieces = v_ref.shape[1] // piece

    def rows(i):
        return pl.ds(pl.multiple_of(i * piece, BLOCK), piece)

    def fetch(i, j):
        slot = lax.rem(i, AHEAD)
        return pltpu.make_async_copy(
            v_ref.at[j, rows(i), :], ins.at[slot, j], in_sems.at[slot, j]
        )

    scales = pltpu.make_async_copy(s_ref, raw, s_sem)
    scales.start()
    for i in range(min(AHEAD, pieces)):
        for j in range(3):
            fetch(i, j).start()
    scales.wait()
    held[...] = raw[...].astype(F32)
    done_ref[...] = jnp.zeros(done_ref.shape, F32)

    def one(i, carry):
        for j in range(3):
            fetch(i, j).wait()
            for b in range(piece // BLOCK):
                scale = held[j, pl.ds(i * (piece // BLOCK) + b, 1), :]
                at = pl.ds(pl.multiple_of(i * piece + b * BLOCK, BLOCK), BLOCK)
                values = ins[lax.rem(i, AHEAD), j, b * BLOCK : (b + 1) * BLOCK, :]
                weights[j][at, :] = (values.astype(F32) * scale).astype(BF16)

            @pl.when(i + AHEAD < pieces)
            def _(j=j):
                fetch(i + AHEAD, j).start()

        return carry

    lax.fori_loop(0, pieces, one, 0)


def prepared(values, scales, *earlier):
    _, rows, channels = values.shape
    piece = min(rows, 512)
    *weights, ready = pl.pallas_call(
        prepare_kernel,
        in_specs=[LATER_SPEC] * (2 + len(earlier)),
        out_specs=[VMEM_SPEC] * 4,
        out_shape=[pltpu.VMEM((rows, channels), BF16)] * 3
        + [jax.ShapeDtypeStruct((8, 128), F32)],
        scratch_shapes=[
            pltpu.VMEM(scales.shape, BF16),
            pltpu.VMEM(scales.shape, F32),
            pltpu.VMEM((AHEAD, 3, piece, channels), BF16),
            pltpu.SemaphoreType.DMA((AHEAD, 3)),
            pltpu.SemaphoreType.DMA,
        ],
        compiler_params=params(16),
        cost_estimate=cost(values.size * 4, 4 * values.size),
        name="prepare",
    )(in_hbm(values), in_hbm(scales), *earlier)
    return weights, ready


Z1, Z0, X, CORE = 8, 4, 2, 1
MINE = (0, Z0, X, X + Z0)
OTHERS = tuple(mask + CORE for mask in MINE)


def slices_of(masks):
    low = lax.rem(lax.axis_index("tensor"), Z1)
    return [low ^ mask for mask in masks]


def run_starts(runs, run):
    if runs == 1:
        return [0]
    y = lax.axis_index("fsdp")
    return [pl.multiple_of(y * run, BLOCK), pl.multiple_of((1 - y) * run, BLOCK)]


def piece_rows(masks, n, rows):
    if masks is None:
        return pl.ds(n * rows, rows)
    return pl.ds(pl.multiple_of(slices_of(masks)[n] * rows, BLOCK), rows)


def load_kernel(in_ref, *refs):
    out_ref, sem = refs[-2:]
    copy = pltpu.make_async_copy(in_ref, out_ref, sem)
    copy.start()
    copy.wait()


def loaded(array, *earlier):
    return pl.pallas_call(
        load_kernel,
        in_specs=[LATER_SPEC] * (1 + len(earlier)),
        out_specs=VMEM_SPEC,
        out_shape=pltpu.VMEM(array.shape, array.dtype),
        scratch_shapes=[pltpu.SemaphoreType.DMA],
        compiler_params=params(8),
        cost_estimate=cost(0, 4 * array.size),
        name="loaded",
    )(in_hbm(array), *earlier)


def assembled(masks, refs, held):
    for n, ref in enumerate(refs):
        held[:, piece_rows(masks, n, ref.shape[1])] = ref[...]


def proj_part(runs, held_ref, w_ref, out_ref):
    run = held_ref.shape[0] // runs
    total = jnp.dot(held_ref[...], w_ref[...], preferred_element_type=F32)
    for h, start in enumerate(run_starts(runs, run)):
        out_ref[:, pl.ds(start, run)] = total[h * run : (h + 1) * run].astype(BF16).T


def pair_kernel(masks, runs, *refs):
    xs, (key_ref, value_ref, out_ref, held_ref) = refs[:-4], refs[-4:]
    assembled(masks, xs, held_ref)
    proj_part(runs, held_ref, key_ref, out_ref.at[0])
    proj_part(runs, held_ref, value_ref, out_ref.at[1])


def query_kernel(runs, held_ref, w_ref, out_ref):
    proj_part(runs, held_ref, w_ref, out_ref)


def proj_partial(xs, masks, runs, weights):
    tokens = xs[0].shape[0]
    depth, channels = weights[0].shape
    flops = 2 * tokens * depth * channels
    weights = [in_vmem(weight) for weight in weights]
    pair, held = pl.pallas_call(
        functools.partial(pair_kernel, masks, runs),
        in_specs=[VMEM_SPEC] * (len(xs) + 2),
        out_specs=[VMEM_SPEC] * 2,
        out_shape=[
            jax.ShapeDtypeStruct((2, channels, tokens), BF16),
            pltpu.VMEM((tokens, depth), BF16),
        ],
        compiler_params=params(16),
        cost_estimate=cost(2 * flops, 4 * depth * channels),
        name="proj_pair",
    )(*xs, *weights[1:])
    queries = pl.pallas_call(
        functools.partial(query_kernel, runs),
        in_specs=[VMEM_SPEC] * 2,
        out_specs=VMEM_SPEC,
        out_shape=jax.ShapeDtypeStruct((channels, tokens), BF16),
        compiler_params=params(16),
        cost_estimate=cost(flops, 2 * depth * channels),
        name="proj_queries",
    )(held, weights[0])
    return pair, queries


def grad_z_kernel(masks, runs, *refs):
    xs, (w_ref, out_ref, held) = refs[:-3], refs[-3:]
    total = None
    for n, x_ref in enumerate(xs):
        term = lax.dot_general(
            w_ref[:, piece_rows(masks, n, x_ref.shape[1])],
            x_ref[...],
            (((1,), (1,)), ((), ())),
            preferred_element_type=F32,
        )
        total = term if total is None else total + term
    run = total.shape[1] // runs
    for h, start in enumerate(run_starts(runs, run)):
        out_ref[:, pl.ds(start, run)] = total[:, h * run : (h + 1) * run].astype(BF16)


def grad_z_partial(xs, masks, runs, out_weight):
    tokens = xs[0].shape[0]
    channels, depth = out_weight.shape
    return pl.pallas_call(
        functools.partial(grad_z_kernel, masks, runs),
        in_specs=[VMEM_SPEC] * (len(xs) + 1),
        out_specs=VMEM_SPEC,
        out_shape=jax.ShapeDtypeStruct((channels, tokens), BF16),
        scratch_shapes=[pltpu.VMEM((tokens, depth), BF16)],
        compiler_params=params(16),
        cost_estimate=cost(2 * tokens * depth * channels, 2 * depth * channels),
        name="grad_z_partial",
    )(*xs, in_vmem(out_weight))


def iotas():
    shape = (BLOCK, BLOCK)
    return lax.broadcasted_iota(jnp.int32, shape, 0), lax.broadcasted_iota(jnp.int32, shape, 1)


def sheared(array):
    return pltpu.roll(array, 0, 1, stride=1, stride_axis=0)


def toeplitz_kernel(taps_ref, *refs):
    past_ref, next_ref = refs[-2:]
    row, lane = iotas()
    for g in range(taps_ref.shape[0]):
        ahead = sheared(jnp.broadcast_to(taps_ref[g : g + 1, :], (BLOCK, BLOCK)))
        behind = ahead.T
        past_ref[g, :BLOCK] = jnp.where(lane < row, ahead, 0.0).astype(BF16)
        past_ref[g, BLOCK:] = jnp.where(lane >= row, ahead, 0.0).astype(BF16)
        next_ref[g, :BLOCK] = jnp.where(lane <= row, behind, 0.0).astype(BF16)
        next_ref[g, BLOCK:] = jnp.where(lane > row, behind, 0.0).astype(BF16)


def toeplitz(filters, *earlier):
    groups, taps = filters.shape
    step = min(8, groups)
    shape = pltpu.VMEM((groups, 2 * BLOCK, taps), BF16)
    return pl.pallas_call(
        toeplitz_kernel,
        grid=(groups // step,),
        in_specs=[pl.BlockSpec((step, taps), lambda i: (i, 0))]
        + [LATER_SPEC] * len(earlier),
        out_specs=[pl.BlockSpec((step, 2 * BLOCK, taps), lambda i: (i, 0, 0))] * 2,
        out_shape=[shape, shape],
        compiler_params=params(16),
        cost_estimate=cost(groups * taps * 2000, groups * taps * 1024),
        name="toeplitz",
    )(filters, *earlier)


def block_of(array, i):
    blocks = array.shape[1] // BLOCK
    if 0 <= i < blocks:
        return array[:, i * BLOCK : (i + 1) * BLOCK]
    return jnp.zeros((array.shape[0], BLOCK), array.dtype)


def paired(array, by):
    blocks = array.shape[1] // BLOCK
    low, high = min(by, 0), max(by, 0)
    return jnp.concatenate(
        [
            jnp.concatenate([block_of(array, i + low), block_of(array, i + high)], 1)
            for i in range(blocks)
        ],
        0,
    )


def unstacked(array, blocks):
    rows = array.shape[0] // blocks
    return jnp.concatenate([array[i * rows : (i + 1) * rows] for i in range(blocks)], 1)


def summed(refs, part=...):
    total = refs[0][part].astype(F32)
    for ref in refs[1:]:
        total = total + ref[part].astype(F32)
    return total.astype(BF16)


def conv_kernel(parts, groups, *refs):
    shares, (past_ref, pair_ref, prod_ref, conv_ref) = refs[:parts], refs[parts:]
    key, value = summed(shares, 0), summed(shares, 1)
    pair_ref[0] = key
    pair_ref[1] = value
    product = (key.astype(F32) * value.astype(F32)).astype(BF16)
    prod_ref[...] = product
    channels, tokens = product.shape
    per = channels // groups
    for g in range(groups):
        rows = slice(g * per, (g + 1) * per)
        result = jnp.dot(paired(product[rows], -1), past_ref[g], preferred_element_type=F32)
        conv_ref[rows] = unstacked(result, tokens // BLOCK)


def conv_forward(shares, past):
    _, channels, tokens = shares[0].shape
    groups = past.shape[0]
    steps = max(1, groups // 32)
    chunk = channels // steps
    parts = len(shares)
    two = pl.BlockSpec((2, chunk, tokens), lambda i: (0, i, 0))
    one = pl.BlockSpec((chunk, tokens), lambda i: (i, 0))
    return pl.pallas_call(
        functools.partial(conv_kernel, parts, groups // steps),
        grid=(steps,),
        in_specs=[two] * parts
        + [pl.BlockSpec((groups // steps,) + past.shape[1:], lambda i: (i, 0, 0))],
        out_specs=[two, one, one],
        out_shape=[
            jax.ShapeDtypeStruct((2, channels, tokens), BF16),
            jax.ShapeDtypeStruct((channels, tokens), BF16),
            jax.ShapeDtypeStruct((channels, tokens), F32),
        ],
        compiler_params=params(16),
        cost_estimate=cost(4 * channels * tokens * BLOCK * 8, channels * tokens * 24),
        name="conv_forward",
    )(*shares, past)


def conv_back_kernel(parts, groups, *refs):
    shares, queries = refs[:parts], refs[parts : 2 * parts]
    pair_ref, conv_ref, next_ref, out_ref, grad_ref = refs[2 * parts :]
    grad_z = shares[0][...].astype(F32)
    for ref in shares[1:]:
        grad_z = grad_z + ref[...].astype(F32)
    out_ref[0] = (grad_z * conv_ref[...]).astype(BF16)
    grad = (grad_z * summed(queries).astype(F32)).astype(BF16)
    grad_ref[...] = grad
    channels, tokens = grad.shape
    per = channels // groups
    for g in range(groups):
        rows = slice(g * per, (g + 1) * per)
        result = jnp.dot(paired(grad[rows], 1), next_ref[g], preferred_element_type=F32)
        result = unstacked(result, tokens // BLOCK)
        out_ref[1, rows] = (result * pair_ref[1, rows].astype(F32)).astype(BF16)
        out_ref[2, rows] = (result * pair_ref[0, rows].astype(F32)).astype(BF16)


def conv_backward(shares, queries, pair, conv, after):
    channels, tokens = conv.shape
    groups = after.shape[0]
    steps = max(1, groups // 32)
    chunk = channels // steps
    parts = len(shares)
    three = pl.BlockSpec((3, chunk, tokens), lambda i: (0, i, 0))
    one = pl.BlockSpec((chunk, tokens), lambda i: (i, 0))
    return pl.pallas_call(
        functools.partial(conv_back_kernel, parts, groups // steps),
        grid=(steps,),
        in_specs=[one] * (2 * parts)
        + [
            pl.BlockSpec((2, chunk, tokens), lambda i: (0, i, 0)),
            one,
            pl.BlockSpec((groups // steps,) + after.shape[1:], lambda i: (i, 0, 0)),
        ],
        out_specs=[three, one],
        out_shape=[
            jax.ShapeDtypeStruct((3, channels, tokens), BF16),
            jax.ShapeDtypeStruct((channels, tokens), BF16),
        ],
        compiler_params=params(16),
        cost_estimate=cost(4 * channels * tokens * BLOCK * 8, channels * tokens * 24),
        name="conv_backward",
    )(*shares, *queries, pair, conv, after)


def taps_kernel(groups, prod_ref, grad_ref, out_ref):
    row, lane = iotas()
    flip = (row + lane == BLOCK - 1).astype(F32).astype(BF16)
    channels, tokens = prod_ref.shape
    per = channels // groups
    blocks = tokens // BLOCK

    def cut(ref, i):
        return ref[:, i * BLOCK : (i + 1) * BLOCK]

    turned = [
        jnp.dot(cut(prod_ref, i), flip, preferred_element_type=F32).astype(BF16)
        for i in range(blocks)
    ]
    grad = [cut(grad_ref, i) for i in range(blocks)]

    def correlated(earlier, later, rows):
        return lax.dot_general(
            jnp.concatenate([block[rows] for block in earlier], 0),
            jnp.concatenate([block[rows] for block in later], 0),
            (((0,), (0,)), ((), ())),
            preferred_element_type=F32,
        )

    for g in range(groups):
        rows = slice(g * per, (g + 1) * per)
        within = correlated(turned, grad, rows)
        before = correlated(turned[:-1], grad[1:], rows)
        folded = jnp.where(row + lane >= BLOCK - 1, within, before)
        out_ref[g : g + 1, :] = jnp.sum(sheared(folded), axis=0, keepdims=True)
    out_ref[...] = pltpu.roll(out_ref[...], 1, 1) / TOK_DEV


def taps_gradient(product, grad, groups):
    channels, tokens = product.shape
    steps = max(1, groups // 8)
    chunk = channels // steps
    one = pl.BlockSpec((chunk, tokens), lambda i: (i, 0))
    return pl.pallas_call(
        functools.partial(taps_kernel, groups // steps),
        grid=(steps,),
        in_specs=[one, one],
        out_specs=pl.BlockSpec((groups // steps, BLOCK), lambda i: (i, 0)),
        out_shape=jax.ShapeDtypeStruct((groups, BLOCK), F32),
        compiler_params=params(16),
        cost_estimate=cost(4 * channels * tokens * BLOCK * 8, channels * tokens * 24),
        name="taps_gradient",
    )(product, grad)


def input_kernel(masks, *refs):
    w_refs, (g_ref, out_ref) = refs[:3], refs[3:]
    pieces, rows, _ = out_ref.shape
    for i in range(pieces):
        at = piece_rows(masks, i, rows)
        w = jnp.concatenate([ref[at, :] for ref in w_refs], 1)
        out_ref[i] = jnp.dot(w, g_ref[...], preferred_element_type=F32).astype(BF16)


def input_partial(masks, pieces, rows, weights, grad_proj):
    _, channels, tokens = grad_proj.shape
    return pl.pallas_call(
        functools.partial(input_kernel, masks),
        in_specs=[VMEM_SPEC] * 4,
        out_specs=VMEM_SPEC,
        out_shape=jax.ShapeDtypeStruct((pieces, rows, tokens), BF16),
        compiler_params=params(16),
        cost_estimate=cost(
            2 * tokens * pieces * rows * 3 * channels, 2 * pieces * rows * (3 * channels + tokens)
        ),
        name="input_partial",
    )(*[in_vmem(weight) for weight in weights], grad_proj.reshape(3 * channels, tokens))


def across(array, mask):
    return lax.ppermute(array, "tensor", [(i, i ^ mask) for i in range(16)])


def other_row(array):
    return lax.ppermute(array, "fsdp", [(0, 1), (1, 0)])


def in_square(array, turn):
    pairs = []
    for i in range(32):
        y, k = divmod(i, 16)
        target = turn(y, k // Z1)
        if target is not None:
            pairs.append((i, target[0] * 16 + target[1] * Z1 + k % Z1))
    return lax.ppermute(array, ("fsdp", "tensor"), pairs)


def from_turn(y, z1):
    return (y, 1 - z1) if y == z1 else (1 - y, z1)


def over_diagonal(y, z1):
    return None if y == z1 else (1 - y, 1 - z1)


def first_stage(array):
    return in_square(array, from_turn), in_square(array, over_diagonal)


def second_stage(own, order=(1, 2, 3)):
    got = {n: across(own, MINE[n]) for n in order}
    return [own] + [got[n] for n in (1, 2, 3)]


def both_cores(same):
    return same + [across(piece, CORE) for piece in same]


def split_kernel(parts, same_ref, *refs):
    got_refs, out_refs = refs[:parts], refs[parts:]
    pieces = same_ref.shape[0]
    got = [ref.at[n] for ref in got_refs for n in range(ref.shape[0])]
    y = lax.axis_index("fsdp")
    leave = pl.ds(pl.multiple_of((1 - y) * TOK_DEV, BLOCK), TOK_DEV)
    stay = pl.ds(pl.multiple_of(y * TOK_DEV, BLOCK), TOK_DEV)
    for n in range(pieces):
        for at, out_ref in ((leave, out_refs[n]), (stay, out_refs[pieces + n])):
            total = same_ref[n, :, at].astype(F32) + got[n][:, at].astype(F32)
            out_ref[...] = total.astype(BF16)


def split(same, *got):
    pieces, rows, _ = same.shape
    out = jax.ShapeDtypeStruct((rows, TOK_DEV), BF16)
    halves = pl.pallas_call(
        functools.partial(split_kernel, len(got)),
        in_specs=[VMEM_SPEC] * (1 + len(got)),
        out_specs=[VMEM_SPEC] * (2 * pieces),
        out_shape=[out] * (2 * pieces),
        compiler_params=params(8),
        cost_estimate=cost(0, 6 * same.size),
        name="split",
    )(same, *got)
    return halves[:pieces], halves[pieces:]


def sum_kernel(*refs):
    total = refs[0][...].astype(F32)
    for ref in refs[1:-1]:
        total = total + ref[...].astype(F32)
    refs[-1][...] = total.astype(BF16)


def total_of(pieces):
    return pl.pallas_call(
        sum_kernel,
        in_specs=[VMEM_SPEC] * len(pieces),
        out_specs=VMEM_SPEC,
        out_shape=jax.ShapeDtypeStruct(pieces[0].shape, BF16),
        compiler_params=params(8),
        cost_estimate=cost(0, 8 * pieces[0].size),
        name="total",
    )(*pieces)


def sides_kernel(*refs):
    far_ref, keep_ref, send_ref = refs[-3:]
    home = at_home()
    near = refs[0][...].astype(F32)
    for ref in refs[1:-3]:
        near = near + ref[...].astype(F32)
    near = near.astype(BF16)

    @pl.when(home)
    def _():
        keep_ref[...] = near
        send_ref[...] = far_ref[...]

    @pl.when(jnp.logical_not(home))
    def _():
        keep_ref[...] = far_ref[...]
        send_ref[...] = near


def sides(pieces, far):
    out = jax.ShapeDtypeStruct(far.shape, BF16)
    return pl.pallas_call(
        sides_kernel,
        in_specs=[VMEM_SPEC] * (len(pieces) + 1),
        out_specs=[VMEM_SPEC] * 2,
        out_shape=[out] * 2,
        compiler_params=params(8),
        cost_estimate=cost(0, 8 * far.size),
        name="sides",
    )(*pieces, far)


def last_kernel(keep_ref, got_ref, out_ref):
    total = keep_ref[...].astype(F32) + got_ref[...].astype(F32)
    out_ref[...] = total.astype(BF16).T


def last_sum(keep, got):
    return pl.pallas_call(
        last_kernel,
        in_specs=[VMEM_SPEC] * 2,
        out_specs=VMEM_SPEC,
        out_shape=jax.ShapeDtypeStruct(keep.shape[::-1], BF16),
        compiler_params=params(8),
        cost_estimate=cost(0, 6 * keep.size),
        name="last_sum",
    )(keep, got)


def moved(pieces):
    return [pieces[0]] + [across(piece, mask) for piece, mask in zip(pieces[1:], MINE[1:])]


def scattered(same, *others):
    leave, stay = split(same, *[across(part, CORE) for part in others])
    leave, stay = moved(leave), moved(stay)
    far = other_row(total_of(leave))
    keep, send = sides(stay, far)
    return last_sum(keep, across(send, Z1))


def on_small_slice(tokens, values, scales, filters, out_weight, cotangent):
    rows = tokens.shape[1]
    token_stage = first_stage(tokens)
    weights, ready = prepared(values, scales)
    token_own = own_slice(in_hbm(tokens), *token_stage, ready)
    token_same = second_stage(token_own, (2, 1, 3))
    past, later = toeplitz(filters, token_own)
    out_held = loaded(out_weight, past)
    cotangent = copied(cotangent, token_own)
    cot_own = own_slice(cotangent, *first_stage(cotangent))
    late = relayed([token_same[3]], out_held, cot_own)
    token_same = [*token_same[:3], *late]
    xs = both_cores(token_same)
    cot_same = second_stage(cot_own)
    pair, queries = proj_partial(xs, MINE + OTHERS, 2, weights)
    cot_same = list(relayed(cot_same, queries))
    pair, product, conv = conv_forward([pair, other_row(pair)], past)
    z_part = grad_z_partial(both_cores(cot_same), MINE + OTHERS, 2, out_held)
    grad_proj, grad = conv_backward(
        [z_part, other_row(z_part)], [queries, other_row(queries)], pair, conv, later
    )
    others = [
        input_partial(masks, len(masks), rows, weights, grad_proj)
        for masks in (OTHERS[:3], OTHERS[3:])
    ]
    same = input_partial(MINE, 4, rows, weights, grad_proj)
    return scattered(same, *others), taps_gradient(product, grad, filters.shape[0])


def on_any_slice(tokens, values, scales, filters, out_weight, cotangent):
    count = lax.axis_size("fsdp")
    rows = values.shape[1]
    piece = min(rows, 512)
    pieces = rows // piece

    def gather(array):
        whole = lax.all_gather(array, "tensor", axis=1, tiled=True)
        mine = lax.all_to_all(whole, "fsdp", 1, 0, tiled=True)
        return [mine[:, i * piece : (i + 1) * piece] for i in range(pieces)]

    def shares(array):
        every = lax.all_gather(array, "fsdp", axis=0)
        return [every[i] for i in range(count)]

    weights, _ = prepared(values, scales)
    out_held = loaded(out_weight)
    past, later = toeplitz(filters)
    pair, queries = proj_partial(gather(tokens), None, 1, weights)
    pair, product, conv = conv_forward(shares(pair), past)
    z_part = grad_z_partial(gather(cotangent), None, 1, out_held)
    grad_proj, grad = conv_backward(shares(z_part), shares(queries), pair, conv, later)
    partial = input_partial(None, pieces, piece, weights, grad_proj)
    partial = partial.reshape(rows, partial.shape[2]).astype(F32)
    partial = lax.all_to_all(partial, "fsdp", 1, 0, tiled=True)
    total = lax.psum_scatter(partial, "tensor", scatter_dimension=0, tiled=True)
    return total.T.astype(BF16), taps_gradient(product, grad, filters.shape[0])


def on_device(tokens, in_values, in_scales, filters, out_weight, cotangent):
    values = jnp.transpose(in_values, (1, 0, 2))
    scales = jnp.transpose(in_scales, (1, 0, 2))
    small = lax.axis_size("fsdp") == 2 and lax.axis_size("tensor") == 16
    inner = on_small_slice if small else on_any_slice
    return inner(tokens, values, scales, filters, out_weight, cotangent)


def solution(mesh):
    placed = (
        P("fsdp", "tensor"),
        P("fsdp", None, "tensor"),
        P("fsdp", None, "tensor"),
        P("tensor", None),
        P("tensor", "fsdp"),
        P("fsdp", "tensor"),
    )
    return jax.shard_map(
        on_device,
        mesh=mesh,
        in_specs=placed,
        out_specs=(P("fsdp", "tensor"), P("tensor", None)),
        check_vma=False,
    )
```

```python
import functools

import jax
import jax.numpy as jnp
from jax import lax
from jax.experimental import pallas as pl
from jax.experimental.pallas import tpu as pltpu
from jax.sharding import PartitionSpec as P

BLOCK = 128
TOK_DEV = 128
BF16 = jnp.bfloat16
F32 = jnp.float32
MIB = 1 << 20


def cost(flops, read):
    return pl.CostEstimate(flops=int(flops) >> 12, bytes_accessed=int(read) >> 12, transcendentals=0)


def params(mib):
    return pltpu.CompilerParams(vmem_limit_bytes=mib * MIB)


def in_hbm(array):
    return pltpu.with_memory_space_constraint(array, pltpu.HBM)


VMEM_SPEC = pl.BlockSpec(memory_space=pltpu.VMEM)
SMEM_SPEC = pl.BlockSpec(memory_space=pltpu.SMEM)
LATER_SPEC = pl.BlockSpec(memory_space=pl.ANY)


def copy_kernel(in_ref, *refs):
    refs[-1][...] = in_ref[...]


def copied(array, *earlier):
    return pl.pallas_call(
        copy_kernel,
        in_specs=[VMEM_SPEC] + [LATER_SPEC] * len(earlier),
        out_specs=VMEM_SPEC,
        out_shape=jax.ShapeDtypeStruct(array.shape, array.dtype),
        compiler_params=params(8),
        cost_estimate=cost(0, 4 * array.size),
        name="copied",
    )(array, *earlier)


def at_home():
    return lax.axis_index("tensor") // Z1 == lax.axis_index("fsdp")


def own_kernel(array_ref, turned_ref, crossed_ref, *refs):
    out_ref, sem = refs[-2:]
    run = array_ref.shape[0]
    home = at_home()

    @pl.when(home)
    def _():
        copy = pltpu.make_async_copy(array_ref, out_ref.at[pl.ds(0, run), :], sem)
        copy.start()
        out_ref[run:] = turned_ref[...]
        copy.wait()

    @pl.when(jnp.logical_not(home))
    def _():
        out_ref[:run] = turned_ref[...]
        out_ref[run:] = crossed_ref[...]


def own_slice(array, turned, crossed, *earlier):
    return pl.pallas_call(
        own_kernel,
        in_specs=[LATER_SPEC] + [VMEM_SPEC] * 2 + [LATER_SPEC] * len(earlier),
        out_specs=VMEM_SPEC,
        out_shape=jax.ShapeDtypeStruct((2 * array.shape[0], array.shape[1]), array.dtype),
        scratch_shapes=[pltpu.SemaphoreType.DMA],
        compiler_params=params(8),
        cost_estimate=cost(0, 10 * array.size),
        name="own_slice",
    )(array, turned, crossed, *earlier)


def relay_kernel(*refs):
    del refs


def relayed(arrays, *earlier):
    count = len(arrays)
    return pl.pallas_call(
        relay_kernel,
        in_specs=[LATER_SPEC] * (count + len(earlier)),
        out_specs=[LATER_SPEC] * count,
        out_shape=[jax.ShapeDtypeStruct(array.shape, array.dtype) for array in arrays],
        input_output_aliases={n: n for n in range(count)},
        compiler_params=params(8),
        cost_estimate=cost(0, 0),
        name="relayed",
    )(*arrays, *earlier)


def in_vmem(array):
    return pltpu.with_memory_space_constraint(array, pltpu.VMEM)


AHEAD = 3


def prepare_kernel(v_ref, s_ref, *refs):
    weights, (done_ref, raw, held, ins, in_sems, s_sem) = refs[-9:-6], refs[-6:]
    piece = ins.shape[2]
    pieces = v_ref.shape[1] // piece

    def rows(i):
        return pl.ds(pl.multiple_of(i * piece, BLOCK), piece)

    def fetch(i, j):
        slot = lax.rem(i, AHEAD)
        return pltpu.make_async_copy(
            v_ref.at[j, rows(i), :], ins.at[slot, j], in_sems.at[slot, j]
        )

    scales = pltpu.make_async_copy(s_ref, raw, s_sem)
    scales.start()
    for i in range(min(AHEAD, pieces)):
        for j in range(3):
            fetch(i, j).start()
    scales.wait()
    held[...] = raw[...].astype(F32)
    done_ref[...] = jnp.zeros(done_ref.shape, F32)

    def one(i, carry):
        for j in range(3):
            fetch(i, j).wait()
            for b in range(piece // BLOCK):
                scale = held[j, pl.ds(i * (piece // BLOCK) + b, 1), :]
                at = pl.ds(pl.multiple_of(i * piece + b * BLOCK, BLOCK), BLOCK)
                values = ins[lax.rem(i, AHEAD), j, b * BLOCK : (b + 1) * BLOCK, :]
                weights[j][at, :] = (values.astype(F32) * scale).astype(BF16)

            @pl.when(i + AHEAD < pieces)
            def _(j=j):
                fetch(i + AHEAD, j).start()

        return carry

    lax.fori_loop(0, pieces, one, 0)


def prepared(values, scales, *earlier):
    _, rows, channels = values.shape
    piece = min(rows, 512)
    *weights, ready = pl.pallas_call(
        prepare_kernel,
        in_specs=[LATER_SPEC] * (2 + len(earlier)),
        out_specs=[VMEM_SPEC] * 4,
        out_shape=[pltpu.VMEM((rows, channels), BF16)] * 3
        + [jax.ShapeDtypeStruct((8, 128), F32)],
        scratch_shapes=[
            pltpu.VMEM(scales.shape, BF16),
            pltpu.VMEM(scales.shape, F32),
            pltpu.VMEM((AHEAD, 3, piece, channels), BF16),
            pltpu.SemaphoreType.DMA((AHEAD, 3)),
            pltpu.SemaphoreType.DMA,
        ],
        compiler_params=params(16),
        cost_estimate=cost(values.size * 4, 4 * values.size),
        name="prepare",
    )(in_hbm(values), in_hbm(scales), *earlier)
    return weights, ready


Z1, Z0, X, CORE = 8, 4, 2, 1
MINE = (0, Z0, X, X + Z0)
OTHERS = tuple(mask + CORE for mask in MINE)


def slices_of(masks):
    low = lax.rem(lax.axis_index("tensor"), Z1)
    return [low ^ mask for mask in masks]


def run_starts(runs, run):
    if runs == 1:
        return [0]
    y = lax.axis_index("fsdp")
    return [pl.multiple_of(y * run, BLOCK), pl.multiple_of((1 - y) * run, BLOCK)]


def piece_rows(masks, n, rows):
    if masks is None:
        return pl.ds(n * rows, rows)
    return pl.ds(pl.multiple_of(slices_of(masks)[n] * rows, BLOCK), rows)


def load_kernel(in_ref, *refs):
    out_ref, sem = refs[-2:]
    copy = pltpu.make_async_copy(in_ref, out_ref, sem)
    copy.start()
    copy.wait()


def loaded(array, *earlier):
    return pl.pallas_call(
        load_kernel,
        in_specs=[LATER_SPEC] * (1 + len(earlier)),
        out_specs=VMEM_SPEC,
        out_shape=pltpu.VMEM(array.shape, array.dtype),
        scratch_shapes=[pltpu.SemaphoreType.DMA],
        compiler_params=params(8),
        cost_estimate=cost(0, 4 * array.size),
        name="loaded",
    )(in_hbm(array), *earlier)


def assembled(masks, refs, held):
    for n, ref in enumerate(refs):
        held[:, piece_rows(masks, n, ref.shape[1])] = ref[...]


def proj_part(runs, held_ref, w_ref, out_ref):
    run = held_ref.shape[0] // runs
    total = jnp.dot(held_ref[...], w_ref[...], preferred_element_type=F32)
    for h, start in enumerate(run_starts(runs, run)):
        out_ref[:, pl.ds(start, run)] = total[h * run : (h + 1) * run].astype(BF16).T


def pair_kernel(masks, runs, *refs):
    xs, (key_ref, value_ref, out_ref, held_ref) = refs[:-4], refs[-4:]
    assembled(masks, xs, held_ref)
    proj_part(runs, held_ref, key_ref, out_ref.at[0])
    proj_part(runs, held_ref, value_ref, out_ref.at[1])


def query_kernel(runs, held_ref, w_ref, out_ref):
    proj_part(runs, held_ref, w_ref, out_ref)


def proj_partial(xs, masks, runs, weights):
    tokens = xs[0].shape[0]
    depth, channels = weights[0].shape
    flops = 2 * tokens * depth * channels
    weights = [in_vmem(weight) for weight in weights]
    pair, held = pl.pallas_call(
        functools.partial(pair_kernel, masks, runs),
        in_specs=[VMEM_SPEC] * (len(xs) + 2),
        out_specs=[VMEM_SPEC] * 2,
        out_shape=[
            jax.ShapeDtypeStruct((2, channels, tokens), BF16),
            pltpu.VMEM((tokens, depth), BF16),
        ],
        compiler_params=params(16),
        cost_estimate=cost(2 * flops, 4 * depth * channels),
        name="proj_pair",
    )(*xs, *weights[1:])
    queries = pl.pallas_call(
        functools.partial(query_kernel, runs),
        in_specs=[VMEM_SPEC] * 2,
        out_specs=VMEM_SPEC,
        out_shape=jax.ShapeDtypeStruct((channels, tokens), BF16),
        compiler_params=params(16),
        cost_estimate=cost(flops, 2 * depth * channels),
        name="proj_queries",
    )(held, weights[0])
    return pair, queries


def grad_z_kernel(masks, runs, *refs):
    xs, (w_ref, out_ref, held) = refs[:-3], refs[-3:]
    total = None
    for n, x_ref in enumerate(xs):
        term = lax.dot_general(
            w_ref[:, piece_rows(masks, n, x_ref.shape[1])],
            x_ref[...],
            (((1,), (1,)), ((), ())),
            preferred_element_type=F32,
        )
        total = term if total is None else total + term
    run = total.shape[1] // runs
    for h, start in enumerate(run_starts(runs, run)):
        out_ref[:, pl.ds(start, run)] = total[:, h * run : (h + 1) * run].astype(BF16)


def grad_z_partial(xs, masks, runs, out_weight):
    tokens = xs[0].shape[0]
    channels, depth = out_weight.shape
    return pl.pallas_call(
        functools.partial(grad_z_kernel, masks, runs),
        in_specs=[VMEM_SPEC] * (len(xs) + 1),
        out_specs=VMEM_SPEC,
        out_shape=jax.ShapeDtypeStruct((channels, tokens), BF16),
        scratch_shapes=[pltpu.VMEM((tokens, depth), BF16)],
        compiler_params=params(16),
        cost_estimate=cost(2 * tokens * depth * channels, 2 * depth * channels),
        name="grad_z_partial",
    )(*xs, in_vmem(out_weight))


def iotas():
    shape = (BLOCK, BLOCK)
    return lax.broadcasted_iota(jnp.int32, shape, 0), lax.broadcasted_iota(jnp.int32, shape, 1)


def sheared(array):
    return pltpu.roll(array, 0, 1, stride=1, stride_axis=0)


def toeplitz_kernel(taps_ref, *refs):
    past_ref, next_ref = refs[-2:]
    row, lane = iotas()
    for g in range(taps_ref.shape[0]):
        ahead = sheared(jnp.broadcast_to(taps_ref[g : g + 1, :], (BLOCK, BLOCK)))
        behind = ahead.T
        past_ref[g, :BLOCK] = jnp.where(lane < row, ahead, 0.0).astype(BF16)
        past_ref[g, BLOCK:] = jnp.where(lane >= row, ahead, 0.0).astype(BF16)
        next_ref[g, :BLOCK] = jnp.where(lane <= row, behind, 0.0).astype(BF16)
        next_ref[g, BLOCK:] = jnp.where(lane > row, behind, 0.0).astype(BF16)


def toeplitz(filters, *earlier):
    groups, taps = filters.shape
    step = min(16, groups)
    shape = pltpu.VMEM((groups, 2 * BLOCK, taps), BF16)
    return pl.pallas_call(
        toeplitz_kernel,
        grid=(groups // step,),
        in_specs=[pl.BlockSpec((step, taps), lambda i: (i, 0))]
        + [LATER_SPEC] * len(earlier),
        out_specs=[pl.BlockSpec((step, 2 * BLOCK, taps), lambda i: (i, 0, 0))] * 2,
        out_shape=[shape, shape],
        compiler_params=params(16),
        cost_estimate=cost(groups * taps * 2000, groups * taps * 1024),
        name="toeplitz",
    )(filters, *earlier)


def block_of(array, i):
    blocks = array.shape[1] // BLOCK
    if 0 <= i < blocks:
        return array[:, i * BLOCK : (i + 1) * BLOCK]
    return jnp.zeros((array.shape[0], BLOCK), array.dtype)


def paired(array, by):
    blocks = array.shape[1] // BLOCK
    low, high = min(by, 0), max(by, 0)
    return jnp.concatenate(
        [
            jnp.concatenate([block_of(array, i + low), block_of(array, i + high)], 1)
            for i in range(blocks)
        ],
        0,
    )


def unstacked(array, blocks):
    rows = array.shape[0] // blocks
    return jnp.concatenate([array[i * rows : (i + 1) * rows] for i in range(blocks)], 1)


def summed(refs, part=...):
    total = refs[0][part].astype(F32)
    for ref in refs[1:]:
        total = total + ref[part].astype(F32)
    return total.astype(BF16)


def conv_kernel(parts, groups, *refs):
    shares, (past_ref, pair_ref, prod_ref, conv_ref) = refs[:parts], refs[parts:]
    key, value = summed(shares, 0), summed(shares, 1)
    pair_ref[0] = key
    pair_ref[1] = value
    product = (key.astype(F32) * value.astype(F32)).astype(BF16)
    prod_ref[...] = product
    channels, tokens = product.shape
    per = channels // groups
    for g in range(groups):
        rows = slice(g * per, (g + 1) * per)
        result = jnp.dot(paired(product[rows], -1), past_ref[g], preferred_element_type=F32)
        conv_ref[rows] = unstacked(result, tokens // BLOCK)


def conv_forward(shares, past):
    _, channels, tokens = shares[0].shape
    groups = past.shape[0]
    steps = max(1, groups // 32)
    chunk = channels // steps
    parts = len(shares)
    two = pl.BlockSpec((2, chunk, tokens), lambda i: (0, i, 0))
    one = pl.BlockSpec((chunk, tokens), lambda i: (i, 0))
    return pl.pallas_call(
        functools.partial(conv_kernel, parts, groups // steps),
        grid=(steps,),
        in_specs=[two] * parts
        + [pl.BlockSpec((groups // steps,) + past.shape[1:], lambda i: (i, 0, 0))],
        out_specs=[two, one, one],
        out_shape=[
            jax.ShapeDtypeStruct((2, channels, tokens), BF16),
            jax.ShapeDtypeStruct((channels, tokens), BF16),
            jax.ShapeDtypeStruct((channels, tokens), F32),
        ],
        compiler_params=params(16),
        cost_estimate=cost(4 * channels * tokens * BLOCK * 8, channels * tokens * 24),
        name="conv_forward",
    )(*shares, past)


def conv_back_kernel(parts, groups, *refs):
    shares, queries = refs[:parts], refs[parts : 2 * parts]
    pair_ref, conv_ref, next_ref, out_ref, grad_ref = refs[2 * parts :]
    grad_z = shares[0][...].astype(F32)
    for ref in shares[1:]:
        grad_z = grad_z + ref[...].astype(F32)
    out_ref[0] = (grad_z * conv_ref[...]).astype(BF16)
    grad = (grad_z * summed(queries).astype(F32)).astype(BF16)
    grad_ref[...] = grad
    channels, tokens = grad.shape
    per = channels // groups
    for g in range(groups):
        rows = slice(g * per, (g + 1) * per)
        result = jnp.dot(paired(grad[rows], 1), next_ref[g], preferred_element_type=F32)
        result = unstacked(result, tokens // BLOCK)
        out_ref[1, rows] = (result * pair_ref[1, rows].astype(F32)).astype(BF16)
        out_ref[2, rows] = (result * pair_ref[0, rows].astype(F32)).astype(BF16)


def conv_backward(shares, queries, pair, conv, after):
    channels, tokens = conv.shape
    groups = after.shape[0]
    steps = max(1, groups // 32)
    chunk = channels // steps
    parts = len(shares)
    three = pl.BlockSpec((3, chunk, tokens), lambda i: (0, i, 0))
    one = pl.BlockSpec((chunk, tokens), lambda i: (i, 0))
    return pl.pallas_call(
        functools.partial(conv_back_kernel, parts, groups // steps),
        grid=(steps,),
        in_specs=[one] * (2 * parts)
        + [
            pl.BlockSpec((2, chunk, tokens), lambda i: (0, i, 0)),
            one,
            pl.BlockSpec((groups // steps,) + after.shape[1:], lambda i: (i, 0, 0)),
        ],
        out_specs=[three, one],
        out_shape=[
            jax.ShapeDtypeStruct((3, channels, tokens), BF16),
            jax.ShapeDtypeStruct((channels, tokens), BF16),
        ],
        compiler_params=params(16),
        cost_estimate=cost(4 * channels * tokens * BLOCK * 8, channels * tokens * 24),
        name="conv_backward",
    )(*shares, *queries, pair, conv, after)


def taps_kernel(groups, prod_ref, grad_ref, out_ref):
    row, lane = iotas()
    flip = (row + lane == BLOCK - 1).astype(F32).astype(BF16)
    channels, tokens = prod_ref.shape
    per = channels // groups
    blocks = tokens // BLOCK

    def cut(ref, i):
        return ref[:, i * BLOCK : (i + 1) * BLOCK]

    turned = [
        jnp.dot(cut(prod_ref, i), flip, preferred_element_type=F32).astype(BF16)
        for i in range(blocks)
    ]
    grad = [cut(grad_ref, i) for i in range(blocks)]

    def correlated(earlier, later, rows):
        return lax.dot_general(
            jnp.concatenate([block[rows] for block in earlier], 0),
            jnp.concatenate([block[rows] for block in later], 0),
            (((0,), (0,)), ((), ())),
            preferred_element_type=F32,
        )

    for g in range(groups):
        rows = slice(g * per, (g + 1) * per)
        within = correlated(turned, grad, rows)
        before = correlated(turned[:-1], grad[1:], rows)
        folded = jnp.where(row + lane >= BLOCK - 1, within, before)
        out_ref[g : g + 1, :] = jnp.sum(sheared(folded), axis=0, keepdims=True)
    out_ref[...] = pltpu.roll(out_ref[...], 1, 1) / TOK_DEV


def taps_gradient(product, grad, groups):
    channels, tokens = product.shape
    steps = max(1, groups // 8)
    chunk = channels // steps
    one = pl.BlockSpec((chunk, tokens), lambda i: (i, 0))
    return pl.pallas_call(
        functools.partial(taps_kernel, groups // steps),
        grid=(steps,),
        in_specs=[one, one],
        out_specs=pl.BlockSpec((groups // steps, BLOCK), lambda i: (i, 0)),
        out_shape=jax.ShapeDtypeStruct((groups, BLOCK), F32),
        compiler_params=params(16),
        cost_estimate=cost(4 * channels * tokens * BLOCK * 8, channels * tokens * 24),
        name="taps_gradient",
    )(product, grad)


def input_kernel(masks, *refs):
    w_refs, (g_ref, out_ref) = refs[:3], refs[3:]
    pieces, rows, _ = out_ref.shape
    for i in range(pieces):
        at = piece_rows(masks, i, rows)
        w = jnp.concatenate([ref[at, :] for ref in w_refs], 1)
        out_ref[i] = jnp.dot(w, g_ref[...], preferred_element_type=F32).astype(BF16)


def input_partial(masks, pieces, rows, weights, grad_proj):
    _, channels, tokens = grad_proj.shape
    return pl.pallas_call(
        functools.partial(input_kernel, masks),
        in_specs=[VMEM_SPEC] * 4,
        out_specs=VMEM_SPEC,
        out_shape=jax.ShapeDtypeStruct((pieces, rows, tokens), BF16),
        compiler_params=params(16),
        cost_estimate=cost(
            2 * tokens * pieces * rows * 3 * channels, 2 * pieces * rows * (3 * channels + tokens)
        ),
        name="input_partial",
    )(*[in_vmem(weight) for weight in weights], grad_proj.reshape(3 * channels, tokens))


def across(array, mask):
    return lax.ppermute(array, "tensor", [(i, i ^ mask) for i in range(16)])


def other_row(array):
    return lax.ppermute(array, "fsdp", [(0, 1), (1, 0)])


def in_square(array, turn):
    pairs = []
    for i in range(32):
        y, k = divmod(i, 16)
        target = turn(y, k // Z1)
        if target is not None:
            pairs.append((i, target[0] * 16 + target[1] * Z1 + k % Z1))
    return lax.ppermute(array, ("fsdp", "tensor"), pairs)


def from_turn(y, z1):
    return (y, 1 - z1) if y == z1 else (1 - y, z1)


def over_diagonal(y, z1):
    return None if y == z1 else (1 - y, 1 - z1)


def first_stage(array):
    return in_square(array, from_turn), in_square(array, over_diagonal)


def second_stage(own, order=(1, 2, 3)):
    got = {n: across(own, MINE[n]) for n in order}
    return [own] + [got[n] for n in (1, 2, 3)]


def both_cores(same):
    return same + [across(piece, CORE) for piece in same]


def split_kernel(parts, same_ref, *refs):
    got_refs, out_refs = refs[:parts], refs[parts:]
    pieces = same_ref.shape[0]
    got = [ref.at[n] for ref in got_refs for n in range(ref.shape[0])]
    y = lax.axis_index("fsdp")
    leave = pl.ds(pl.multiple_of((1 - y) * TOK_DEV, BLOCK), TOK_DEV)
    stay = pl.ds(pl.multiple_of(y * TOK_DEV, BLOCK), TOK_DEV)
    for n in range(pieces):
        for at, out_ref in ((leave, out_refs[n]), (stay, out_refs[pieces + n])):
            total = same_ref[n, :, at].astype(F32) + got[n][:, at].astype(F32)
            out_ref[...] = total.astype(BF16)


def split(same, *got):
    pieces, rows, _ = same.shape
    out = jax.ShapeDtypeStruct((rows, TOK_DEV), BF16)
    halves = pl.pallas_call(
        functools.partial(split_kernel, len(got)),
        in_specs=[VMEM_SPEC] * (1 + len(got)),
        out_specs=[VMEM_SPEC] * (2 * pieces),
        out_shape=[out] * (2 * pieces),
        compiler_params=params(8),
        cost_estimate=cost(0, 6 * same.size),
        name="split",
    )(same, *got)
    return halves[:pieces], halves[pieces:]


def sum_kernel(*refs):
    total = refs[0][...].astype(F32)
    for ref in refs[1:-1]:
        total = total + ref[...].astype(F32)
    refs[-1][...] = total.astype(BF16)


def total_of(pieces):
    return pl.pallas_call(
        sum_kernel,
        in_specs=[VMEM_SPEC] * len(pieces),
        out_specs=VMEM_SPEC,
        out_shape=jax.ShapeDtypeStruct(pieces[0].shape, BF16),
        compiler_params=params(8),
        cost_estimate=cost(0, 8 * pieces[0].size),
        name="total",
    )(*pieces)


def sides_kernel(*refs):
    far_ref, keep_ref, send_ref = refs[-3:]
    home = at_home()
    near = refs[0][...].astype(F32)
    for ref in refs[1:-3]:
        near = near + ref[...].astype(F32)
    near = near.astype(BF16)

    @pl.when(home)
    def _():
        keep_ref[...] = near
        send_ref[...] = far_ref[...]

    @pl.when(jnp.logical_not(home))
    def _():
        keep_ref[...] = far_ref[...]
        send_ref[...] = near


def sides(pieces, far):
    out = jax.ShapeDtypeStruct(far.shape, BF16)
    return pl.pallas_call(
        sides_kernel,
        in_specs=[VMEM_SPEC] * (len(pieces) + 1),
        out_specs=[VMEM_SPEC] * 2,
        out_shape=[out] * 2,
        compiler_params=params(8),
        cost_estimate=cost(0, 8 * far.size),
        name="sides",
    )(*pieces, far)


def last_kernel(keep_ref, got_ref, out_ref):
    total = keep_ref[...].astype(F32) + got_ref[...].astype(F32)
    out_ref[...] = total.astype(BF16).T


def last_sum(keep, got):
    return pl.pallas_call(
        last_kernel,
        in_specs=[VMEM_SPEC] * 2,
        out_specs=VMEM_SPEC,
        out_shape=jax.ShapeDtypeStruct(keep.shape[::-1], BF16),
        compiler_params=params(8),
        cost_estimate=cost(0, 6 * keep.size),
        name="last_sum",
    )(keep, got)


def moved(pieces):
    return [pieces[0]] + [across(piece, mask) for piece, mask in zip(pieces[1:], MINE[1:])]


def scattered(same, *others):
    leave, stay = split(same, *[across(part, CORE) for part in others])
    leave, stay = moved(leave), moved(stay)
    far = other_row(total_of(leave))
    keep, send = sides(stay, far)
    return last_sum(keep, across(send, Z1))


def on_small_slice(tokens, values, scales, filters, out_weight, cotangent):
    rows = tokens.shape[1]
    token_stage = first_stage(tokens)
    weights, ready = prepared(values, scales)
    token_own = own_slice(in_hbm(tokens), *token_stage, ready)
    token_same = second_stage(token_own, (2, 1, 3))
    past, later = toeplitz(filters, token_own)
    out_held = loaded(out_weight, past)
    cotangent = copied(cotangent, token_own)
    cot_own = own_slice(cotangent, *first_stage(cotangent))
    late = relayed([token_same[3]], out_held, cot_own)
    token_same = [*token_same[:3], *late]
    xs = both_cores(token_same)
    cot_same = second_stage(cot_own)
    pair, queries = proj_partial(xs, MINE + OTHERS, 2, weights)
    cot_same = list(relayed(cot_same, queries))
    pair, product, conv = conv_forward([pair, other_row(pair)], past)
    z_part = grad_z_partial(both_cores(cot_same), MINE + OTHERS, 2, out_held)
    grad_proj, grad = conv_backward(
        [z_part, other_row(z_part)], [queries, other_row(queries)], pair, conv, later
    )
    others = [
        input_partial(masks, len(masks), rows, weights, grad_proj)
        for masks in (OTHERS[:3], OTHERS[3:])
    ]
    same = input_partial(MINE, 4, rows, weights, grad_proj)
    return scattered(same, *others), taps_gradient(product, grad, filters.shape[0])


def on_any_slice(tokens, values, scales, filters, out_weight, cotangent):
    count = lax.axis_size("fsdp")
    rows = values.shape[1]
    piece = min(rows, 512)
    pieces = rows // piece

    def gather(array):
        whole = lax.all_gather(array, "tensor", axis=1, tiled=True)
        mine = lax.all_to_all(whole, "fsdp", 1, 0, tiled=True)
        return [mine[:, i * piece : (i + 1) * piece] for i in range(pieces)]

    def shares(array):
        every = lax.all_gather(array, "fsdp", axis=0)
        return [every[i] for i in range(count)]

    weights, _ = prepared(values, scales)
    out_held = loaded(out_weight)
    past, later = toeplitz(filters)
    pair, queries = proj_partial(gather(tokens), None, 1, weights)
    pair, product, conv = conv_forward(shares(pair), past)
    z_part = grad_z_partial(gather(cotangent), None, 1, out_held)
    grad_proj, grad = conv_backward(shares(z_part), shares(queries), pair, conv, later)
    partial = input_partial(None, pieces, piece, weights, grad_proj)
    partial = partial.reshape(rows, partial.shape[2]).astype(F32)
    partial = lax.all_to_all(partial, "fsdp", 1, 0, tiled=True)
    total = lax.psum_scatter(partial, "tensor", scatter_dimension=0, tiled=True)
    return total.T.astype(BF16), taps_gradient(product, grad, filters.shape[0])


def on_device(tokens, in_values, in_scales, filters, out_weight, cotangent):
    values = jnp.transpose(in_values, (1, 0, 2))
    scales = jnp.transpose(in_scales, (1, 0, 2))
    small = lax.axis_size("fsdp") == 2 and lax.axis_size("tensor") == 16
    inner = on_small_slice if small else on_any_slice
    return inner(tokens, values, scales, filters, out_weight, cotangent)


def solution(mesh):
    placed = (
        P("fsdp", "tensor"),
        P("fsdp", None, "tensor"),
        P("fsdp", None, "tensor"),
        P("tensor", None),
        P("tensor", "fsdp"),
        P("fsdp", "tensor"),
    )
    return jax.shard_map(
        on_device,
        mesh=mesh,
        in_specs=placed,
        out_specs=(P("fsdp", "tensor"), P("tensor", None)),
        check_vma=False,
    )
```
